32 devices in a mesh: energy: 4 (over x, core), atom: 8 (over z, y).
Axes of the slice: x: 2, y: 2, z: 4, core: 2. Of those that a mesh axis runs over, the one named last changes fastest.
Arguments:
- green_blocks: bfloat16 [32, 16, 16, 1024], P('energy', None, None, 'atom'), may hold values from -6 to 6
- derivative: bfloat16 [16, 16, 16], replicated, may hold values from -0.75 to 0.75
- phonon_weight: float32 [8, 1024], P(None, 'atom'), may hold values from 0.02 to 0.3
- occupation: float32 [8], replicated, may hold values from 0.1 to 3
- mode_shift: int32 [8], replicated, may hold values from 1 to 16, as said below
- neighbours: int32 [1024, 16], P('atom'), may hold values from 0 to 1023, as said below
Outputs:
- self_energy: float32 [32, 16, 16, 1024], P('energy', None, None, 'atom')
The draws below stay inside these ranges and needn't reach their ends.
Inputs may be any that keep to these rules, and one draw needn't show every extreme that they name: `mode_shift`: shifts rise strictly with the mode; the first is 1 and the last 16. Slabs are runs of 128 consecutive atoms. For every atom, neighbours 0 to 13 lie in its own slab and the last 2 in other slabs. Over the atoms of one slab, at most 74 of these remote neighbours lie in any one other slab; in an order of the other slabs that differs from slab to slab, exactly 74 lie in each of the first 3 slabs, the rest in the next one and none in the others. One slab, drawn anew, receives exactly 74 from every other slab.
All inputs are finite; a program needn't handle non-finite values.
Results may differ from the reference program's by a relative error of at most 0.005.
Values may be sent and summed in bfloat16 or wider, within the bound.
No kernel may reach another device: no remote copies, remote signals or barrier semaphores. Data moves between devices by JAX's collectives and lax.ppermute only.
A program may use at most 64 MiB of HBM per device.

```python
import math
import jax
import jax.numpy as jnp
from jax import lax

ORB = 16
NEIGH = 16
REMOTE_BONDS = 2
MODES = 8
ATOM_DEV = 128
ENERGIES = 32
ATOMS = 1024
LOCAL_BONDS = 14
REMOTE = 256
CAP = 74


def draw_mode_shift(key, part):
    middle = ENERGIES // 2
    modes_index = lax.iota(jnp.int32, MODES)
    baseline = 1 + modes_index * (middle - 1) // (MODES - 1)
    spacing = max((middle - 1) // (MODES - 1), 1)
    jitter = jax.random.randint(jax.random.fold_in(key, 11), (MODES,), 0, spacing)
    interior = (modes_index > 0) & (modes_index < MODES - 1)
    return jnp.where(interior, baseline + jitter, baseline).astype(jnp.int32)


def draw_neighbours(key, part):
    slab_count = ATOMS // ATOM_DEV
    base_key = jax.random.fold_in(key, 23)
    key_local, key_perm, key_order, key_busy, key_target = jax.random.split(base_key, 5)
    atom_index = lax.iota(jnp.int32, ATOMS)
    own_slab = atom_index // ATOM_DEV
    local_ids = own_slab[:, None] * ATOM_DEV + jax.random.randint(key_local, (ATOMS, LOCAL_BONDS), 0, ATOM_DEV)
    busiest = jax.random.randint(key_busy, (), 0, slab_count)
    perm_keys = jax.random.split(key_perm, slab_count)
    slot_numbers = jax.vmap(lambda single: jax.random.permutation(single, REMOTE))(perm_keys)
    order_keys = jax.random.split(key_order, slab_count)
    scores = jax.vmap(lambda single: jax.random.permutation(single, slab_count))(order_keys)
    slab_index = lax.iota(jnp.int32, slab_count)
    scores = jnp.where(slab_index[None, :] == busiest, -1, scores)
    scores = jnp.where(slab_index[None, :] == slab_index[:, None], slab_count + 1, scores)
    visit_order = jnp.argsort(scores, axis=1, stable=True).astype(jnp.int32)
    position = slot_numbers // CAP
    target_slab = jnp.take_along_axis(visit_order, position, axis=1)
    remote_ids = target_slab * ATOM_DEV + jax.random.randint(key_target, (slab_count, REMOTE), 0, ATOM_DEV)
    remote_ids = remote_ids.reshape(ATOMS, REMOTE_BONDS)
    return jnp.concatenate([local_ids, remote_ids], 1).astype(jnp.int32)


def block_scale(stream_key, shape, pieces, low, largest):
    gain, own = 1.0, jax.random.fold_in(stream_key, 6)
    for dim, shards_of in pieces:
        steps = jnp.exp(jax.random.uniform(jax.random.fold_in(own, dim), (shards_of,), jnp.float32, low / len(pieces), largest / len(pieces)))
        gain = gain * jnp.repeat(steps, shape[dim] // shards_of).reshape([-1 if axis == dim else 1 for axis in range(len(shape))])
    return gain


def noise(stream_key, shape, scale, bound, shards=(), kind=jnp.bfloat16):
    array = jax.random.normal(stream_key, shape, jnp.float32) * scale
    if len(shards) > 0:
        array = block_scale(stream_key, shape, shards, -0.22, 0.18) * array
    return jnp.clip(array, min=-bound, max=bound).astype(kind)


def setup_inputs(seed: int = 0) -> dict:
    streams_of = jax.random.split(jax.random.key(seed), 7)
    return {
        "green_blocks": noise(streams_of[0], (ENERGIES, ORB, ORB, ATOMS), 1.0, 6.0, ((0, 4), (3, 8))),
        "derivative": noise(streams_of[1], (NEIGH, ORB, ORB), (4 * ORB) ** -0.5, 0.75),
        "phonon_weight": jnp.clip(jnp.exp(math.log(0.3) - 2.7080503 * jax.random.uniform(streams_of[2], (MODES, ATOMS), jnp.float32) ** block_scale(streams_of[2], (MODES, ATOMS), ((1, 8),), -0.2, 0.2)), 0.02, 0.3),
        "occupation": jnp.clip(jnp.exp(jax.random.uniform(streams_of[3], (MODES,), jnp.float32, math.log(0.1), math.log(3.0))), 0.1, 3.0),
        "mode_shift": draw_mode_shift(jax.random.fold_in(streams_of[6], 71), 0),
        "neighbours": draw_neighbours(jax.random.fold_in(streams_of[6], 71), 0),
    }


def reference(green_blocks, derivative, phonon_weight, occupation, mode_shift, neighbours):
    occupied = occupation[:, None]
    emission = (phonon_weight * (occupied + 1.0)).astype(jnp.bfloat16)
    absorption = (phonon_weight * occupied).astype(jnp.bfloat16)
    emission, absorption = lax.optimization_barrier((emission, absorption))
    emission = emission.astype(jnp.float32)
    absorption = absorption.astype(jnp.float32)
    middle = ENERGIES // 2
    padded = jnp.pad(green_blocks, ((middle, middle), (0, 0), (0, 0), (0, 0)))
    mixed = jnp.zeros(green_blocks.shape, jnp.float32)
    for mode in range(MODES):
        shift_value = mode_shift[mode].astype(jnp.int32)
        backward = lax.dynamic_slice_in_dim(padded, (middle - shift_value).astype(jnp.int32), ENERGIES, 0)
        forward = lax.dynamic_slice_in_dim(padded, (middle + shift_value).astype(jnp.int32), ENERGIES, 0)
        mixed = mixed + emission[mode] * backward.astype(jnp.float32)
        mixed = mixed + absorption[mode] * forward.astype(jnp.float32)
    mixed = mixed.astype(jnp.bfloat16).astype(jnp.float32)
    self_energy = jnp.zeros(green_blocks.shape, jnp.float32)
    for column in range(NEIGH):
        matrix = derivative[column].astype(jnp.float32)
        left_product = jnp.einsum("pr,ersn->epsn", matrix, mixed).astype(jnp.bfloat16)
        bond_term = jnp.einsum("epsn,qs->epqn", left_product.astype(jnp.float32), matrix)
        self_energy = self_energy.at[:, :, :, neighbours[:, column]].add(bond_term)
    return self_energy
```

```python
import functools

import jax
import jax.numpy as jnp
from jax import lax
from jax.experimental import pallas as pl
from jax.experimental.pallas import tpu as pltpu
from jax.sharding import PartitionSpec as P

REMOTE_BONDS = 2
CHUNKS = 2
VMEM_LIMIT = 48 * 1024 * 1024

VMEM = pl.BlockSpec(memory_space=pltpu.VMEM)
SMEM = pl.BlockSpec(memory_space=pltpu.SMEM)
ANY = pl.BlockSpec(memory_space=pl.ANY)


def params():
    return pltpu.CompilerParams(vmem_limit_bytes=VMEM_LIMIT)


def cost(flops, nbytes):
    return pl.CostEstimate(flops=int(flops), bytes_accessed=int(nbytes), transcendentals=0)


def swap(value, axis, mask):
    count = lax.axis_size(axis)
    return lax.ppermute(value, axis, [(i, i ^ mask) for i in range(count)])


def load_pair(own_ref, mate_ref, pair_ref, sems):
    rows = own_ref.shape[0]
    core = lax.axis_index("energy") % 2
    copies = [
        pltpu.make_async_copy(own_ref, pair_ref.at[pl.ds(core * rows, rows)], sems.at[0]),
        pltpu.make_async_copy(mate_ref, pair_ref.at[pl.ds((1 - core) * rows, rows)], sems.at[1]),
    ]
    for copy in copies:
        copy.start()
    for copy in copies:
        copy.wait()


def mix_terms(terms, pair_ref, store):
    square = pair_ref.shape[1]
    step = min(64, square)

    def body(block, carry):
        rows = pl.ds(pl.multiple_of(block * step, step), step)
        total = None
        for slot, weight in terms:
            term = weight * pair_ref[slot, rows, :].astype(jnp.float32)
            total = term if total is None else total + term
        store(rows, total)
        return carry

    lax.fori_loop(0, square // step, body, 0)


def couplings(weight_ref, occupation_ref, mode):
    weight = weight_ref[pl.ds(mode, 1), :]
    occupied = occupation_ref[mode]
    emission = (weight * (occupied + 1.0)).astype(jnp.bfloat16).astype(jnp.float32)
    absorption = (weight * occupied).astype(jnp.bfloat16).astype(jnp.float32)
    return emission, absorption


def clipped(source, base, span, weight):
    slot = source - base
    inside = jnp.logical_and(slot >= 0, slot < span)
    return jnp.clip(slot, 0, span - 1), weight * jnp.where(inside, 1.0, 0.0)


def mix_away_kernel(
    offset, first, shift_ref, occupation_ref, weight_ref, own_ref, mate_ref, out_ref, pair_ref, sems
):
    rows = own_ref.shape[0]
    modes = weight_ref.shape[0]
    me = lax.axis_index("energy")
    base = me // 2 * 2 * rows
    target = me ^ (2 * offset)
    above = target > me
    load_pair(own_ref, mate_ref, pair_ref, sems)
    for row in range(out_ref.shape[0]):
        energy = target * rows + first + row
        terms = []
        for mode in range(modes):
            emission, absorption = couplings(weight_ref, occupation_ref, mode)
            weight = jnp.where(above, emission, absorption)
            shift = shift_ref[mode]
            source = energy + jnp.where(above, -shift, shift)
            terms.append(clipped(source, base, 2 * rows, weight))

        def store(rows_at, total, row=row):
            out_ref[row, rows_at, :] = total.astype(out_ref.dtype)

        mix_terms(terms, pair_ref, store)


def mix_own_kernel(
    shift_ref, occupation_ref, weight_ref, own_ref, mate_ref, *rest
):
    out_refs, (pair_ref, sems) = rest[:-2], rest[-2:]
    rows = own_ref.shape[0]
    modes = weight_ref.shape[0]
    me = lax.axis_index("energy")
    base = me // 2 * 2 * rows
    load_pair(own_ref, mate_ref, pair_ref, sems)
    part = out_refs[0].shape[0]
    for index, out_ref in enumerate(out_refs):
        for row in range(part):
            energy = me * rows + index * part + row
            terms = []
            for mode in range(modes):
                emission, absorption = couplings(weight_ref, occupation_ref, mode)
                shift = shift_ref[mode]
                terms.append(clipped(energy - shift, base, 2 * rows, emission))
                terms.append(clipped(energy + shift, base, 2 * rows, absorption))

            def store(rows_at, total, row=row, out_ref=out_ref):
                out_ref[row, rows_at, :] = total

            mix_terms(terms, pair_ref, store)


def hot(columns, width):
    lanes = lax.broadcasted_iota(jnp.int32, (columns.shape[0], width), 1)
    return jnp.where(columns == lanes, 1.0, 0.0).astype(jnp.bfloat16)


def prepare_kernel(derivative_ref, neighbours_ref, local_k_ref, remote_k_ref, local_hot_ref):
    bonds, orbital, _ = derivative_ref.shape
    square = orbital * orbital
    atoms = neighbours_ref.shape[0]
    local_bonds = bonds - REMOTE_BONDS
    row = lax.broadcasted_iota(jnp.int32, (square, orbital), 0)
    row_of = lax.broadcasted_iota(jnp.int32, (square, orbital), 1)
    column = lax.broadcasted_iota(jnp.int32, (orbital, square), 1)
    column_of = lax.broadcasted_iota(jnp.int32, (orbital, square), 0)

    def pick(condition):
        return jnp.where(condition, 1.0, 0.0).astype(jnp.bfloat16)

    row_high, row_low = pick(row // orbital == row_of), pick(row % orbital == row_of)
    column_high, column_low = pick(column // orbital == column_of), pick(column % orbital == column_of)

    def spread(left, matrix, right):
        wide = jnp.dot(matrix, right, preferred_element_type=jnp.float32).astype(jnp.bfloat16)
        return jnp.dot(left, wide, preferred_element_type=jnp.float32)

    for bond in range(bonds):
        matrix = derivative_ref[bond]
        product = (
            spread(row_high, matrix, column_high) * spread(row_low, matrix, column_low)
        ).astype(jnp.bfloat16)
        if bond < local_bonds:
            local_k_ref[:, bond * square : (bond + 1) * square] = product
        else:
            at = bond - local_bonds
            remote_k_ref[:, at * square : (at + 1) * square] = product
    first = lax.axis_index("atom") * atoms
    for bond in range(local_bonds):
        local_hot_ref[:, bond * atoms : (bond + 1) * atoms] = hot(
            neighbours_ref[:, bond : bond + 1] - first, atoms
        )


def remote_hot_kernel(masks, flip, targets_ref, out_ref):
    bonds = targets_ref.shape[1]
    me = lax.axis_index("atom")
    atoms = out_ref.shape[0] // len(masks)
    for place, mask in enumerate(masks):
        source = me ^ mask
        ids = targets_ref[pl.ds(pl.multiple_of(source * atoms, atoms), atoms), :]
        for which, slab in enumerate((me, me ^ flip)):
            for bond in range(bonds):
                at = (which * bonds + bond) * atoms
                out_ref[place * atoms : (place + 1) * atoms, at : at + atoms] = hot(
                    ids[:, bond : bond + 1] - slab * atoms, atoms
                )


def local_kernel(mixed_ref, hot_ref, k_ref, out_ref, sums_ref):
    rows, square, atoms = mixed_ref.shape
    bonds = hot_ref.shape[1] // atoms
    group = sums_ref.shape[1] // atoms
    for start in range(0, rows, group):
        for inner in range(group):
            summed = jnp.dot(
                mixed_ref[start + inner], hot_ref[...], preferred_element_type=jnp.float32
            ).astype(jnp.bfloat16)
            for bond in range(bonds):
                sums_ref[bond * square : (bond + 1) * square, inner * atoms : (inner + 1) * atoms] = (
                    summed[:, bond * atoms : (bond + 1) * atoms]
                )
        result = jnp.dot(k_ref[...], sums_ref[...], preferred_element_type=jnp.float32)
        for inner in range(group):
            out_ref[start + inner] = result[:, inner * atoms : (inner + 1) * atoms]


def remote_kernel(source_count, *refs):
    source_refs = refs[:source_count]
    hot_ref, k_ref, local_ref, out_ref, away_ref = refs[source_count:]
    rows, square, atoms = local_ref.shape
    bonds = k_ref.shape[1] // square
    for row in range(rows):
        sources = jnp.concatenate([ref[row] for ref in source_refs], axis=1)
        summed = jnp.dot(sources, hot_ref[...], preferred_element_type=jnp.float32).astype(
            jnp.bfloat16
        )
        stacked = jnp.concatenate(
            [
                jnp.concatenate(
                    [
                        summed[:, (which * bonds + bond) * atoms : (which * bonds + bond + 1) * atoms]
                        for which in range(2)
                    ],
                    axis=1,
                )
                for bond in range(bonds)
            ],
            axis=0,
        )
        result = jnp.dot(k_ref[...], stacked, preferred_element_type=jnp.float32)
        out_ref[row] = result[:, :atoms] + local_ref[row]
        away_ref[row] = result[:, atoms:].astype(away_ref.dtype)


def per_device(green_blocks, derivative, phonon_weight, occupation, mode_shift, neighbours):
    rows, orbital, _, atoms = green_blocks.shape
    square = orbital * orbital
    bonds = derivative.shape[0]
    local_bonds = bonds - REMOTE_BONDS
    pairs = lax.axis_size("energy") // 2
    slabs = lax.axis_size("atom")
    flip = 2
    high = [4 * i for i in range(slabs // 4)]
    masks = high + [mask ^ 1 for mask in high]
    chunks = min(CHUNKS, rows)
    part = rows // chunks
    green = green_blocks.reshape(rows, square, atoms)
    block = jax.ShapeDtypeStruct((part, square, atoms), jnp.bfloat16)
    wide_block = jax.ShapeDtypeStruct((part, square, atoms), jnp.float32)
    pair_scratch = [
        pltpu.VMEM((2 * rows, square, atoms), jnp.bfloat16),
        pltpu.SemaphoreType.DMA((2,)),
    ]

    targets = lax.all_gather(neighbours[:, local_bonds:], "atom", axis=0, tiled=True)
    mate = swap(green, "energy", 1)

    local_k, remote_k, local_hot = pl.pallas_call(
        prepare_kernel,
        out_shape=(
            jax.ShapeDtypeStruct((square, local_bonds * square), jnp.bfloat16),
            jax.ShapeDtypeStruct((square, REMOTE_BONDS * square), jnp.bfloat16),
            jax.ShapeDtypeStruct((atoms, local_bonds * atoms), jnp.bfloat16),
        ),
        in_specs=[VMEM, VMEM],
        out_specs=(VMEM, VMEM, VMEM),
        compiler_params=params(),
        cost_estimate=cost(2e9, 3e6),
    )(derivative, neighbours)
    remote_hot = pl.pallas_call(
        functools.partial(remote_hot_kernel, masks, flip),
        out_shape=jax.ShapeDtypeStruct(
            (len(masks) * atoms, 2 * REMOTE_BONDS * atoms), jnp.bfloat16
        ),
        in_specs=[VMEM],
        out_specs=VMEM,
        compiler_params=params(),
        cost_estimate=cost(1e8, 1e6),
    )(targets)

    mix_in_specs = [SMEM, SMEM, VMEM, ANY, ANY]
    mix_args = (mode_shift, occupation, phonon_weight, green, mate)

    arrived = []
    for chunk in range(chunks):
        received = []
        for offset in range(1, pairs):
            away = pl.pallas_call(
                functools.partial(mix_away_kernel, offset, chunk * part),
                out_shape=block,
                in_specs=mix_in_specs,
                out_specs=VMEM,
                scratch_shapes=pair_scratch,
                compiler_params=params(),
                cost_estimate=cost(1e9, 2e6),
            )(*mix_args)
            received.append(swap(away, "energy", 2 * offset))
        arrived.append(received)
    own = pl.pallas_call(
        mix_own_kernel,
        out_shape=(wide_block,) * chunks,
        in_specs=mix_in_specs,
        out_specs=(VMEM,) * chunks,
        scratch_shapes=pair_scratch,
        compiler_params=params(),
        cost_estimate=cost(2e9, 2e6),
    )(*mix_args)

    results = []
    for chunk in range(chunks):
        total = own[chunk]
        for received in arrived[chunk]:
            total = total + received.astype(jnp.float32)
        mixed = total.astype(jnp.bfloat16)
        across = [mixed] + [swap(mixed, "atom", mask) for mask in high[1:]]
        sources = across + [swap(value, "atom", 1) for value in across]
        local = pl.pallas_call(
            local_kernel,
            out_shape=wide_block,
            in_specs=[VMEM] * 3,
            out_specs=VMEM,
            scratch_shapes=[
                pltpu.VMEM((local_bonds * square, min(2, part) * atoms), jnp.bfloat16)
            ],
            compiler_params=params(),
            cost_estimate=cost(2e9, 3e6),
        )(mixed, local_hot, local_k)
        partial, away = pl.pallas_call(
            functools.partial(remote_kernel, len(sources)),
            out_shape=(wide_block, block),
            in_specs=[VMEM] * (len(sources) + 3),
            out_specs=(VMEM, VMEM),
            compiler_params=params(),
            cost_estimate=cost(1e9, 3e6),
        )(*sources, remote_hot, remote_k, local)
        results.append((partial, swap(away, "atom", flip)))
    combined = jnp.concatenate(
        [partial + received.astype(jnp.float32) for partial, received in results], 0
    )
    return combined.reshape(rows, orbital, orbital, atoms)


def solution(mesh):
    in_specs = (P("energy", None, None, "atom"), P(), P(None, "atom"), P(), P(), P("atom", None))
    out_specs = P("energy", None, None, "atom")
    return jax.shard_map(
        per_device, mesh=mesh, in_specs=in_specs, out_specs=out_specs, check_vma=False
    )
```

```python
import functools

import jax
import jax.numpy as jnp
from jax import lax
from jax.experimental import pallas as pl
from jax.experimental.pallas import tpu as pltpu
from jax.sharding import PartitionSpec as P

REMOTE_BONDS = 2
CHUNKS = 2
ID_ROWS = 16
COST = 1.0
SUBLANES = 8
VMEM_LIMIT = 48 * 1024 * 1024

VMEM = pl.BlockSpec(memory_space=pltpu.VMEM)
HBM = pl.BlockSpec(memory_space=pltpu.HBM)
ANY = pl.BlockSpec(memory_space=pl.ANY)
F32, BF16 = jnp.float32, jnp.bfloat16


def params():
    return pltpu.CompilerParams(vmem_limit_bytes=VMEM_LIMIT)


def cost(flops, nbytes):
    return pl.CostEstimate(flops=int(flops * COST), bytes_accessed=int(nbytes * COST), transcendentals=0)


def swap(value, axis, mask):
    count = lax.axis_size(axis)
    return lax.ppermute(value, axis, [(i, i ^ mask) for i in range(count)])


def dot(left, right):
    return jnp.dot(left, right, preferred_element_type=F32)


def dot_nt(left, right):
    return lax.dot_general(left, right, (((1,), (1,)), ((), ())), preferred_element_type=F32)


def table_kernel(
    shift_hbm, occupation_hbm, weight_hbm, table_ref, shift_ref, occupation_ref, weight_ref, sems
):
    groups, rows, spare = table_ref.shape[:3]
    span = spare - 1
    modes = weight_ref.shape[0]
    copies = [
        pltpu.make_async_copy(shift_hbm, shift_ref, sems.at[0]),
        pltpu.make_async_copy(occupation_hbm, occupation_ref, sems.at[1]),
        pltpu.make_async_copy(weight_hbm, weight_ref, sems.at[2]),
    ]
    for copy in copies:
        copy.start()
    table_ref[...] = jnp.zeros_like(table_ref)
    for copy in copies:
        copy.wait()
    me = lax.axis_index("energy")
    base = me // 2 * span

    def put(group, row, source, value):
        slot = source - base
        inside = jnp.logical_and(slot >= 0, slot < span)
        table_ref[group, row, jnp.where(inside, slot, span)] = value

    for mode in range(modes):
        shift = shift_ref[mode]
        occupied = occupation_ref[mode]
        weight = jnp.broadcast_to(weight_ref[mode : mode + 1, :], table_ref.shape[3:])
        emission = (weight * (occupied + 1.0)).astype(BF16).astype(F32)
        absorption = (weight * occupied).astype(BF16).astype(F32)
        for group in range(groups):
            target = me ^ (2 * group)
            for row in range(rows):
                energy = target * rows + row
                if group == 0:
                    put(group, row, energy - shift, emission)
                    put(group, row, energy + shift, absorption)
                else:
                    above = target > me
                    put(
                        group,
                        row,
                        jnp.where(above, energy - shift, energy + shift),
                        jnp.where(above, emission, absorption),
                    )


def mix_kernel(group, first, table_ref, pair_ref, *rest):
    out_ref = rest[-1]
    span, square, atoms = pair_ref.shape
    rows = out_ref.shape[0]
    tile = table_ref.shape[3]
    step = min(32, square)

    def body(block, carry):
        at = pl.multiple_of(block * step, step)
        totals = [None] * rows
        for slot in range(span):
            values = pair_ref[slot, pl.ds(at, step), :].astype(F32).reshape(
                step // tile, tile, atoms
            )
            for row in range(rows):
                term = table_ref[group, first + row, slot][None] * values
                totals[row] = term if totals[row] is None else totals[row] + term
        for row in range(rows):
            out_ref[row, pl.ds(at, step), :] = totals[row].reshape(step, atoms).astype(out_ref.dtype)
        return carry

    lax.fori_loop(0, square // step, body, 0)


def hot(row, width):
    numbers = lax.broadcasted_iota(jnp.int32, (width, row.shape[1]), 0)
    return jnp.where(row == numbers, 1.0, 0.0).astype(BF16)


def prepare_kernel(derivative_ref, columns_ref, after_ref, local_k_ref, remote_k_ref, local_hot_ref):
    bonds, orbital, _ = derivative_ref.shape
    square = orbital * orbital
    atoms = columns_ref.shape[1]
    local_bonds = bonds - REMOTE_BONDS
    row = lax.broadcasted_iota(jnp.int32, (square, orbital), 0)
    row_of = lax.broadcasted_iota(jnp.int32, (square, orbital), 1)
    column = lax.broadcasted_iota(jnp.int32, (orbital, square), 1)
    column_of = lax.broadcasted_iota(jnp.int32, (orbital, square), 0)

    def pick(condition):
        return jnp.where(condition, 1.0, 0.0).astype(BF16)

    row_high, row_low = pick(row // orbital == row_of), pick(row % orbital == row_of)
    column_high, column_low = pick(column // orbital == column_of), pick(column % orbital == column_of)

    def spread(left, matrix, right):
        return dot(left, dot(matrix, right).astype(BF16))

    for bond in range(bonds):
        matrix = derivative_ref[bond]
        product = (
            spread(row_high, matrix, column_high) * spread(row_low, matrix, column_low)
        ).astype(BF16)
        if bond < local_bonds:
            local_k_ref[:, bond * square : (bond + 1) * square] = product
        else:
            at = bond - local_bonds
            remote_k_ref[:, at * square : (at + 1) * square] = product
    first = lax.axis_index("atom") * atoms
    for bond in range(local_bonds):
        local_hot_ref[bond * atoms : (bond + 1) * atoms, :] = hot(
            columns_ref[bond : bond + 1, :] - first, atoms
        )


def remote_hot_kernel(bonds, flip, *refs):
    id_refs, out_ref = refs[:-1], refs[-1]
    atoms = id_refs[0].shape[1]
    me = lax.axis_index("atom")
    for place, ids_ref in enumerate(id_refs):
        ids = ids_ref[...].astype(F32).astype(jnp.int32)
        for which, slab in enumerate((me, me ^ flip)):
            for bond in range(bonds):
                at = (which * bonds + bond) * atoms
                number = (ids[2 * bond : 2 * bond + 1, :] - slab) * atoms + ids[
                    2 * bond + 1 : 2 * bond + 2, :
                ]
                out_ref[at : at + atoms, place * atoms : (place + 1) * atoms] = hot(number, atoms)


def local_kernel(mixed_ref, hot_ref, k_ref, *rest):
    out_ref, sums_ref = rest[-2:]
    rows, square, atoms = out_ref.shape
    bonds = hot_ref.shape[0] // atoms
    group = sums_ref.shape[1] // atoms
    for start in range(0, rows, group):
        count = min(group, rows - start)
        for inner in range(count):
            at = (start + inner) * square
            summed = dot_nt(mixed_ref[at : at + square, :], hot_ref[...]).astype(BF16)
            for bond in range(bonds):
                sums_ref[bond * square : (bond + 1) * square, inner * atoms : (inner + 1) * atoms] = (
                    summed[:, bond * atoms : (bond + 1) * atoms]
                )
        result = dot(k_ref[...], sums_ref[:, : count * atoms])
        for inner in range(count):
            out_ref[start + inner] = result[:, inner * atoms : (inner + 1) * atoms]


def remote_kernel(offsets, *refs):
    source_refs = refs[: len(offsets)]
    hot_ref, k_ref, local_ref = refs[len(offsets) : len(offsets) + 3]
    out_ref, away_ref = refs[-2:]
    rows, square, atoms = local_ref.shape
    bonds = k_ref.shape[1] // square
    for row in range(rows):
        sources = jnp.concatenate(
            [
                ref[offset + row * square : offset + (row + 1) * square, :]
                for offset, ref in zip(offsets, source_refs)
            ],
            axis=1,
        )
        summed = dot_nt(sources, hot_ref[...]).astype(BF16)
        stacked = jnp.concatenate(
            [
                jnp.concatenate(
                    [
                        summed[:, (which * bonds + bond) * atoms : (which * bonds + bond + 1) * atoms]
                        for which in range(2)
                    ],
                    axis=1,
                )
                for bond in range(bonds)
            ],
            axis=0,
        )
        result = dot(k_ref[...], stacked)
        out_ref[row] = result[:, :atoms] + local_ref[row]
        away_ref[row] = result[:, atoms:].astype(away_ref.dtype)


def per_device(green_blocks, derivative, phonon_weight, occupation, mode_shift, neighbours):
    rows, orbital, _, atoms = green_blocks.shape
    square = orbital * orbital
    bonds = derivative.shape[0]
    modes = phonon_weight.shape[0]
    local_bonds = bonds - REMOTE_BONDS
    pairs = lax.axis_size("energy") // 2
    slabs = lax.axis_size("atom")
    flip = 2
    high = [4 * i for i in range(slabs // 4)]
    chunks = min(CHUNKS, rows)
    last = max(1, 3 * rows // 8)
    sizes = [rows - last, last] if chunks == 2 else [rows]
    firsts = [sum(sizes[:chunk]) for chunk in range(chunks)]
    green = green_blocks.reshape(rows, square, atoms)
    columns = neighbours.T

    mate = swap(green, "energy", 1)
    table = pl.pallas_call(
        table_kernel,
        out_shape=jax.ShapeDtypeStruct((pairs, rows, 2 * rows + 1, SUBLANES, atoms), F32),
        in_specs=[HBM] * 3,
        out_specs=VMEM,
        scratch_shapes=[
            pltpu.SMEM((modes,), jnp.int32),
            pltpu.SMEM((modes,), F32),
            pltpu.VMEM((modes, atoms), F32),
            pltpu.SemaphoreType.DMA((3,)),
        ],
        compiler_params=params(),
        cost_estimate=cost(1e6, 1e6),
    )(mode_shift, occupation, phonon_weight)
    odd = lax.axis_index("energy") % 2 == 1
    pair = jnp.where(
        odd, jnp.concatenate([mate, green], 0), jnp.concatenate([green, mate], 0)
    )

    def mix(group, chunk, kind, after):
        return pl.pallas_call(
            functools.partial(mix_kernel, group, firsts[chunk]),
            out_shape=jax.ShapeDtypeStruct((sizes[chunk], square, atoms), kind),
            in_specs=[VMEM, VMEM] + [ANY] * len(after),
            out_specs=VMEM,
            compiler_params=params(),
            cost_estimate=cost(5e8, 1e6),
        )(table, pair, *after)

    def prepare(after):
        return pl.pallas_call(
            prepare_kernel,
            out_shape=(
                jax.ShapeDtypeStruct((square, local_bonds * square), BF16),
                jax.ShapeDtypeStruct((square, REMOTE_BONDS * square), BF16),
                jax.ShapeDtypeStruct((local_bonds * atoms, atoms), BF16),
            ),
            in_specs=[VMEM, VMEM, ANY],
            out_specs=(VMEM, VMEM, VMEM),
            compiler_params=params(),
            cost_estimate=cost(2e9, 3e6),
        )(derivative, columns, after)

    def local_sum(chunk, after):
        return pl.pallas_call(
            local_kernel,
            out_shape=jax.ShapeDtypeStruct((sizes[chunk], square, atoms), F32),
            in_specs=[VMEM] * 3 + [ANY] * len(after),
            out_specs=VMEM,
            scratch_shapes=[
                pltpu.VMEM((local_bonds * square, min(2, sizes[chunk]) * atoms), BF16)
            ],
            compiler_params=params(),
            cost_estimate=cost(2e9, 3e6),
        )(mixed[chunk], local_hot, local_k, *after)

    remote_ids = columns[local_bonds:, :]
    ids = jnp.stack([remote_ids // atoms, remote_ids % atoms], 1).reshape(-1, atoms)
    ids = jnp.pad(ids, ((0, ID_ROWS - ids.shape[0]), (0, 0))).astype(BF16)

    own, arrived = [], []
    after = []
    for chunk in range(chunks):
        away = [mix(group, chunk, BF16, after) for group in range(1, pairs)]
        arrived.append([swap(value, "energy", 2 * group) for group, value in enumerate(away, 1)])
        if chunk == 0:
            local_k, remote_k, local_hot = prepare(away[0])
            own.append(mix(0, chunk, F32, [local_hot]))
            after = own[-1:]
        else:
            after = away[:1]
    mixed, local = [], []
    for chunk in range(chunks):
        if chunk > 0:
            own.append(mix(0, chunk, F32, after + mixed[-1:] + local[-1:]))
        total = own[chunk]
        for received in arrived[chunk]:
            total = total + received.astype(F32)
        total = total.astype(BF16).reshape(-1, atoms)
        mixed.append(jnp.concatenate([total, ids], 0) if chunk == 0 else total)
        if chunk > 0:
            local.append(local_sum(chunk - 1, mixed[-1:]))
    local.append(local_sum(chunks - 1, local[-1:]))

    beside = swap(jnp.concatenate(mixed, 0), "atom", 1)
    starts = [sum(value.shape[0] for value in mixed[:chunk]) for chunk in range(chunks)]

    remote_hot = None
    results = []
    for chunk in range(chunks):
        across = [swap(mixed[chunk], "atom", mask) for mask in high[1:]]
        beyond = [swap(value, "atom", 1) for value in across]
        sources = [mixed[chunk], beside] + across + beyond
        offsets = [0, starts[chunk]] + [0] * (len(across) + len(beyond))
        if remote_hot is None:
            ends = sizes[0] * square
            id_blocks = [
                value[offset + ends : offset + ends + ID_ROWS]
                for offset, value in zip(offsets, sources)
            ]
            remote_hot = pl.pallas_call(
                functools.partial(remote_hot_kernel, REMOTE_BONDS, flip),
                out_shape=jax.ShapeDtypeStruct(
                    (2 * REMOTE_BONDS * atoms, len(sources) * atoms), BF16
                ),
                in_specs=[VMEM] * len(sources),
                out_specs=VMEM,
                compiler_params=params(),
                cost_estimate=cost(1e8, 1e6),
            )(*id_blocks)
        after = local[-1:] + [partial for partial, _ in results[-1:]]
        partial, away = pl.pallas_call(
            functools.partial(remote_kernel, offsets),
            out_shape=(
                jax.ShapeDtypeStruct((sizes[chunk], square, atoms), F32),
                jax.ShapeDtypeStruct((sizes[chunk], square, atoms), BF16),
            ),
            in_specs=[VMEM] * (len(sources) + 3) + [ANY] * len(after),
            out_specs=(VMEM, VMEM),
            compiler_params=params(),
            cost_estimate=cost(1e9, 3e6),
        )(*sources, remote_hot, remote_k, local[chunk], *after)
        results.append((partial, swap(away, "atom", flip)))
    combined = jnp.concatenate(
        [partial + received.astype(F32) for partial, received in results], 0
    )
    return combined.reshape(rows, orbital, orbital, atoms)


def solution(mesh):
    in_specs = (P("energy", None, None, "atom"), P(), P(None, "atom"), P(), P(), P("atom", None))
    out_specs = P("energy", None, None, "atom")
    return jax.shard_map(
        per_device, mesh=mesh, in_specs=in_specs, out_specs=out_specs, check_vma=False
    )
```

```python
import functools

import jax
import jax.numpy as jnp
from jax import lax
from jax.experimental import pallas as pl
from jax.experimental.pallas import tpu as pltpu
from jax.sharding import PartitionSpec as P

REMOTE_BONDS = 2
ID_ROWS = 16
P_PART = 4
COST = 1.0
SUBLANES = 8
VMEM_LIMIT = 48 * 1024 * 1024

VMEM = pl.BlockSpec(memory_space=pltpu.VMEM)
HBM = pl.BlockSpec(memory_space=pltpu.HBM)
ANY = pl.BlockSpec(memory_space=pl.ANY)
F32, BF16 = jnp.float32, jnp.bfloat16


def params():
    return pltpu.CompilerParams(vmem_limit_bytes=VMEM_LIMIT)


def cost(flops, nbytes):
    return pl.CostEstimate(flops=int(flops * COST), bytes_accessed=int(nbytes * COST), transcendentals=0)


def swap(value, axis, mask):
    count = lax.axis_size(axis)
    return lax.ppermute(value, axis, [(i, i ^ mask) for i in range(count)])


def dot(left, right):
    return jnp.dot(left, right, preferred_element_type=F32)


def dot_nt(left, right):
    return lax.dot_general(left, right, (((1,), (1,)), ((), ())), preferred_element_type=F32)


def table_kernel(packed_ref, table_ref, scalar_ref, sem):
    groups, rows, spare = table_ref.shape[:3]
    span = spare - 1
    modes = packed_ref.shape[0] - SUBLANES
    copy = pltpu.make_async_copy(packed_ref.at[pl.ds(modes, SUBLANES)], scalar_ref, sem)
    copy.start()
    table_ref[...] = jnp.zeros_like(table_ref)
    copy.wait()
    me = lax.axis_index("energy")
    base = me // 2 * span

    def put(group, row, source, value):
        slot = source - base
        inside = jnp.logical_and(slot >= 0, slot < span)
        table_ref[group, row, jnp.where(inside, slot, span)] = value

    for mode in range(modes):
        occupied = scalar_ref[0, mode]
        shift = scalar_ref[1, mode].astype(jnp.int32)
        weight = jnp.broadcast_to(packed_ref[mode : mode + 1, :], table_ref.shape[3:])
        emission = (weight * (occupied + 1.0)).astype(BF16).astype(F32)
        absorption = (weight * occupied).astype(BF16).astype(F32)
        for group in range(groups):
            target = me ^ (2 * group)
            for row in range(rows):
                energy = target * rows + row
                if group == 0:
                    put(group, row, energy - shift, emission)
                    put(group, row, energy + shift, absorption)
                else:
                    above = target > me
                    put(
                        group,
                        row,
                        jnp.where(above, energy - shift, energy + shift),
                        jnp.where(above, emission, absorption),
                    )


def mix_kernel(group, first, table_ref, pair_ref, *rest):
    out_ref = rest[-1]
    span, square, atoms = pair_ref.shape
    rows = out_ref.shape[0]
    tile = table_ref.shape[3]
    step = min(32, square)

    def body(block, carry):
        at = pl.multiple_of(block * step, step)
        totals = [None] * rows
        for slot in range(span):
            values = pair_ref[slot, pl.ds(at, step), :].astype(F32).reshape(
                step // tile, tile, atoms
            )
            for row in range(rows):
                term = table_ref[group, first + row, slot][None] * values
                totals[row] = term if totals[row] is None else totals[row] + term
        for row in range(rows):
            out_ref[row, pl.ds(at, step), :] = totals[row].reshape(step, atoms).astype(out_ref.dtype)
        return carry

    lax.fori_loop(0, square // step, body, 0)


def hot(row, width):
    numbers = lax.broadcasted_iota(jnp.int32, (width, row.shape[1]), 0)
    return jnp.where(row == numbers, 1.0, 0.0).astype(BF16)


def prepare_kernel(derivative_ref, columns_ref, after_ref, local_k_ref, remote_k_ref, local_hot_ref, ids_ref):
    bonds, orbital, _ = derivative_ref.shape
    square = orbital * orbital
    atoms = columns_ref.shape[1]
    local_bonds = bonds - REMOTE_BONDS
    row = lax.broadcasted_iota(jnp.int32, (square, orbital), 0)
    row_of = lax.broadcasted_iota(jnp.int32, (square, orbital), 1)
    column = lax.broadcasted_iota(jnp.int32, (orbital, square), 1)
    column_of = lax.broadcasted_iota(jnp.int32, (orbital, square), 0)

    def pick(condition):
        return jnp.where(condition, 1.0, 0.0).astype(BF16)

    row_high, row_low = pick(row // orbital == row_of), pick(row % orbital == row_of)
    column_high, column_low = pick(column // orbital == column_of), pick(column % orbital == column_of)

    def spread(left, matrix, right):
        return dot(left, dot(matrix, right).astype(BF16))

    for bond in range(bonds):
        matrix = derivative_ref[bond]
        product = (
            spread(row_high, matrix, column_high) * spread(row_low, matrix, column_low)
        ).astype(BF16)
        if bond < local_bonds:
            local_k_ref[:, bond * square : (bond + 1) * square] = product
        else:
            at = bond - local_bonds
            remote_k_ref[:, at * square : (at + 1) * square] = product
    first = lax.axis_index("atom") * atoms
    for bond in range(local_bonds):
        local_hot_ref[bond * atoms : (bond + 1) * atoms, :] = hot(
            columns_ref[bond : bond + 1, :] - first, atoms
        )
    rows = []
    for bond in range(local_bonds, bonds):
        number = columns_ref[bond : bond + 1, :]
        rows += [number // atoms, number % atoms]
    place = lax.broadcasted_iota(jnp.int32, ids_ref.shape, 0)
    ids = jnp.zeros(ids_ref.shape, jnp.int32)
    for at, row in enumerate(rows):
        ids = jnp.where(place == at, row, ids)
    ids_ref[...] = ids.astype(F32).astype(BF16)


def pass_kernel(value_ref, after_ref, out_ref):
    out_ref[...] = value_ref[...]


def remote_hot_kernel(bonds, flips, *refs):
    id_refs, out_ref = refs[:-2], refs[-1]
    atoms = id_refs[0].shape[1]
    me = lax.axis_index("atom")
    for place, ids_ref in enumerate(id_refs):
        ids = ids_ref[ids_ref.shape[0] - ID_ROWS :, :].astype(F32).astype(jnp.int32)
        for which, flip in enumerate(flips):
            slab = me ^ flip
            for bond in range(bonds):
                at = (which * bonds + bond) * atoms
                number = (ids[2 * bond : 2 * bond + 1, :] - slab) * atoms + ids[
                    2 * bond + 1 : 2 * bond + 2, :
                ]
                out_ref[at : at + atoms, place * atoms : (place + 1) * atoms] = hot(number, atoms)


def local_kernel(mixed_ref, hot_ref, k_ref, *rest):
    out_ref, sums_ref = rest[-2:]
    rows, square, atoms = out_ref.shape
    bonds = hot_ref.shape[0] // atoms
    group = sums_ref.shape[1] // atoms
    for start in range(0, rows, group):
        count = min(group, rows - start)
        for inner in range(count):
            at = (start + inner) * square
            summed = dot_nt(mixed_ref[at : at + square, :], hot_ref[...]).astype(BF16)
            for bond in range(bonds):
                sums_ref[bond * square : (bond + 1) * square, inner * atoms : (inner + 1) * atoms] = (
                    summed[:, bond * atoms : (bond + 1) * atoms]
                )
        result = dot(k_ref[...], sums_ref[:, : count * atoms])
        for inner in range(count):
            out_ref[start + inner] = result[:, inner * atoms : (inner + 1) * atoms]


def remote_sums(source_refs, hot_ref, k_ref, rows, first, count, store):
    atoms = source_refs[0].shape[1]
    square = k_ref.shape[0]
    bonds = k_ref.shape[1] // square
    width = bonds * atoms
    group = max(1, 2 // count)
    for start in range(0, rows, group):
        inner = range(start, min(start + group, rows))
        pieces = [[] for _ in range(bonds)]
        for row in inner:
            sources = jnp.concatenate(
                [ref[row * square : (row + 1) * square, :] for ref in source_refs], axis=1
            )
            summed = dot_nt(sources, hot_ref[first * width : (first + count) * width, :])
            summed = summed.astype(BF16)
            for which in range(count):
                for bond in range(bonds):
                    at = which * width + bond * atoms
                    pieces[bond].append(summed[:, at : at + atoms])
        stacked = jnp.concatenate([jnp.concatenate(piece, axis=1) for piece in pieces], axis=0)
        result = dot(k_ref[...], stacked)
        for place, row in enumerate(inner):
            for which in range(count):
                at = (place * count + which) * atoms
                store(row, which, result[:, at : at + atoms])


def away_kernel(source_count, *refs):
    source_refs = refs[:source_count]
    hot_ref, k_ref = refs[source_count : source_count + 2]
    count = hot_ref.shape[0] // (k_ref.shape[1] // k_ref.shape[0] * source_refs[0].shape[1]) - 1
    out_refs = refs[len(refs) - count :]
    rows = out_refs[0].shape[0]

    def store(row, which, value):
        out_refs[which][row] = value.astype(BF16)

    remote_sums(source_refs, hot_ref, k_ref, rows, 1, count, store)


def stay_kernel(source_count, *refs):
    source_refs = refs[:source_count]
    hot_ref, k_ref, local_ref = refs[source_count : source_count + 3]
    out_ref = refs[-1]

    def store(row, which, value):
        out_ref[row] = value + local_ref[row]

    remote_sums(source_refs, hot_ref, k_ref, out_ref.shape[0], 0, 1, store)


def per_device(green_blocks, derivative, phonon_weight, occupation, mode_shift, neighbours):
    rows, orbital, _, atoms = green_blocks.shape
    square = orbital * orbital
    bonds = derivative.shape[0]
    modes = phonon_weight.shape[0]
    local_bonds = bonds - REMOTE_BONDS
    pairs = lax.axis_size("energy") // 2
    slabs = lax.axis_size("atom")
    high = [4 * i for i in range(1, slabs // 4)]
    last = max(1, rows * P_PART // 8)
    sizes = [rows - last, last]
    firsts = [0, sizes[0]]
    chunks = len(sizes)
    green = green_blocks.reshape(rows, square, atoms)
    columns = neighbours.T

    mate = swap(green, "energy", 1)

    def lanes(row):
        return jnp.pad(row.astype(F32), (0, atoms - modes))[None, :]

    packed = jnp.concatenate([phonon_weight, lanes(occupation), lanes(mode_shift)], 0)
    packed = jnp.pad(packed, ((0, SUBLANES - 2), (0, 0)))
    table = pl.pallas_call(
        table_kernel,
        out_shape=jax.ShapeDtypeStruct((pairs, rows, 2 * rows + 1, SUBLANES, atoms), F32),
        in_specs=[VMEM],
        out_specs=VMEM,
        scratch_shapes=[pltpu.SMEM((SUBLANES, atoms), F32), pltpu.SemaphoreType.DMA],
        compiler_params=params(),
        cost_estimate=cost(1e6, 1e6),
    )(packed)
    odd = lax.axis_index("energy") % 2 == 1
    pair = jnp.where(
        odd, jnp.concatenate([mate, green], 0), jnp.concatenate([green, mate], 0)
    )

    def mix(group, chunk, kind, after):
        return pl.pallas_call(
            functools.partial(mix_kernel, group, firsts[chunk]),
            out_shape=jax.ShapeDtypeStruct((sizes[chunk], square, atoms), kind),
            in_specs=[VMEM, VMEM] + [ANY] * len(after),
            out_specs=VMEM,
            compiler_params=params(),
            cost_estimate=cost(5e8, 1e6),
        )(table, pair, *after)

    def prepare(after):
        return pl.pallas_call(
            prepare_kernel,
            out_shape=(
                jax.ShapeDtypeStruct((square, local_bonds * square), BF16),
                jax.ShapeDtypeStruct((square, REMOTE_BONDS * square), BF16),
                jax.ShapeDtypeStruct((local_bonds * atoms, atoms), BF16),
                jax.ShapeDtypeStruct((ID_ROWS, atoms), BF16),
            ),
            in_specs=[VMEM, VMEM, ANY],
            out_specs=(VMEM,) * 4,
            compiler_params=params(),
            cost_estimate=cost(2e9, 3e6),
        )(derivative, columns, after)

    def local_sum(chunk, after):
        return pl.pallas_call(
            local_kernel,
            out_shape=jax.ShapeDtypeStruct((sizes[chunk], square, atoms), F32),
            in_specs=[VMEM] * 3 + [ANY] * len(after),
            out_specs=VMEM,
            scratch_shapes=[
                pltpu.VMEM((local_bonds * square, min(2, sizes[chunk]) * atoms), BF16)
            ],
            compiler_params=params(),
            cost_estimate=cost(2e9, 3e6),
        )(mixed[chunk], local_hot, local_k, *after)

    own, arrived = [], []
    after = []
    for chunk in range(chunks):
        away = [mix(group, chunk, BF16, after) for group in range(1, pairs)]
        arrived.append([swap(value, "energy", 2 * group) for group, value in enumerate(away, 1)])
        if chunk == 0:
            own.append(mix(0, chunk, F32, away[:1]))
            after = own[-1:]
        else:
            local_k, remote_k, local_hot, ids = prepare(away[0])
    mixed = []
    for chunk in range(chunks):
        if chunk > 0:
            own.append(mix(0, chunk, F32, mixed[-1:] + [local_hot]))
        total = own[chunk]
        for received in arrived[chunk]:
            total = total + received.astype(F32)
        mixed.append(jnp.concatenate([total.astype(BF16).reshape(-1, atoms), ids], 0))

    def ordered(value, after):
        return pl.pallas_call(
            pass_kernel,
            out_shape=jax.ShapeDtypeStruct(value.shape, value.dtype),
            in_specs=[VMEM, ANY],
            out_specs=VMEM,
            compiler_params=params(),
            cost_estimate=cost(1e6, 1e6),
        )(value, after)

    plans = [([2], high), (high, [2])]
    across = [[mixed[chunk]] + [swap(mixed[chunk], "atom", mask) for mask in masks]
              for chunk, (masks, _) in enumerate(plans)]
    local = [local_sum(0, mixed[-1:])]
    after = local[0]
    results, arrivals = [], []
    for chunk, (_, flips) in enumerate(plans):
        beside = across[chunk]
        if chunk > 0:
            beside = beside[:1] + [ordered(value, after) for value in beside[1:]]
            after = beside[1]
            local.append(local_sum(chunk, [after]))
            results.append(stay_sum(*waiting, after))
            after = results[-1]
        sources = across[chunk] + [swap(value, "atom", 1) for value in beside]
        hots = pl.pallas_call(
            functools.partial(remote_hot_kernel, REMOTE_BONDS, [0] + flips),
            out_shape=jax.ShapeDtypeStruct(
                ((1 + len(flips)) * REMOTE_BONDS * atoms, len(sources) * atoms), BF16
            ),
            in_specs=[VMEM] * len(sources) + [ANY],
            out_specs=VMEM,
            compiler_params=params(),
            cost_estimate=cost(1e8, 1e6),
        )(*sources, after)
        block = jax.ShapeDtypeStruct((sizes[chunk], square, atoms), BF16)
        away = pl.pallas_call(
            functools.partial(away_kernel, len(sources)),
            out_shape=(block,) * len(flips),
            in_specs=[VMEM] * (len(sources) + 2) + [ANY],
            out_specs=(VMEM,) * len(flips),
            compiler_params=params(),
            cost_estimate=cost(1e9, 3e6),
        )(*sources, hots, remote_k, after)
        received = [swap(value, "atom", flip) for value, flip in zip(away, flips)]

        def stay_sum(chunk, sources, hots, after):
            return pl.pallas_call(
                functools.partial(stay_kernel, len(sources)),
                out_shape=jax.ShapeDtypeStruct((sizes[chunk], square, atoms), F32),
                in_specs=[VMEM] * (len(sources) + 3) + [ANY],
                out_specs=VMEM,
                compiler_params=params(),
                cost_estimate=cost(1e9, 3e6),
            )(*sources, hots, remote_k, local[chunk], after)

        arrivals.append(received)
        waiting = (chunk, sources, hots)
        after = away[0]
    results.append(stay_sum(*waiting, after))
    combined = []
    for stay, received in zip(results, arrivals):
        for value in received:
            stay = stay + value.astype(F32)
        combined.append(stay)
    return jnp.concatenate(combined, 0).reshape(rows, orbital, orbital, atoms)


def solution(mesh):
    in_specs = (P("energy", None, None, "atom"), P(), P(None, "atom"), P(), P(), P("atom", None))
    out_specs = P("energy", None, None, "atom")
    return jax.shard_map(
        per_device, mesh=mesh, in_specs=in_specs, out_specs=out_specs, check_vma=False
    )
```

```python
import functools

import jax
import jax.numpy as jnp
from jax import lax
from jax.experimental import pallas as pl
from jax.experimental.pallas import tpu as pltpu
from jax.sharding import PartitionSpec as P

REMOTE_BONDS = 2
ID_ROWS = 16
P_PART = 4
COST = 1.0
SUBLANES = 8
VMEM_LIMIT = 48 * 1024 * 1024

VMEM = pl.BlockSpec(memory_space=pltpu.VMEM)
SMEM = pl.BlockSpec(memory_space=pltpu.SMEM)
ANY = pl.BlockSpec(memory_space=pl.ANY)
F32, BF16 = jnp.float32, jnp.bfloat16


def params():
    return pltpu.CompilerParams(vmem_limit_bytes=VMEM_LIMIT)


def cost(flops, nbytes):
    return pl.CostEstimate(flops=int(flops * COST), bytes_accessed=int(nbytes * COST), transcendentals=0)


def swap(value, axis, mask):
    count = lax.axis_size(axis)
    return lax.ppermute(value, axis, [(i, i ^ mask) for i in range(count)])


def dot(left, right):
    return jnp.dot(left, right, preferred_element_type=F32)


def dot_nt(left, right):
    return lax.dot_general(left, right, (((1,), (1,)), ((), ())), preferred_element_type=F32)


def mix_kernel(group, first, shift_ref, coupling_ref, own_ref, mate_ref, *rest):
    out_ref, table_ref = rest[-2:]
    span, square, atoms = own_ref.shape
    rows = out_ref.shape[0]
    tile = table_ref.shape[2]
    modes = coupling_ref.shape[0] // 2
    me = lax.axis_index("energy")
    base = me // 2 * 2 * span
    move = me % 2 * span
    target = me ^ (2 * group)
    table_ref[...] = jnp.zeros_like(table_ref)
    couplings = coupling_ref[...].astype(F32)

    def put(row, source, value):
        place = source - base
        slot = jnp.where(place < span, place + move, place - move)
        inside = jnp.logical_and(place >= 0, place < 2 * span)
        table_ref[row, jnp.where(inside, slot, 2 * span)] = value

    for mode in range(modes):
        shift = shift_ref[mode]
        emission = jnp.broadcast_to(couplings[mode : mode + 1, :], (tile, atoms))
        absorption = jnp.broadcast_to(couplings[modes + mode : modes + mode + 1, :], (tile, atoms))
        if group > 0:
            above = target > me
            sign = jnp.where(above, -shift, shift)
            coupling = jnp.where(above, emission, absorption)
        for row in range(rows):
            energy = target * span + first + row
            if group == 0:
                put(row, energy - shift, emission)
                put(row, energy + shift, absorption)
            else:
                put(row, energy + sign, coupling)

    step = min(32, square)

    def body(block, carry):
        at = pl.multiple_of(block * step, step)
        totals = [None] * rows
        for slot in range(2 * span):
            ref = own_ref if slot < span else mate_ref
            values = ref[slot % span, pl.ds(at, step), :].astype(F32).reshape(
                step // tile, tile, atoms
            )
            for row in range(rows):
                term = table_ref[row, slot][None] * values
                totals[row] = term if totals[row] is None else totals[row] + term
        for row in range(rows):
            out_ref[row, pl.ds(at, step), :] = totals[row].reshape(step, atoms).astype(out_ref.dtype)
        return carry

    lax.fori_loop(0, square // step, body, 0)


def hot(row, width):
    numbers = lax.broadcasted_iota(jnp.int32, (width, row.shape[1]), 0)
    return jnp.where(row == numbers, 1.0, 0.0).astype(BF16)


def prepare_kernel(derivative_ref, columns_ref, after_ref, local_k_ref, remote_k_ref, local_hot_ref, ids_ref):
    bonds, orbital, _ = derivative_ref.shape
    square = orbital * orbital
    atoms = columns_ref.shape[1]
    local_bonds = bonds - REMOTE_BONDS
    row = lax.broadcasted_iota(jnp.int32, (square, orbital), 0)
    row_of = lax.broadcasted_iota(jnp.int32, (square, orbital), 1)
    column = lax.broadcasted_iota(jnp.int32, (orbital, square), 1)
    column_of = lax.broadcasted_iota(jnp.int32, (orbital, square), 0)

    def pick(condition):
        return jnp.where(condition, 1.0, 0.0).astype(BF16)

    row_high, row_low = pick(row // orbital == row_of), pick(row % orbital == row_of)
    column_high, column_low = pick(column // orbital == column_of), pick(column % orbital == column_of)

    def spread(left, matrix, right):
        return dot(left, dot(matrix, right).astype(BF16))

    for bond in range(bonds):
        matrix = derivative_ref[bond]
        product = (
            spread(row_high, matrix, column_high) * spread(row_low, matrix, column_low)
        ).astype(BF16)
        if bond < local_bonds:
            local_k_ref[:, bond * square : (bond + 1) * square] = product
        else:
            at = bond - local_bonds
            remote_k_ref[:, at * square : (at + 1) * square] = product
    first = lax.axis_index("atom") * atoms
    for bond in range(local_bonds):
        local_hot_ref[bond * atoms : (bond + 1) * atoms, :] = hot(
            columns_ref[bond : bond + 1, :] - first, atoms
        )
    rows = []
    for bond in range(local_bonds, bonds):
        number = columns_ref[bond : bond + 1, :]
        rows += [number // atoms, number % atoms]
    place = lax.broadcasted_iota(jnp.int32, ids_ref.shape, 0)
    ids = jnp.zeros(ids_ref.shape, jnp.int32)
    for at, row in enumerate(rows):
        ids = jnp.where(place == at, row, ids)
    ids_ref[...] = ids.astype(F32).astype(BF16)


def pass_kernel(value_ref, after_ref, out_ref):
    out_ref[...] = value_ref[...]


def remote_hot_kernel(bonds, flips, *refs):
    id_refs, out_ref = refs[:-2], refs[-1]
    atoms = id_refs[0].shape[1]
    me = lax.axis_index("atom")
    for place, ids_ref in enumerate(id_refs):
        ids = ids_ref[ids_ref.shape[0] - ID_ROWS :, :].astype(F32).astype(jnp.int32)
        for which, flip in enumerate(flips):
            slab = me ^ flip
            for bond in range(bonds):
                at = (which * bonds + bond) * atoms
                number = (ids[2 * bond : 2 * bond + 1, :] - slab) * atoms + ids[
                    2 * bond + 1 : 2 * bond + 2, :
                ]
                out_ref[at : at + atoms, place * atoms : (place + 1) * atoms] = hot(number, atoms)


def local_kernel(mixed_ref, hot_ref, k_ref, *rest):
    out_ref, sums_ref = rest[-2:]
    rows, square, atoms = out_ref.shape
    bonds = hot_ref.shape[0] // atoms
    group = sums_ref.shape[1] // atoms
    for start in range(0, rows, group):
        count = min(group, rows - start)
        for inner in range(count):
            at = (start + inner) * square
            summed = dot_nt(mixed_ref[at : at + square, :], hot_ref[...]).astype(BF16)
            for bond in range(bonds):
                sums_ref[bond * square : (bond + 1) * square, inner * atoms : (inner + 1) * atoms] = (
                    summed[:, bond * atoms : (bond + 1) * atoms]
                )
        result = dot(k_ref[...], sums_ref[:, : count * atoms])
        for inner in range(count):
            out_ref[start + inner] = result[:, inner * atoms : (inner + 1) * atoms]


def remote_sums(source_refs, hot_ref, k_ref, rows, first, count, store):
    atoms = source_refs[0].shape[1]
    square = k_ref.shape[0]
    bonds = k_ref.shape[1] // square
    width = bonds * atoms
    group = max(1, 2 // count)
    for start in range(0, rows, group):
        inner = range(start, min(start + group, rows))
        pieces = [[] for _ in range(bonds)]
        for row in inner:
            sources = jnp.concatenate(
                [ref[row * square : (row + 1) * square, :] for ref in source_refs], axis=1
            )
            summed = dot_nt(sources, hot_ref[first * width : (first + count) * width, :])
            summed = summed.astype(BF16)
            for which in range(count):
                for bond in range(bonds):
                    at = which * width + bond * atoms
                    pieces[bond].append(summed[:, at : at + atoms])
        stacked = jnp.concatenate([jnp.concatenate(piece, axis=1) for piece in pieces], axis=0)
        result = dot(k_ref[...], stacked)
        for place, row in enumerate(inner):
            for which in range(count):
                at = (place * count + which) * atoms
                store(row, which, result[:, at : at + atoms])


def away_kernel(source_count, *refs):
    source_refs = refs[:source_count]
    hot_ref, k_ref = refs[source_count : source_count + 2]
    count = hot_ref.shape[0] // (k_ref.shape[1] // k_ref.shape[0] * source_refs[0].shape[1]) - 1
    out_refs = refs[len(refs) - count :]
    rows = out_refs[0].shape[0]

    def store(row, which, value):
        out_refs[which][row] = value.astype(BF16)

    remote_sums(source_refs, hot_ref, k_ref, rows, 1, count, store)


def stay_kernel(source_count, *refs):
    source_refs = refs[:source_count]
    hot_ref, k_ref, local_ref = refs[source_count : source_count + 3]
    out_ref = refs[-1]

    def store(row, which, value):
        out_ref[row] = value + local_ref[row]

    remote_sums(source_refs, hot_ref, k_ref, out_ref.shape[0], 0, 1, store)


def per_device(green_blocks, derivative, phonon_weight, occupation, mode_shift, neighbours):
    rows, orbital, _, atoms = green_blocks.shape
    square = orbital * orbital
    bonds = derivative.shape[0]
    modes = phonon_weight.shape[0]
    local_bonds = bonds - REMOTE_BONDS
    pairs = lax.axis_size("energy") // 2
    slabs = lax.axis_size("atom")
    high = [4 * i for i in range(1, slabs // 4)]
    last = max(1, rows * P_PART // 8)
    sizes = [rows - last, last]
    firsts = [0, sizes[0]]
    chunks = len(sizes)
    green = green_blocks.reshape(rows, square, atoms)
    columns = neighbours.T

    mate = swap(green, "energy", 1)

    occupied = occupation[:, None]
    couplings = jnp.concatenate(
        [phonon_weight * (occupied + 1.0), phonon_weight * occupied], 0
    ).astype(BF16)

    def mix(group, chunk, kind, after):
        return pl.pallas_call(
            functools.partial(mix_kernel, group, firsts[chunk]),
            out_shape=jax.ShapeDtypeStruct((sizes[chunk], square, atoms), kind),
            in_specs=[SMEM, VMEM, VMEM, VMEM] + [ANY] * len(after),
            out_specs=VMEM,
            scratch_shapes=[pltpu.VMEM((sizes[chunk], 2 * rows + 1, SUBLANES, atoms), F32)],
            compiler_params=params(),
            cost_estimate=cost(5e8, 1e6),
        )(mode_shift, couplings, green, mate, *after)

    def prepare(after):
        return pl.pallas_call(
            prepare_kernel,
            out_shape=(
                jax.ShapeDtypeStruct((square, local_bonds * square), BF16),
                jax.ShapeDtypeStruct((square, REMOTE_BONDS * square), BF16),
                jax.ShapeDtypeStruct((local_bonds * atoms, atoms), BF16),
                jax.ShapeDtypeStruct((ID_ROWS, atoms), BF16),
            ),
            in_specs=[VMEM, VMEM, ANY],
            out_specs=(VMEM,) * 4,
            compiler_params=params(),
            cost_estimate=cost(2e9, 3e6),
        )(derivative, columns, after)

    def local_sum(chunk, after):
        return pl.pallas_call(
            local_kernel,
            out_shape=jax.ShapeDtypeStruct((sizes[chunk], square, atoms), F32),
            in_specs=[VMEM] * 3 + [ANY] * len(after),
            out_specs=VMEM,
            scratch_shapes=[
                pltpu.VMEM((local_bonds * square, min(2, sizes[chunk]) * atoms), BF16)
            ],
            compiler_params=params(),
            cost_estimate=cost(2e9, 3e6),
        )(mixed[chunk], local_hot, local_k, *after)

    own, arrived = [], []
    after = []
    for chunk in range(chunks):
        away = [mix(group, chunk, BF16, after) for group in range(1, pairs)]
        arrived.append([swap(value, "energy", 2 * group) for group, value in enumerate(away, 1)])
        if chunk == 0:
            own.append(mix(0, chunk, F32, away[:1]))
            after = own[-1:]
        else:
            local_k, remote_k, local_hot, ids = prepare(away[0])
    mixed = []
    for chunk in range(chunks):
        if chunk > 0:
            own.append(mix(0, chunk, F32, mixed[-1:] + [local_hot]))
        total = own[chunk]
        for received in arrived[chunk]:
            total = total + received.astype(F32)
        mixed.append(jnp.concatenate([total.astype(BF16).reshape(-1, atoms), ids], 0))

    def ordered(value, after):
        return pl.pallas_call(
            pass_kernel,
            out_shape=jax.ShapeDtypeStruct(value.shape, value.dtype),
            in_specs=[VMEM, ANY],
            out_specs=VMEM,
            compiler_params=params(),
            cost_estimate=cost(1e6, 1e6),
        )(value, after)

    plans = [([2, 1, 3], high), (high, [2])]
    across = [[mixed[chunk]] + [swap(mixed[chunk], "atom", mask) for mask in masks]
              for chunk, (masks, _) in enumerate(plans)]
    local = [local_sum(0, mixed[-1:])]
    after = local[0]
    results, arrivals = [], []
    for chunk, (_, flips) in enumerate(plans):
        if chunk == 0:
            sources = across[chunk]
        else:
            beside = [mixed[chunk]] + [ordered(value, after) for value in across[chunk][1:]]
            sources = across[chunk] + [swap(value, "atom", 1) for value in beside]
            after = beside[1]
            local.append(local_sum(chunk, [after]))
            results.append(stay_sum(*waiting, after))
            after = results[-1]
        hots = pl.pallas_call(
            functools.partial(remote_hot_kernel, REMOTE_BONDS, [0] + flips),
            out_shape=jax.ShapeDtypeStruct(
                ((1 + len(flips)) * REMOTE_BONDS * atoms, len(sources) * atoms), BF16
            ),
            in_specs=[VMEM] * len(sources) + [ANY],
            out_specs=VMEM,
            compiler_params=params(),
            cost_estimate=cost(1e8, 1e6),
        )(*sources, after)
        block = jax.ShapeDtypeStruct((sizes[chunk], square, atoms), BF16)
        away = pl.pallas_call(
            functools.partial(away_kernel, len(sources)),
            out_shape=(block,) * len(flips),
            in_specs=[VMEM] * (len(sources) + 2) + [ANY],
            out_specs=(VMEM,) * len(flips),
            compiler_params=params(),
            cost_estimate=cost(1e9, 3e6),
        )(*sources, hots, remote_k, after)
        received = [swap(value, "atom", flip) for value, flip in zip(away, flips)]

        def stay_sum(chunk, sources, hots, after):
            return pl.pallas_call(
                functools.partial(stay_kernel, len(sources)),
                out_shape=jax.ShapeDtypeStruct((sizes[chunk], square, atoms), F32),
                in_specs=[VMEM] * (len(sources) + 3) + [ANY],
                out_specs=VMEM,
                compiler_params=params(),
                cost_estimate=cost(1e9, 3e6),
            )(*sources, hots, remote_k, local[chunk], after)

        arrivals.append(received)
        waiting = (chunk, sources, hots)
        after = away[0]
    results.append(stay_sum(*waiting, after))
    combined = []
    for stay, received in zip(results, arrivals):
        for value in received:
            stay = stay + value.astype(F32)
        combined.append(stay)
    return jnp.concatenate(combined, 0).reshape(rows, orbital, orbital, atoms)


def solution(mesh):
    in_specs = (P("energy", None, None, "atom"), P(), P(None, "atom"), P(), P(), P("atom", None))
    out_specs = P("energy", None, None, "atom")
    return jax.shard_map(
        per_device, mesh=mesh, in_specs=in_specs, out_specs=out_specs, check_vma=False
    )
```

```python
import functools

import jax
import jax.numpy as jnp
from jax import lax
from jax.experimental import pallas as pl
from jax.experimental.pallas import tpu as pltpu
from jax.sharding import PartitionSpec as P

REMOTE_BONDS = 2
ID_ROWS = 16
P_PART = 4
COST = 1.0
SUBLANES = 8
VMEM_LIMIT = 48 * 1024 * 1024

VMEM = pl.BlockSpec(memory_space=pltpu.VMEM)
SMEM = pl.BlockSpec(memory_space=pltpu.SMEM)
ANY = pl.BlockSpec(memory_space=pl.ANY)
F32, BF16 = jnp.float32, jnp.bfloat16


def params():
    return pltpu.CompilerParams(vmem_limit_bytes=VMEM_LIMIT)


def cost(flops, nbytes):
    return pl.CostEstimate(flops=int(flops * COST), bytes_accessed=int(nbytes * COST), transcendentals=0)


def swap(value, axis, mask):
    count = lax.axis_size(axis)
    return lax.ppermute(value, axis, [(i, i ^ mask) for i in range(count)])


def dot(left, right):
    return jnp.dot(left, right, preferred_element_type=F32)


def dot_nt(left, right):
    return lax.dot_general(left, right, (((1,), (1,)), ((), ())), preferred_element_type=F32)


def mix_kernel(group, first, shift_ref, coupling_ref, own_ref, mate_ref, *rest):
    out_ref, table_ref = rest[-2:]
    span, square, atoms = own_ref.shape
    rows = out_ref.shape[0]
    tile = table_ref.shape[2]
    modes = coupling_ref.shape[0] // 2
    me = lax.axis_index("energy")
    base = me // 2 * 2 * span
    move = me % 2 * span
    target = me ^ (2 * group)
    table_ref[...] = jnp.zeros_like(table_ref)
    couplings = coupling_ref[...].astype(F32)

    def put(row, source, value):
        place = source - base
        slot = jnp.where(place < span, place + move, place - move)
        inside = jnp.logical_and(place >= 0, place < 2 * span)
        table_ref[row, jnp.where(inside, slot, 2 * span)] = value

    for mode in range(modes):
        shift = shift_ref[mode]
        emission = jnp.broadcast_to(couplings[mode : mode + 1, :], (tile, atoms))
        absorption = jnp.broadcast_to(couplings[modes + mode : modes + mode + 1, :], (tile, atoms))
        if group > 0:
            above = target > me
            sign = jnp.where(above, -shift, shift)
            coupling = jnp.where(above, emission, absorption)
        for row in range(rows):
            energy = target * span + first + row
            if group == 0:
                put(row, energy - shift, emission)
                put(row, energy + shift, absorption)
            else:
                put(row, energy + sign, coupling)

    step = min(32, square)

    def body(block, carry):
        at = pl.multiple_of(block * step, step)
        totals = [None] * rows
        for slot in range(2 * span):
            ref = own_ref if slot < span else mate_ref
            values = ref[slot % span, pl.ds(at, step), :].astype(F32).reshape(
                step // tile, tile, atoms
            )
            for row in range(rows):
                term = table_ref[row, slot][None] * values
                totals[row] = term if totals[row] is None else totals[row] + term
        for row in range(rows):
            out_ref[row, pl.ds(at, step), :] = totals[row].reshape(step, atoms).astype(out_ref.dtype)
        return carry

    lax.fori_loop(0, square // step, body, 0)


def hot(row, width):
    numbers = lax.broadcasted_iota(jnp.int32, (width, row.shape[1]), 0)
    return jnp.where(row == numbers, 1.0, 0.0).astype(BF16)


def prepare_kernel(derivative_ref, columns_ref, after_ref, local_k_ref, remote_k_ref, local_hot_ref, ids_ref):
    bonds, orbital, _ = derivative_ref.shape
    square = orbital * orbital
    atoms = columns_ref.shape[1]
    local_bonds = bonds - REMOTE_BONDS
    row = lax.broadcasted_iota(jnp.int32, (square, orbital), 0)
    row_of = lax.broadcasted_iota(jnp.int32, (square, orbital), 1)
    column = lax.broadcasted_iota(jnp.int32, (orbital, square), 1)
    column_of = lax.broadcasted_iota(jnp.int32, (orbital, square), 0)

    def pick(condition):
        return jnp.where(condition, 1.0, 0.0).astype(BF16)

    row_high, row_low = pick(row // orbital == row_of), pick(row % orbital == row_of)
    column_high, column_low = pick(column // orbital == column_of), pick(column % orbital == column_of)

    def spread(left, matrix, right):
        return dot(left, dot(matrix, right).astype(BF16))

    for bond in range(bonds):
        matrix = derivative_ref[bond]
        product = (
            spread(row_high, matrix, column_high) * spread(row_low, matrix, column_low)
        ).astype(BF16)
        if bond < local_bonds:
            local_k_ref[:, bond * square : (bond + 1) * square] = product
        else:
            at = bond - local_bonds
            remote_k_ref[:, at * square : (at + 1) * square] = product
    first = lax.axis_index("atom") * atoms
    for bond in range(local_bonds):
        local_hot_ref[bond * atoms : (bond + 1) * atoms, :] = hot(
            columns_ref[bond : bond + 1, :] - first, atoms
        )
    rows = []
    for bond in range(local_bonds, bonds):
        number = columns_ref[bond : bond + 1, :]
        rows += [number // atoms, number % atoms]
    place = lax.broadcasted_iota(jnp.int32, ids_ref.shape, 0)
    ids = jnp.zeros(ids_ref.shape, jnp.int32)
    for at, row in enumerate(rows):
        ids = jnp.where(place == at, row, ids)
    ids_ref[...] = ids.astype(F32).astype(BF16)


def pass_kernel(value_ref, after_ref, out_ref):
    out_ref[...] = value_ref[...]


def remote_hot_kernel(bonds, flips, *refs):
    id_refs, out_ref = refs[:-2], refs[-1]
    atoms = id_refs[0].shape[1]
    me = lax.axis_index("atom")
    for place, ids_ref in enumerate(id_refs):
        ids = ids_ref[ids_ref.shape[0] - ID_ROWS :, :].astype(F32).astype(jnp.int32)
        for which, flip in enumerate(flips):
            slab = me ^ flip
            for bond in range(bonds):
                at = (which * bonds + bond) * atoms
                number = (ids[2 * bond : 2 * bond + 1, :] - slab) * atoms + ids[
                    2 * bond + 1 : 2 * bond + 2, :
                ]
                out_ref[at : at + atoms, place * atoms : (place + 1) * atoms] = hot(number, atoms)


def local_kernel(mixed_ref, hot_ref, k_ref, *rest):
    out_ref, sums_ref = rest[-2:]
    rows, square, atoms = out_ref.shape
    bonds = hot_ref.shape[0] // atoms
    group = sums_ref.shape[1] // atoms
    for start in range(0, rows, group):
        count = min(group, rows - start)
        for inner in range(count):
            at = (start + inner) * square
            summed = dot_nt(mixed_ref[at : at + square, :], hot_ref[...]).astype(BF16)
            for bond in range(bonds):
                sums_ref[bond * square : (bond + 1) * square, inner * atoms : (inner + 1) * atoms] = (
                    summed[:, bond * atoms : (bond + 1) * atoms]
                )
        result = dot(k_ref[...], sums_ref[:, : count * atoms])
        for inner in range(count):
            out_ref[start + inner] = result[:, inner * atoms : (inner + 1) * atoms]


def remote_sums(source_refs, hot_ref, k_ref, rows, first, count, store):
    atoms = source_refs[0].shape[1]
    square = k_ref.shape[0]
    bonds = k_ref.shape[1] // square
    width = bonds * atoms
    group = max(1, 2 // count)
    for start in range(0, rows, group):
        inner = range(start, min(start + group, rows))
        pieces = [[] for _ in range(bonds)]
        for row in inner:
            sources = jnp.concatenate(
                [ref[row * square : (row + 1) * square, :] for ref in source_refs], axis=1
            )
            summed = dot_nt(sources, hot_ref[first * width : (first + count) * width, :])
            summed = summed.astype(BF16)
            for which in range(count):
                for bond in range(bonds):
                    at = which * width + bond * atoms
                    pieces[bond].append(summed[:, at : at + atoms])
        stacked = jnp.concatenate([jnp.concatenate(piece, axis=1) for piece in pieces], axis=0)
        result = dot(k_ref[...], stacked)
        for place, row in enumerate(inner):
            for which in range(count):
                at = (place * count + which) * atoms
                store(row, which, result[:, at : at + atoms])


def away_kernel(source_count, *refs):
    source_refs = refs[:source_count]
    hot_ref, k_ref = refs[source_count : source_count + 2]
    count = hot_ref.shape[0] // (k_ref.shape[1] // k_ref.shape[0] * source_refs[0].shape[1]) - 1
    out_refs = refs[len(refs) - count :]
    rows = out_refs[0].shape[0]

    def store(row, which, value):
        out_refs[which][row] = value.astype(BF16)

    remote_sums(source_refs, hot_ref, k_ref, rows, 1, count, store)


def stay_kernel(source_count, *refs):
    source_refs = refs[:source_count]
    hot_ref, k_ref, local_ref = refs[source_count : source_count + 3]
    out_ref = refs[-1]

    def store(row, which, value):
        out_ref[row] = value + local_ref[row]

    remote_sums(source_refs, hot_ref, k_ref, out_ref.shape[0], 0, 1, store)


def per_device(green_blocks, derivative, phonon_weight, occupation, mode_shift, neighbours):
    rows, orbital, _, atoms = green_blocks.shape
    square = orbital * orbital
    bonds = derivative.shape[0]
    modes = phonon_weight.shape[0]
    local_bonds = bonds - REMOTE_BONDS
    pairs = lax.axis_size("energy") // 2
    slabs = lax.axis_size("atom")
    high = [4 * i for i in range(1, slabs // 4)]
    last = max(1, rows * P_PART // 8)
    sizes = [rows - last, last]
    firsts = [0, sizes[0]]
    chunks = len(sizes)
    green = green_blocks.reshape(rows, square, atoms)
    columns = neighbours.T

    mate = swap(green, "energy", 1)

    kind = lax.broadcasted_iota(jnp.int32, (2, modes, atoms), 0)
    occupied = jnp.broadcast_to(occupation[None, :, None], kind.shape)
    couplings = phonon_weight[None] * jnp.where(kind == 0, occupied + 1.0, occupied)
    couplings = couplings.reshape(2 * modes, atoms).astype(BF16)

    def mix(group, chunk, kind, after):
        return pl.pallas_call(
            functools.partial(mix_kernel, group, firsts[chunk]),
            out_shape=jax.ShapeDtypeStruct((sizes[chunk], square, atoms), kind),
            in_specs=[SMEM, VMEM, VMEM, VMEM] + [ANY] * len(after),
            out_specs=VMEM,
            scratch_shapes=[pltpu.VMEM((sizes[chunk], 2 * rows + 1, SUBLANES, atoms), F32)],
            compiler_params=params(),
            cost_estimate=cost(5e8, 1e6),
        )(mode_shift, couplings, green, mate, *after)

    def prepare(after):
        return pl.pallas_call(
            prepare_kernel,
            out_shape=(
                jax.ShapeDtypeStruct((square, local_bonds * square), BF16),
                jax.ShapeDtypeStruct((square, REMOTE_BONDS * square), BF16),
                jax.ShapeDtypeStruct((local_bonds * atoms, atoms), BF16),
                jax.ShapeDtypeStruct((ID_ROWS, atoms), BF16),
            ),
            in_specs=[VMEM, VMEM, ANY],
            out_specs=(VMEM,) * 4,
            compiler_params=params(),
            cost_estimate=cost(2e9, 3e6),
        )(derivative, columns, after)

    def local_sum(chunk, after):
        return pl.pallas_call(
            local_kernel,
            out_shape=jax.ShapeDtypeStruct((sizes[chunk], square, atoms), F32),
            in_specs=[VMEM] * 3 + [ANY] * len(after),
            out_specs=VMEM,
            scratch_shapes=[
                pltpu.VMEM((local_bonds * square, min(2, sizes[chunk]) * atoms), BF16)
            ],
            compiler_params=params(),
            cost_estimate=cost(2e9, 3e6),
        )(mixed[chunk], local_hot, local_k, *after)

    own, arrived = [], []
    after = []
    for chunk in range(chunks):
        away = [mix(group, chunk, BF16, after) for group in range(1, pairs)]
        arrived.append([swap(value, "energy", 2 * group) for group, value in enumerate(away, 1)])
        if chunk == 0:
            own.append(mix(0, chunk, F32, away[:1]))
            after = own[-1:]
        else:
            local_k, remote_k, local_hot, ids = prepare(away[0])
    mixed = []
    for chunk in range(chunks):
        if chunk > 0:
            own.append(mix(0, chunk, F32, mixed[-1:] + [local_hot]))
        total = own[chunk]
        for received in arrived[chunk]:
            total = total + received.astype(F32)
        mixed.append(jnp.concatenate([total.astype(BF16).reshape(-1, atoms), ids], 0))

    def ordered(value, after):
        return pl.pallas_call(
            pass_kernel,
            out_shape=jax.ShapeDtypeStruct(value.shape, value.dtype),
            in_specs=[VMEM, ANY],
            out_specs=VMEM,
            compiler_params=params(),
            cost_estimate=cost(1e6, 1e6),
        )(value, after)

    def one_hots(sources, flips, after):
        return pl.pallas_call(
            functools.partial(remote_hot_kernel, REMOTE_BONDS, [0] + flips),
            out_shape=jax.ShapeDtypeStruct(
                ((1 + len(flips)) * REMOTE_BONDS * atoms, len(sources) * atoms), BF16
            ),
            in_specs=[VMEM] * len(sources) + [ANY],
            out_specs=VMEM,
            compiler_params=params(),
            cost_estimate=cost(1e8, 1e6),
        )(*sources, after)

    def away_sums(chunk, sources, hots, flips, after):
        block = jax.ShapeDtypeStruct((sizes[chunk], square, atoms), BF16)
        return pl.pallas_call(
            functools.partial(away_kernel, len(sources)),
            out_shape=(block,) * len(flips),
            in_specs=[VMEM] * (len(sources) + 2) + [ANY],
            out_specs=(VMEM,) * len(flips),
            compiler_params=params(),
            cost_estimate=cost(1e9, 3e6),
        )(*sources, hots, remote_k, after)

    def stay_sum(chunk, sources, hots, local, after):
        return pl.pallas_call(
            functools.partial(stay_kernel, len(sources)),
            out_shape=jax.ShapeDtypeStruct((sizes[chunk], square, atoms), F32),
            in_specs=[VMEM] * (len(sources) + 3) + [ANY],
            out_specs=VMEM,
            compiler_params=params(),
            cost_estimate=cost(1e9, 3e6),
        )(*sources, hots, remote_k, local, after)

    def send(values, masks):
        return [swap(value, "atom", mask) for value, mask in zip(values, masks)]

    outer, inner = mixed
    far = send([outer] * len(high), high)
    near = send([inner] * 3, [2, 1, 3])
    local_outer = local_sum(0, [inner])
    passed = [ordered(value, local_outer) for value in far]
    outer_sources = [outer] + far + send([outer] + passed, [1] * (1 + len(passed)))
    local_inner = local_sum(1, passed[:1])
    inner_sources = [inner] + near
    inner_hots = one_hots(inner_sources, high, local_inner)
    inner_away = away_sums(1, inner_sources, inner_hots, high, local_inner)
    outer_hots = one_hots(outer_sources, [2], inner_away[0])
    outer_away = away_sums(0, outer_sources, outer_hots, [2], inner_away[0])
    inner_stay = stay_sum(1, inner_sources, inner_hots, local_inner, outer_away[0])
    outer_stay = stay_sum(0, outer_sources, outer_hots, local_outer, inner_stay)
    results = [outer_stay, inner_stay]
    arrivals = [send(outer_away, [2]), send(inner_away, high)]
    combined = []
    for stay, received in zip(results, arrivals):
        for value in received:
            stay = stay + value.astype(F32)
        combined.append(stay)
    return jnp.concatenate(combined, 0).reshape(rows, orbital, orbital, atoms)


def solution(mesh):
    in_specs = (P("energy", None, None, "atom"), P(), P(None, "atom"), P(), P(), P("atom", None))
    out_specs = P("energy", None, None, "atom")
    return jax.shard_map(
        per_device, mesh=mesh, in_specs=in_specs, out_specs=out_specs, check_vma=False
    )
```

```python
import functools

import jax
import jax.numpy as jnp
from jax import lax
from jax.experimental import pallas as pl
from jax.experimental.pallas import tpu as pltpu
from jax.sharding import PartitionSpec as P

REMOTE_BONDS = 2
ID_ROWS = 16
P_PART = 4
COST = 1.0
SUBLANES = 8
VMEM_LIMIT = 48 * 1024 * 1024

VMEM = pl.BlockSpec(memory_space=pltpu.VMEM)
SMEM = pl.BlockSpec(memory_space=pltpu.SMEM)
ANY = pl.BlockSpec(memory_space=pl.ANY)
F32, BF16 = jnp.float32, jnp.bfloat16


def params():
    return pltpu.CompilerParams(vmem_limit_bytes=VMEM_LIMIT)


def cost(flops, nbytes):
    return pl.CostEstimate(flops=int(flops * COST), bytes_accessed=int(nbytes * COST), transcendentals=0)


def swap(value, axis, mask):
    count = lax.axis_size(axis)
    return lax.ppermute(value, axis, [(i, i ^ mask) for i in range(count)])


def dot(left, right):
    return jnp.dot(left, right, preferred_element_type=F32)


def dot_nt(left, right):
    return lax.dot_general(left, right, (((1,), (1,)), ((), ())), preferred_element_type=F32)


def mix_kernel(group, first, shift_ref, coupling_ref, own_ref, mate_ref, *rest):
    out_ref, table_ref = rest[-2:]
    span, square, atoms = own_ref.shape
    rows = out_ref.shape[0]
    tile = table_ref.shape[2]
    modes = coupling_ref.shape[0] // 2
    me = lax.axis_index("energy")
    base = me // 2 * 2 * span
    move = me % 2 * span
    target = me ^ (2 * group)
    table_ref[...] = jnp.zeros_like(table_ref)
    couplings = coupling_ref[...].astype(F32)

    def put(row, source, value):
        place = source - base
        slot = jnp.where(place < span, place + move, place - move)
        inside = jnp.logical_and(place >= 0, place < 2 * span)
        table_ref[row, jnp.where(inside, slot, 2 * span)] = value

    for mode in range(modes):
        shift = shift_ref[mode]
        emission = jnp.broadcast_to(couplings[mode : mode + 1, :], (tile, atoms))
        absorption = jnp.broadcast_to(couplings[modes + mode : modes + mode + 1, :], (tile, atoms))
        if group > 0:
            above = target > me
            sign = jnp.where(above, -shift, shift)
            coupling = jnp.where(above, emission, absorption)
        for row in range(rows):
            energy = target * span + first + row
            if group == 0:
                put(row, energy - shift, emission)
                put(row, energy + shift, absorption)
            else:
                put(row, energy + sign, coupling)

    step = min(32, square)

    def body(block, carry):
        at = pl.multiple_of(block * step, step)
        totals = [None] * rows
        for slot in range(2 * span):
            ref = own_ref if slot < span else mate_ref
            values = ref[slot % span, pl.ds(at, step), :].astype(F32).reshape(
                step // tile, tile, atoms
            )
            for row in range(rows):
                term = table_ref[row, slot][None] * values
                totals[row] = term if totals[row] is None else totals[row] + term
        for row in range(rows):
            out_ref[row, pl.ds(at, step), :] = totals[row].reshape(step, atoms).astype(out_ref.dtype)
        return carry

    lax.fori_loop(0, square // step, body, 0)


def hot(row, width):
    numbers = lax.broadcasted_iota(jnp.int32, (width, row.shape[1]), 0)
    return jnp.where(row == numbers, 1.0, 0.0).astype(BF16)


def prepare_kernel(derivative_ref, columns_ref, after_ref, local_k_ref, remote_k_ref, local_hot_ref, ids_ref):
    bonds, orbital, _ = derivative_ref.shape
    square = orbital * orbital
    atoms = columns_ref.shape[1]
    local_bonds = bonds - REMOTE_BONDS
    row = lax.broadcasted_iota(jnp.int32, (square, orbital), 0)
    row_of = lax.broadcasted_iota(jnp.int32, (square, orbital), 1)
    column = lax.broadcasted_iota(jnp.int32, (orbital, square), 1)
    column_of = lax.broadcasted_iota(jnp.int32, (orbital, square), 0)

    def pick(condition):
        return jnp.where(condition, 1.0, 0.0).astype(BF16)

    row_high, row_low = pick(row // orbital == row_of), pick(row % orbital == row_of)
    column_high, column_low = pick(column // orbital == column_of), pick(column % orbital == column_of)

    def spread(left, matrix, right):
        return dot(left, dot(matrix, right).astype(BF16))

    for bond in range(bonds):
        matrix = derivative_ref[bond]
        product = (
            spread(row_high, matrix, column_high) * spread(row_low, matrix, column_low)
        ).astype(BF16)
        if bond < local_bonds:
            local_k_ref[:, bond * square : (bond + 1) * square] = product
        else:
            at = bond - local_bonds
            remote_k_ref[:, at * square : (at + 1) * square] = product
    first = lax.axis_index("atom") * atoms
    for bond in range(local_bonds):
        local_hot_ref[bond * atoms : (bond + 1) * atoms, :] = hot(
            columns_ref[bond : bond + 1, :] - first, atoms
        )
    rows = []
    for bond in range(local_bonds, bonds):
        number = columns_ref[bond : bond + 1, :]
        rows += [number // atoms, number % atoms]
    place = lax.broadcasted_iota(jnp.int32, ids_ref.shape, 0)
    ids = jnp.zeros(ids_ref.shape, jnp.int32)
    for at, row in enumerate(rows):
        ids = jnp.where(place == at, row, ids)
    ids_ref[...] = ids.astype(F32).astype(BF16)


def stage_kernel(green_ref, shift_ref, green_out, shift_out):
    green_out[...] = green_ref[...]
    for mode in range(shift_ref.shape[0]):
        shift_out[mode] = shift_ref[mode]


def pass_kernel(pieces, value_ref, after_ref, *out_refs):
    for index, ((first, end), out_ref) in enumerate(zip(pieces, out_refs)):
        out_ref[: end - first, :] = value_ref[first:end, :]
        if index == 0:
            out_ref[end - first :, :] = value_ref[value_ref.shape[0] - ID_ROWS :, :]


def remote_hot_kernel(bonds, flips, *refs):
    id_refs, out_ref = refs[:-2], refs[-1]
    atoms = id_refs[0].shape[1]
    me = lax.axis_index("atom")
    for place, ids_ref in enumerate(id_refs):
        ids = ids_ref[ids_ref.shape[0] - ID_ROWS :, :].astype(F32).astype(jnp.int32)
        for which, flip in enumerate(flips):
            slab = me ^ flip
            for bond in range(bonds):
                at = (which * bonds + bond) * atoms
                number = (ids[2 * bond : 2 * bond + 1, :] - slab) * atoms + ids[
                    2 * bond + 1 : 2 * bond + 2, :
                ]
                out_ref[at : at + atoms, place * atoms : (place + 1) * atoms] = hot(number, atoms)


def local_kernel(mixed_ref, hot_ref, k_ref, *rest):
    out_ref, sums_ref = rest[-2:]
    rows, square, atoms = out_ref.shape
    bonds = hot_ref.shape[0] // atoms
    group = sums_ref.shape[1] // atoms
    for start in range(0, rows, group):
        count = min(group, rows - start)
        for inner in range(count):
            at = (start + inner) * square
            summed = dot_nt(mixed_ref[at : at + square, :], hot_ref[...]).astype(BF16)
            for bond in range(bonds):
                sums_ref[bond * square : (bond + 1) * square, inner * atoms : (inner + 1) * atoms] = (
                    summed[:, bond * atoms : (bond + 1) * atoms]
                )
        result = dot(k_ref[...], sums_ref[:, : count * atoms])
        for inner in range(count):
            out_ref[start + inner] = result[:, inner * atoms : (inner + 1) * atoms]


def remote_sums(source_refs, offsets, hot_ref, k_ref, rows, first, count, store):
    atoms = source_refs[0].shape[1]
    square = k_ref.shape[0]
    bonds = k_ref.shape[1] // square
    width = bonds * atoms
    group = max(1, 2 // count)
    for start in range(0, rows, group):
        inner = range(start, min(start + group, rows))
        pieces = [[] for _ in range(bonds)]
        for row in inner:
            sources = jnp.concatenate(
                [
                    ref[at + row * square : at + (row + 1) * square, :]
                    for at, ref in zip(offsets, source_refs)
                ],
                axis=1,
            )
            summed = dot_nt(sources, hot_ref[first * width : (first + count) * width, :])
            summed = summed.astype(BF16)
            for which in range(count):
                for bond in range(bonds):
                    at = which * width + bond * atoms
                    pieces[bond].append(summed[:, at : at + atoms])
        stacked = jnp.concatenate([jnp.concatenate(piece, axis=1) for piece in pieces], axis=0)
        result = dot(k_ref[...], stacked)
        for place, row in enumerate(inner):
            for which in range(count):
                at = (place * count + which) * atoms
                store(row, which, result[:, at : at + atoms])


def away_kernel(offsets, *refs):
    source_count = len(offsets)
    source_refs = refs[:source_count]
    hot_ref, k_ref = refs[source_count : source_count + 2]
    count = hot_ref.shape[0] // (k_ref.shape[1] // k_ref.shape[0] * source_refs[0].shape[1]) - 1
    out_refs = refs[len(refs) - count :]
    rows = out_refs[0].shape[0]

    def store(row, which, value):
        out_refs[which][row] = value.astype(BF16)

    remote_sums(source_refs, offsets, hot_ref, k_ref, rows, 1, count, store)


def stay_kernel(offsets, skip, *refs):
    source_count = len(offsets)
    source_refs = refs[:source_count]
    hot_ref, k_ref, local_ref = refs[source_count : source_count + 3]
    out_ref = refs[-1]

    def store(row, which, value):
        out_ref[row] = value + local_ref[skip + row]

    remote_sums(source_refs, offsets, hot_ref, k_ref, out_ref.shape[0], 0, 1, store)


def per_device(green_blocks, derivative, phonon_weight, occupation, mode_shift, neighbours):
    rows, orbital, _, atoms = green_blocks.shape
    square = orbital * orbital
    bonds = derivative.shape[0]
    modes = phonon_weight.shape[0]
    local_bonds = bonds - REMOTE_BONDS
    pairs = lax.axis_size("energy") // 2
    slabs = lax.axis_size("atom")
    high = [4 * i for i in range(1, slabs // 4)]
    last = max(1, rows * P_PART // 8)
    sizes = [rows - last, last]
    firsts = [0, sizes[0]]
    chunks = len(sizes)
    green = green_blocks.reshape(rows, square, atoms)
    columns = neighbours.T

    mate = swap(green, "energy", 1)

    absorption = phonon_weight * occupation[:, None]
    couplings = jnp.concatenate([absorption + phonon_weight, absorption], 0).astype(BF16)
    green_near, shift_near = pl.pallas_call(
        stage_kernel,
        out_shape=(
            jax.ShapeDtypeStruct(green.shape, green.dtype),
            jax.ShapeDtypeStruct(mode_shift.shape, mode_shift.dtype),
        ),
        in_specs=[VMEM, SMEM],
        out_specs=(VMEM, SMEM),
        compiler_params=params(),
        cost_estimate=cost(1e6, 1e6),
    )(green, mode_shift)

    def mix(group, chunk, kind, after):
        return pl.pallas_call(
            functools.partial(mix_kernel, group, firsts[chunk]),
            out_shape=jax.ShapeDtypeStruct((sizes[chunk], square, atoms), kind),
            in_specs=[SMEM, VMEM, VMEM, VMEM] + [ANY] * len(after),
            out_specs=VMEM,
            scratch_shapes=[pltpu.VMEM((sizes[chunk], 2 * rows + 1, SUBLANES, atoms), F32)],
            compiler_params=params(),
            cost_estimate=cost(5e8, 1e6),
        )(shift_near, couplings, green_near, mate, *after)

    def prepare(after):
        return pl.pallas_call(
            prepare_kernel,
            out_shape=(
                jax.ShapeDtypeStruct((square, local_bonds * square), BF16),
                jax.ShapeDtypeStruct((square, REMOTE_BONDS * square), BF16),
                jax.ShapeDtypeStruct((local_bonds * atoms, atoms), BF16),
                jax.ShapeDtypeStruct((ID_ROWS, atoms), BF16),
            ),
            in_specs=[VMEM, VMEM, ANY],
            out_specs=(VMEM,) * 4,
            compiler_params=params(),
            cost_estimate=cost(2e9, 3e6),
        )(derivative, columns, after)

    def local_sum(chunk, after):
        return pl.pallas_call(
            local_kernel,
            out_shape=jax.ShapeDtypeStruct((sizes[chunk], square, atoms), F32),
            in_specs=[VMEM] * 3 + [ANY] * len(after),
            out_specs=VMEM,
            scratch_shapes=[
                pltpu.VMEM((local_bonds * square, min(2, sizes[chunk]) * atoms), BF16)
            ],
            compiler_params=params(),
            cost_estimate=cost(2e9, 3e6),
        )(mixed[chunk], local_hot, local_k, *after)

    own, arrived = [], []
    after = []
    for chunk in range(chunks):
        away = [mix(group, chunk, BF16, after) for group in range(1, pairs)]
        arrived.append([swap(value, "energy", 2 * group) for group, value in enumerate(away, 1)])
        if chunk == 0:
            own.append(mix(0, chunk, F32, away[:1]))
            after = own[-1:]
        else:
            local_k, remote_k, local_hot, ids = prepare(away[0])
    mixed = []
    for chunk in range(chunks):
        if chunk > 0:
            own.append(mix(0, chunk, F32, mixed[-1:] + [local_hot]))
        total = own[chunk]
        for received in arrived[chunk]:
            total = total + received.astype(F32)
        mixed.append(jnp.concatenate([total.astype(BF16).reshape(-1, atoms), ids], 0))

    def ordered(value, pieces, after):
        return pl.pallas_call(
            functools.partial(pass_kernel, pieces),
            out_shape=tuple(
                jax.ShapeDtypeStruct((end - first + (ID_ROWS if first == 0 else 0), atoms), BF16)
                for first, end in pieces
            ),
            in_specs=[VMEM, ANY],
            out_specs=(VMEM,) * len(pieces),
            compiler_params=params(),
            cost_estimate=cost(1e6, 1e6),
        )(value, after)

    def one_hots(sources, flips, after):
        return pl.pallas_call(
            functools.partial(remote_hot_kernel, REMOTE_BONDS, [0] + flips),
            out_shape=jax.ShapeDtypeStruct(
                ((1 + len(flips)) * REMOTE_BONDS * atoms, len(sources) * atoms), BF16
            ),
            in_specs=[VMEM] * len(sources) + [ANY],
            out_specs=VMEM,
            compiler_params=params(),
            cost_estimate=cost(1e8, 1e6),
        )(*sources, after)

    def away_sums(count, sources, offsets, hots, flips, after):
        block = jax.ShapeDtypeStruct((count, square, atoms), BF16)
        return pl.pallas_call(
            functools.partial(away_kernel, offsets),
            out_shape=(block,) * len(flips),
            in_specs=[VMEM] * (len(sources) + 2) + [ANY],
            out_specs=(VMEM,) * len(flips),
            compiler_params=params(),
            cost_estimate=cost(1e9, 3e6),
        )(*sources, hots, remote_k, after)

    def stay_sum(count, skip, sources, offsets, hots, local, after):
        return pl.pallas_call(
            functools.partial(stay_kernel, offsets, skip),
            out_shape=jax.ShapeDtypeStruct((count, square, atoms), F32),
            in_specs=[VMEM] * (len(sources) + 3) + [ANY] * len(after),
            out_specs=VMEM,
            compiler_params=params(),
            cost_estimate=cost(4e9, 3e6),
        )(*sources, hots, remote_k, local, *after)

    def send(values, masks):
        return [swap(value, "atom", mask) for value, mask in zip(values, masks)]

    inner, outer = mixed
    near = [inner] + send([inner] * 3, [2, 1, 3])
    far = [outer] + send([outer] * len(high), high)
    far_beside = send([outer], [1])
    local_inner = local_sum(0, [outer])
    local_outer = local_sum(1, [local_inner])
    straight = [0] * len(near)
    near_hots = one_hots(near, high, local_outer)
    near_away = away_sums(sizes[0], near, straight, near_hots, high, local_outer)
    near_back = send(near_away, high)
    counts = [sizes[1] - sizes[1] // 2, sizes[1] // 2]
    skips = [0, counts[0]]
    pieces = [(skip * square, (skip + count) * square) for skip, count in zip(skips, counts)]
    passed = [ordered(value, pieces, near_away[0]) for value in far[1:]]
    far_next = [[value[index] for value in passed] for index in range(len(pieces))]
    far_next = [send(values, [1] * len(values)) for values in far_next]
    stay_inner = stay_sum(
        sizes[0], 0, near, straight, near_hots, local_inner, passed[0][-1:]
    )
    after = stay_inner
    far_hots = None
    far_away, far_lists = [], []
    for index, (first, _) in enumerate(pieces):
        sources = far + far_beside + far_next[index]
        offsets = [first] * (len(far) + 1) + [0] * len(far_next[index])
        if far_hots is None:
            far_hots = one_hots(sources, [2], after)
        away = away_sums(counts[index], sources, offsets, far_hots, [2], after)
        after = away[0]
        far_away.append(swap(away[0], "atom", 2))
        far_lists.append((sources, offsets))
    results, arrivals = [stay_inner], [near_back]
    for index, (sources, offsets) in enumerate(far_lists):
        after = stay_sum(
            counts[index],
            skips[index],
            sources,
            offsets,
            far_hots,
            local_outer,
            near_back + [after],
        )
        results.append(after)
        arrivals.append([far_away[index]])
    combined = []
    for stay, received in zip(results, arrivals):
        for value in received:
            stay = stay + value.astype(F32)
        combined.append(stay)
    return jnp.concatenate(combined, 0).reshape(rows, orbital, orbital, atoms)


def solution(mesh):
    in_specs = (P("energy", None, None, "atom"), P(), P(None, "atom"), P(), P(), P("atom", None))
    out_specs = P("energy", None, None, "atom")
    return jax.shard_map(
        per_device, mesh=mesh, in_specs=in_specs, out_specs=out_specs, check_vma=False
    )
```

```python
import functools

import jax
import jax.numpy as jnp
from jax import lax
from jax.experimental import pallas as pl
from jax.experimental.pallas import tpu as pltpu
from jax.sharding import PartitionSpec as P

REMOTE_BONDS = 2
ID_ROWS = 16
P_PART = 3
COST = 1.0
SUBLANES = 8
VMEM_LIMIT = 48 * 1024 * 1024

VMEM = pl.BlockSpec(memory_space=pltpu.VMEM)
SMEM = pl.BlockSpec(memory_space=pltpu.SMEM)
ANY = pl.BlockSpec(memory_space=pl.ANY)
F32, BF16 = jnp.float32, jnp.bfloat16


def params():
    return pltpu.CompilerParams(vmem_limit_bytes=VMEM_LIMIT)


def cost(flops, nbytes):
    return pl.CostEstimate(flops=int(flops * COST), bytes_accessed=int(nbytes * COST), transcendentals=0)


def swap(value, axis, mask):
    count = lax.axis_size(axis)
    return lax.ppermute(value, axis, [(i, i ^ mask) for i in range(count)])


def dot(left, right):
    return jnp.dot(left, right, preferred_element_type=F32)


def dot_nt(left, right):
    return lax.dot_general(left, right, (((1,), (1,)), ((), ())), preferred_element_type=F32)


def mix_kernel(group, first, shift_ref, coupling_ref, own_ref, mate_ref, *rest):
    out_ref, table_ref = rest[-2:]
    span, square, atoms = own_ref.shape
    rows = out_ref.shape[0]
    tile = table_ref.shape[2]
    modes = coupling_ref.shape[0] // 2
    me = lax.axis_index("energy")
    base = me // 2 * 2 * span
    move = me % 2 * span
    target = me ^ (2 * group)
    table_ref[...] = jnp.zeros_like(table_ref)
    couplings = coupling_ref[...].astype(F32)

    def put(row, source, value):
        place = source - base
        slot = jnp.where(place < span, place + move, place - move)
        inside = jnp.logical_and(place >= 0, place < 2 * span)
        table_ref[row, jnp.where(inside, slot, 2 * span)] = value

    for mode in range(modes):
        shift = shift_ref[mode]
        emission = jnp.broadcast_to(couplings[mode : mode + 1, :], (tile, atoms))
        absorption = jnp.broadcast_to(couplings[modes + mode : modes + mode + 1, :], (tile, atoms))
        if group > 0:
            above = target > me
            sign = jnp.where(above, -shift, shift)
            coupling = jnp.where(above, emission, absorption)
        for row in range(rows):
            energy = target * span + first + row
            if group == 0:
                put(row, energy - shift, emission)
                put(row, energy + shift, absorption)
            else:
                put(row, energy + sign, coupling)

    step = min(32, square)

    def body(block, carry):
        at = pl.multiple_of(block * step, step)
        totals = [None] * rows
        for slot in range(2 * span):
            ref = own_ref if slot < span else mate_ref
            values = ref[slot % span, pl.ds(at, step), :].astype(F32).reshape(
                step // tile, tile, atoms
            )
            for row in range(rows):
                term = table_ref[row, slot][None] * values
                totals[row] = term if totals[row] is None else totals[row] + term
        for row in range(rows):
            out_ref[row, pl.ds(at, step), :] = totals[row].reshape(step, atoms).astype(out_ref.dtype)
        return carry

    lax.fori_loop(0, square // step, body, 0)


def hot(row, width):
    numbers = lax.broadcasted_iota(jnp.int32, (width, row.shape[1]), 0)
    return jnp.where(row == numbers, 1.0, 0.0).astype(BF16)


def prepare_kernel(derivative_ref, columns_ref, after_ref, local_k_ref, remote_k_ref, local_hot_ref, ids_ref):
    bonds, orbital, _ = derivative_ref.shape
    square = orbital * orbital
    atoms = columns_ref.shape[1]
    local_bonds = bonds - REMOTE_BONDS
    row = lax.broadcasted_iota(jnp.int32, (square, orbital), 0)
    row_of = lax.broadcasted_iota(jnp.int32, (square, orbital), 1)
    column = lax.broadcasted_iota(jnp.int32, (orbital, square), 1)
    column_of = lax.broadcasted_iota(jnp.int32, (orbital, square), 0)

    def pick(condition):
        return jnp.where(condition, 1.0, 0.0).astype(BF16)

    row_high, row_low = pick(row // orbital == row_of), pick(row % orbital == row_of)
    column_high, column_low = pick(column // orbital == column_of), pick(column % orbital == column_of)

    def spread(left, matrix, right):
        return dot(left, dot(matrix, right).astype(BF16))

    for bond in range(bonds):
        matrix = derivative_ref[bond]
        product = (
            spread(row_high, matrix, column_high) * spread(row_low, matrix, column_low)
        ).astype(BF16)
        if bond < local_bonds:
            local_k_ref[:, bond * square : (bond + 1) * square] = product
        else:
            at = bond - local_bonds
            remote_k_ref[:, at * square : (at + 1) * square] = product
    first = lax.axis_index("atom") * atoms
    for bond in range(local_bonds):
        local_hot_ref[bond * atoms : (bond + 1) * atoms, :] = hot(
            columns_ref[bond : bond + 1, :] - first, atoms
        )
    rows = []
    for bond in range(local_bonds, bonds):
        number = columns_ref[bond : bond + 1, :]
        rows += [number // atoms, number % atoms]
    place = lax.broadcasted_iota(jnp.int32, ids_ref.shape, 0)
    ids = jnp.zeros(ids_ref.shape, jnp.int32)
    for at, row in enumerate(rows):
        ids = jnp.where(place == at, row, ids)
    ids_ref[...] = ids.astype(F32).astype(BF16)


def pass_kernel(pieces, value_ref, after_ref, *out_refs):
    for index, ((first, end), out_ref) in enumerate(zip(pieces, out_refs)):
        out_ref[: end - first, :] = value_ref[first:end, :]
        if index == 0:
            out_ref[end - first :, :] = value_ref[value_ref.shape[0] - ID_ROWS :, :]


def remote_hot_kernel(bonds, flips, *refs):
    id_refs, out_ref = refs[:-2], refs[-1]
    atoms = id_refs[0].shape[1]
    me = lax.axis_index("atom")
    for place, ids_ref in enumerate(id_refs):
        ids = ids_ref[ids_ref.shape[0] - ID_ROWS :, :].astype(F32).astype(jnp.int32)
        for which, flip in enumerate(flips):
            slab = me ^ flip
            for bond in range(bonds):
                at = (which * bonds + bond) * atoms
                number = (ids[2 * bond : 2 * bond + 1, :] - slab) * atoms + ids[
                    2 * bond + 1 : 2 * bond + 2, :
                ]
                out_ref[at : at + atoms, place * atoms : (place + 1) * atoms] = hot(number, atoms)


def local_kernel(mixed_ref, hot_ref, k_ref, *rest):
    out_ref, sums_ref = rest[-2:]
    rows, square, atoms = out_ref.shape
    bonds = hot_ref.shape[0] // atoms
    group = sums_ref.shape[1] // atoms
    for start in range(0, rows, group):
        count = min(group, rows - start)
        for inner in range(count):
            at = (start + inner) * square
            summed = dot_nt(mixed_ref[at : at + square, :], hot_ref[...]).astype(BF16)
            for bond in range(bonds):
                sums_ref[bond * square : (bond + 1) * square, inner * atoms : (inner + 1) * atoms] = (
                    summed[:, bond * atoms : (bond + 1) * atoms]
                )
        result = dot(k_ref[...], sums_ref[:, : count * atoms])
        for inner in range(count):
            out_ref[start + inner] = result[:, inner * atoms : (inner + 1) * atoms]


def remote_sums(source_refs, offsets, hot_ref, k_ref, rows, first, count, store):
    atoms = source_refs[0].shape[1]
    square = k_ref.shape[0]
    bonds = k_ref.shape[1] // square
    width = bonds * atoms
    group = max(1, 2 // count)
    for start in range(0, rows, group):
        inner = range(start, min(start + group, rows))
        pieces = [[] for _ in range(bonds)]
        for row in inner:
            sources = jnp.concatenate(
                [
                    ref[at + row * square : at + (row + 1) * square, :]
                    for at, ref in zip(offsets, source_refs)
                ],
                axis=1,
            )
            summed = dot_nt(sources, hot_ref[first * width : (first + count) * width, :])
            summed = summed.astype(BF16)
            for which in range(count):
                for bond in range(bonds):
                    at = which * width + bond * atoms
                    pieces[bond].append(summed[:, at : at + atoms])
        stacked = jnp.concatenate([jnp.concatenate(piece, axis=1) for piece in pieces], axis=0)
        result = dot(k_ref[...], stacked)
        for place, row in enumerate(inner):
            for which in range(count):
                at = (place * count + which) * atoms
                store(row, which, result[:, at : at + atoms])


def away_kernel(offsets, *refs):
    source_count = len(offsets)
    source_refs = refs[:source_count]
    hot_ref, k_ref = refs[source_count : source_count + 2]
    count = hot_ref.shape[0] // (k_ref.shape[1] // k_ref.shape[0] * source_refs[0].shape[1]) - 1
    out_refs = refs[len(refs) - count :]
    rows = out_refs[0].shape[0]

    def store(row, which, value):
        out_refs[which][row] = value.astype(BF16)

    remote_sums(source_refs, offsets, hot_ref, k_ref, rows, 1, count, store)


def stay_kernel(offsets, skip, *refs):
    source_count = len(offsets)
    source_refs = refs[:source_count]
    hot_ref, k_ref, local_ref = refs[source_count : source_count + 3]
    out_ref = refs[-1]

    def store(row, which, value):
        out_ref[row] = value + local_ref[skip + row]

    remote_sums(source_refs, offsets, hot_ref, k_ref, out_ref.shape[0], 0, 1, store)


def per_device(green_blocks, derivative, phonon_weight, occupation, mode_shift, neighbours):
    rows, orbital, _, atoms = green_blocks.shape
    square = orbital * orbital
    bonds = derivative.shape[0]
    modes = phonon_weight.shape[0]
    local_bonds = bonds - REMOTE_BONDS
    pairs = lax.axis_size("energy") // 2
    slabs = lax.axis_size("atom")
    high = [4 * i for i in range(1, slabs // 4)]
    last = max(1, rows * P_PART // 8)
    sizes = [rows - last, last]
    firsts = [0, sizes[0]]
    chunks = len(sizes)
    green = green_blocks.reshape(rows, square, atoms)
    columns = neighbours.T

    mate = swap(green, "energy", 1)

    absorption = phonon_weight * occupation[:, None]
    couplings = jnp.concatenate([absorption + phonon_weight, absorption], 0).astype(BF16)

    def mix(group, chunk, kind, after):
        return pl.pallas_call(
            functools.partial(mix_kernel, group, firsts[chunk]),
            out_shape=jax.ShapeDtypeStruct((sizes[chunk], square, atoms), kind),
            in_specs=[SMEM, VMEM, VMEM, VMEM] + [ANY] * len(after),
            out_specs=VMEM,
            scratch_shapes=[pltpu.VMEM((sizes[chunk], 2 * rows + 1, SUBLANES, atoms), F32)],
            compiler_params=params(),
            cost_estimate=cost(5e8, 1e6),
        )(mode_shift, couplings, green, mate, *after)

    def prepare(after):
        return pl.pallas_call(
            prepare_kernel,
            out_shape=(
                jax.ShapeDtypeStruct((square, local_bonds * square), BF16),
                jax.ShapeDtypeStruct((square, REMOTE_BONDS * square), BF16),
                jax.ShapeDtypeStruct((local_bonds * atoms, atoms), BF16),
                jax.ShapeDtypeStruct((ID_ROWS, atoms), BF16),
            ),
            in_specs=[VMEM, VMEM, ANY],
            out_specs=(VMEM,) * 4,
            compiler_params=params(),
            cost_estimate=cost(2e9, 3e6),
        )(derivative, columns, after)

    def local_sum(chunk, after):
        return pl.pallas_call(
            local_kernel,
            out_shape=jax.ShapeDtypeStruct((sizes[chunk], square, atoms), F32),
            in_specs=[VMEM] * 3 + [ANY] * len(after),
            out_specs=VMEM,
            scratch_shapes=[
                pltpu.VMEM((local_bonds * square, min(2, sizes[chunk]) * atoms), BF16)
            ],
            compiler_params=params(),
            cost_estimate=cost(2e9, 3e6),
        )(mixed[chunk], local_hot, local_k, *after)

    own, arrived = [], []
    after = []
    for chunk in range(chunks):
        away = [mix(group, chunk, BF16, after) for group in range(1, pairs)]
        arrived.append([swap(value, "energy", 2 * group) for group, value in enumerate(away, 1)])
        if chunk == 0:
            own.append(mix(0, chunk, F32, away[:1]))
            after = own[-1:]
        else:
            local_k, remote_k, local_hot, ids = prepare(away[0])
    mixed = []
    for chunk in range(chunks):
        if chunk > 0:
            own.append(mix(0, chunk, F32, mixed[-1:] + [local_hot]))
        total = own[chunk]
        for received in arrived[chunk]:
            total = total + received.astype(F32)
        mixed.append(jnp.concatenate([total.astype(BF16).reshape(-1, atoms), ids], 0))

    def ordered(value, pieces, after):
        return pl.pallas_call(
            functools.partial(pass_kernel, pieces),
            out_shape=tuple(
                jax.ShapeDtypeStruct((end - first + (ID_ROWS if first == 0 else 0), atoms), BF16)
                for first, end in pieces
            ),
            in_specs=[VMEM, ANY],
            out_specs=(VMEM,) * len(pieces),
            compiler_params=params(),
            cost_estimate=cost(1e6, 1e6),
        )(value, after)

    def one_hots(sources, flips, after):
        return pl.pallas_call(
            functools.partial(remote_hot_kernel, REMOTE_BONDS, [0] + flips),
            out_shape=jax.ShapeDtypeStruct(
                ((1 + len(flips)) * REMOTE_BONDS * atoms, len(sources) * atoms), BF16
            ),
            in_specs=[VMEM] * len(sources) + [ANY],
            out_specs=VMEM,
            compiler_params=params(),
            cost_estimate=cost(1e8, 1e6),
        )(*sources, after)

    def away_sums(count, sources, offsets, hots, flips, after):
        block = jax.ShapeDtypeStruct((count, square, atoms), BF16)
        return pl.pallas_call(
            functools.partial(away_kernel, offsets),
            out_shape=(block,) * len(flips),
            in_specs=[VMEM] * (len(sources) + 2) + [ANY],
            out_specs=(VMEM,) * len(flips),
            compiler_params=params(),
            cost_estimate=cost(1e9, 3e6),
        )(*sources, hots, remote_k, after)

    def stay_sum(count, skip, sources, offsets, hots, local, after):
        return pl.pallas_call(
            functools.partial(stay_kernel, offsets, skip),
            out_shape=jax.ShapeDtypeStruct((count, square, atoms), F32),
            in_specs=[VMEM] * (len(sources) + 3) + [ANY] * len(after),
            out_specs=VMEM,
            compiler_params=params(),
            cost_estimate=cost(4e9, 3e6),
        )(*sources, hots, remote_k, local, *after)

    def send(values, masks):
        return [swap(value, "atom", mask) for value, mask in zip(values, masks)]

    inner, outer = mixed
    near = [inner] + send([inner] * 3, [2, 1, 3])
    far = [outer] + send([outer] * len(high), high)
    far_beside = send([outer], [1])
    local_inner = local_sum(0, [outer])
    local_outer = local_sum(1, [local_inner])
    straight = [0] * len(near)
    near_hots = one_hots(near, high, local_outer)
    near_away = away_sums(sizes[0], near, straight, near_hots, high, local_outer)
    near_back = send(near_away, high)
    counts, skips = [sizes[1]], [0]
    pieces = [(skip * square, (skip + count) * square) for skip, count in zip(skips, counts)]
    passed = [ordered(value, pieces, near_away[0]) for value in far[1:]]
    far_next = [[value[index] for value in passed] for index in range(len(pieces))]
    far_next = [send(values, [1] * len(values)) for values in far_next]
    stay_inner = stay_sum(
        sizes[0], 0, near, straight, near_hots, local_inner, passed[0][-1:]
    )
    after = stay_inner
    far_hots = None
    far_away, far_lists = [], []
    for index, (first, _) in enumerate(pieces):
        sources = far + far_beside + far_next[index]
        offsets = [first] * (len(far) + 1) + [0] * len(far_next[index])
        if far_hots is None:
            far_hots = one_hots(sources, [2], after)
        away = away_sums(counts[index], sources, offsets, far_hots, [2], after)
        after = away[0]
        far_away.append(swap(away[0], "atom", 2))
        far_lists.append((sources, offsets))
    results, arrivals = [stay_inner], [near_back]
    for index, (sources, offsets) in enumerate(far_lists):
        after = stay_sum(
            counts[index],
            skips[index],
            sources,
            offsets,
            far_hots,
            local_outer,
            [after],
        )
        results.append(after)
        arrivals.append([far_away[index]])
    combined = []
    for stay, received in zip(results, arrivals):
        for value in received:
            stay = stay + value.astype(F32)
        combined.append(stay)
    return jnp.concatenate(combined, 0).reshape(rows, orbital, orbital, atoms)


def solution(mesh):
    in_specs = (P("energy", None, None, "atom"), P(), P(None, "atom"), P(), P(), P("atom", None))
    out_specs = P("energy", None, None, "atom")
    return jax.shard_map(
        per_device, mesh=mesh, in_specs=in_specs, out_specs=out_specs, check_vma=False
    )
```

```python
import functools

import jax
import jax.numpy as jnp
from jax import lax
from jax.experimental import pallas as pl
from jax.experimental.pallas import tpu as pltpu
from jax.sharding import PartitionSpec as P

REMOTE_BONDS = 2
ID_ROWS = 16
P_PART = 4
COST = 1.0
SUBLANES = 8
VMEM_LIMIT = 48 * 1024 * 1024

VMEM = pl.BlockSpec(memory_space=pltpu.VMEM)
SMEM = pl.BlockSpec(memory_space=pltpu.SMEM)
ANY = pl.BlockSpec(memory_space=pl.ANY)
F32, BF16 = jnp.float32, jnp.bfloat16


def params():
    return pltpu.CompilerParams(vmem_limit_bytes=VMEM_LIMIT)


def cost(flops, nbytes):
    return pl.CostEstimate(flops=int(flops * COST), bytes_accessed=int(nbytes * COST), transcendentals=0)


def swap(value, axis, mask):
    count = lax.axis_size(axis)
    return lax.ppermute(value, axis, [(i, i ^ mask) for i in range(count)])


def dot(left, right):
    return jnp.dot(left, right, preferred_element_type=F32)


def dot_nt(left, right):
    return lax.dot_general(left, right, (((1,), (1,)), ((), ())), preferred_element_type=F32)


def mix_kernel(group, first, shift_ref, coupling_ref, own_ref, mate_ref, *rest):
    out_ref, table_ref = rest[-2:]
    span, square, atoms = own_ref.shape
    rows = out_ref.shape[0]
    tile = table_ref.shape[2]
    modes = coupling_ref.shape[0] // 2
    me = lax.axis_index("energy")
    base = me // 2 * 2 * span
    move = me % 2 * span
    target = me ^ (2 * group)
    table_ref[...] = jnp.zeros_like(table_ref)
    couplings = coupling_ref[...].astype(F32)

    def put(row, source, value):
        place = source - base
        slot = jnp.where(place < span, place + move, place - move)
        inside = jnp.logical_and(place >= 0, place < 2 * span)
        table_ref[row, jnp.where(inside, slot, 2 * span)] = value

    for mode in range(modes):
        shift = shift_ref[mode]
        emission = jnp.broadcast_to(couplings[mode : mode + 1, :], (tile, atoms))
        absorption = jnp.broadcast_to(couplings[modes + mode : modes + mode + 1, :], (tile, atoms))
        if group > 0:
            above = target > me
            sign = jnp.where(above, -shift, shift)
            coupling = jnp.where(above, emission, absorption)
        for row in range(rows):
            energy = target * span + first + row
            if group == 0:
                put(row, energy - shift, emission)
                put(row, energy + shift, absorption)
            else:
                put(row, energy + sign, coupling)

    step = min(32, square)

    def body(block, carry):
        at = pl.multiple_of(block * step, step)
        totals = [None] * rows
        for slot in range(2 * span):
            ref = own_ref if slot < span else mate_ref
            values = ref[slot % span, pl.ds(at, step), :].astype(F32).reshape(
                step // tile, tile, atoms
            )
            for row in range(rows):
                term = table_ref[row, slot][None] * values
                totals[row] = term if totals[row] is None else totals[row] + term
        for row in range(rows):
            out_ref[row, pl.ds(at, step), :] = totals[row].reshape(step, atoms).astype(out_ref.dtype)
        return carry

    lax.fori_loop(0, square // step, body, 0)


def hot(row, width):
    numbers = lax.broadcasted_iota(jnp.int32, (width, row.shape[1]), 0)
    return jnp.where(row == numbers, 1.0, 0.0).astype(BF16)


def prepare_kernel(derivative_ref, columns_ref, after_ref, local_k_ref, remote_k_ref, local_hot_ref, ids_ref):
    bonds, orbital, _ = derivative_ref.shape
    square = orbital * orbital
    atoms = columns_ref.shape[1]
    local_bonds = bonds - REMOTE_BONDS
    row = lax.broadcasted_iota(jnp.int32, (square, orbital), 0)
    row_of = lax.broadcasted_iota(jnp.int32, (square, orbital), 1)
    column = lax.broadcasted_iota(jnp.int32, (orbital, square), 1)
    column_of = lax.broadcasted_iota(jnp.int32, (orbital, square), 0)

    def pick(condition):
        return jnp.where(condition, 1.0, 0.0).astype(BF16)

    row_high, row_low = pick(row // orbital == row_of), pick(row % orbital == row_of)
    column_high, column_low = pick(column // orbital == column_of), pick(column % orbital == column_of)

    def spread(left, matrix, right):
        return dot(left, dot(matrix, right).astype(BF16))

    for bond in range(bonds):
        matrix = derivative_ref[bond]
        product = (
            spread(row_high, matrix, column_high) * spread(row_low, matrix, column_low)
        ).astype(BF16)
        if bond < local_bonds:
            local_k_ref[:, bond * square : (bond + 1) * square] = product
        else:
            at = bond - local_bonds
            remote_k_ref[:, at * square : (at + 1) * square] = product
    first = lax.axis_index("atom") * atoms
    for bond in range(local_bonds):
        local_hot_ref[bond * atoms : (bond + 1) * atoms, :] = hot(
            columns_ref[bond : bond + 1, :] - first, atoms
        )
    rows = []
    for bond in range(local_bonds, bonds):
        number = columns_ref[bond : bond + 1, :]
        rows += [number // atoms, number % atoms]
    place = lax.broadcasted_iota(jnp.int32, ids_ref.shape, 0)
    ids = jnp.zeros(ids_ref.shape, jnp.int32)
    for at, row in enumerate(rows):
        ids = jnp.where(place == at, row, ids)
    ids_ref[...] = ids.astype(F32).astype(BF16)


def pass_kernel(pieces, value_ref, after_ref, *out_refs):
    for index, ((first, end), out_ref) in enumerate(zip(pieces, out_refs)):
        out_ref[: end - first, :] = value_ref[first:end, :]
        if index == 0:
            out_ref[end - first :, :] = value_ref[value_ref.shape[0] - ID_ROWS :, :]


def remote_hot_kernel(bonds, flips, *refs):
    id_refs, out_ref = refs[:-2], refs[-1]
    atoms = id_refs[0].shape[1]
    me = lax.axis_index("atom")
    for place, ids_ref in enumerate(id_refs):
        ids = ids_ref[ids_ref.shape[0] - ID_ROWS :, :].astype(F32).astype(jnp.int32)
        for which, flip in enumerate(flips):
            slab = me ^ flip
            for bond in range(bonds):
                at = (which * bonds + bond) * atoms
                number = (ids[2 * bond : 2 * bond + 1, :] - slab) * atoms + ids[
                    2 * bond + 1 : 2 * bond + 2, :
                ]
                out_ref[at : at + atoms, place * atoms : (place + 1) * atoms] = hot(number, atoms)


def local_kernel(mixed_ref, hot_ref, k_ref, *rest):
    out_ref, sums_ref = rest[-2:]
    rows, square, atoms = out_ref.shape
    bonds = hot_ref.shape[0] // atoms
    group = sums_ref.shape[1] // atoms
    for start in range(0, rows, group):
        count = min(group, rows - start)
        for inner in range(count):
            at = (start + inner) * square
            summed = dot_nt(mixed_ref[at : at + square, :], hot_ref[...]).astype(BF16)
            for bond in range(bonds):
                sums_ref[bond * square : (bond + 1) * square, inner * atoms : (inner + 1) * atoms] = (
                    summed[:, bond * atoms : (bond + 1) * atoms]
                )
        result = dot(k_ref[...], sums_ref[:, : count * atoms])
        for inner in range(count):
            out_ref[start + inner] = result[:, inner * atoms : (inner + 1) * atoms]


def remote_sums(source_refs, offsets, hot_ref, k_ref, rows, first, count, store):
    atoms = source_refs[0].shape[1]
    square = k_ref.shape[0]
    bonds = k_ref.shape[1] // square
    width = bonds * atoms
    group = max(1, 2 // count)
    for start in range(0, rows, group):
        inner = range(start, min(start + group, rows))
        pieces = [[] for _ in range(bonds)]
        for row in inner:
            sources = jnp.concatenate(
                [
                    ref[at + row * square : at + (row + 1) * square, :]
                    for at, ref in zip(offsets, source_refs)
                ],
                axis=1,
            )
            summed = dot_nt(sources, hot_ref[first * width : (first + count) * width, :])
            summed = summed.astype(BF16)
            for which in range(count):
                for bond in range(bonds):
                    at = which * width + bond * atoms
                    pieces[bond].append(summed[:, at : at + atoms])
        stacked = jnp.concatenate([jnp.concatenate(piece, axis=1) for piece in pieces], axis=0)
        result = dot(k_ref[...], stacked)
        for place, row in enumerate(inner):
            for which in range(count):
                at = (place * count + which) * atoms
                store(row, which, result[:, at : at + atoms])


def away_kernel(offsets, *refs):
    source_count = len(offsets)
    source_refs = refs[:source_count]
    hot_ref, k_ref = refs[source_count : source_count + 2]
    count = hot_ref.shape[0] // (k_ref.shape[1] // k_ref.shape[0] * source_refs[0].shape[1]) - 1
    out_refs = refs[len(refs) - count :]
    rows = out_refs[0].shape[0]

    def store(row, which, value):
        out_refs[which][row] = value.astype(BF16)

    remote_sums(source_refs, offsets, hot_ref, k_ref, rows, 1, count, store)


def stay_kernel(offsets, skip, *refs):
    source_count = len(offsets)
    source_refs = refs[:source_count]
    hot_ref, k_ref, local_ref = refs[source_count : source_count + 3]
    out_ref = refs[-1]

    def store(row, which, value):
        out_ref[row] = value + local_ref[skip + row]

    remote_sums(source_refs, offsets, hot_ref, k_ref, out_ref.shape[0], 0, 1, store)


def per_device(green_blocks, derivative, phonon_weight, occupation, mode_shift, neighbours):
    rows, orbital, _, atoms = green_blocks.shape
    square = orbital * orbital
    bonds = derivative.shape[0]
    modes = phonon_weight.shape[0]
    local_bonds = bonds - REMOTE_BONDS
    pairs = lax.axis_size("energy") // 2
    slabs = lax.axis_size("atom")
    high = [4 * i for i in range(1, slabs // 4)]
    last = max(1, rows * P_PART // 8)
    sizes = [rows - last, last]
    firsts = [0, sizes[0]]
    chunks = len(sizes)
    green = green_blocks.reshape(rows, square, atoms)
    columns = neighbours.T

    mate = swap(green, "energy", 1)

    absorption = phonon_weight * occupation[:, None]
    couplings = jnp.concatenate([absorption + phonon_weight, absorption], 0).astype(BF16)

    def mix(group, chunk, kind, after):
        return pl.pallas_call(
            functools.partial(mix_kernel, group, firsts[chunk]),
            out_shape=jax.ShapeDtypeStruct((sizes[chunk], square, atoms), kind),
            in_specs=[SMEM, VMEM, VMEM, VMEM] + [ANY] * len(after),
            out_specs=VMEM,
            scratch_shapes=[pltpu.VMEM((sizes[chunk], 2 * rows + 1, SUBLANES, atoms), F32)],
            compiler_params=params(),
            cost_estimate=cost(5e8, 1e6),
        )(mode_shift, couplings, green, mate, *after)

    def prepare(after):
        return pl.pallas_call(
            prepare_kernel,
            out_shape=(
                jax.ShapeDtypeStruct((square, local_bonds * square), BF16),
                jax.ShapeDtypeStruct((square, REMOTE_BONDS * square), BF16),
                jax.ShapeDtypeStruct((local_bonds * atoms, atoms), BF16),
                jax.ShapeDtypeStruct((ID_ROWS, atoms), BF16),
            ),
            in_specs=[VMEM, VMEM, ANY],
            out_specs=(VMEM,) * 4,
            compiler_params=params(),
            cost_estimate=cost(2e9, 3e6),
        )(derivative, columns, after)

    def local_sum(chunk, after):
        return pl.pallas_call(
            local_kernel,
            out_shape=jax.ShapeDtypeStruct((sizes[chunk], square, atoms), F32),
            in_specs=[VMEM] * 3 + [ANY] * len(after),
            out_specs=VMEM,
            scratch_shapes=[
                pltpu.VMEM((local_bonds * square, min(2, sizes[chunk]) * atoms), BF16)
            ],
            compiler_params=params(),
            cost_estimate=cost(2e9, 3e6),
        )(mixed[chunk], local_hot, local_k, *after)

    own, arrived = [], []
    after = []
    for chunk in range(chunks):
        away = [mix(group, chunk, BF16, after) for group in range(1, pairs)]
        arrived.append([swap(value, "energy", 2 * group) for group, value in enumerate(away, 1)])
        if chunk == 0:
            own.append(mix(0, chunk, F32, away[:1]))
            after = own[-1:]
        else:
            local_k, remote_k, local_hot, ids = prepare(away[0])
    mixed = []
    for chunk in range(chunks):
        if chunk > 0:
            own.append(mix(0, chunk, F32, mixed[-1:] + [local_hot]))
        total = own[chunk]
        for received in arrived[chunk]:
            total = total + received.astype(F32)
        mixed.append(jnp.concatenate([total.astype(BF16).reshape(-1, atoms), ids], 0))

    def ordered(value, pieces, after):
        return pl.pallas_call(
            functools.partial(pass_kernel, pieces),
            out_shape=tuple(
                jax.ShapeDtypeStruct((end - first + (ID_ROWS if first == 0 else 0), atoms), BF16)
                for first, end in pieces
            ),
            in_specs=[VMEM, ANY],
            out_specs=(VMEM,) * len(pieces),
            compiler_params=params(),
            cost_estimate=cost(1e6, 1e6),
        )(value, after)

    def one_hots(sources, flips, after):
        return pl.pallas_call(
            functools.partial(remote_hot_kernel, REMOTE_BONDS, [0] + flips),
            out_shape=jax.ShapeDtypeStruct(
                ((1 + len(flips)) * REMOTE_BONDS * atoms, len(sources) * atoms), BF16
            ),
            in_specs=[VMEM] * len(sources) + [ANY],
            out_specs=VMEM,
            compiler_params=params(),
            cost_estimate=cost(1e8, 1e6),
        )(*sources, after)

    def away_sums(count, sources, offsets, hots, flips, after):
        block = jax.ShapeDtypeStruct((count, square, atoms), BF16)
        return pl.pallas_call(
            functools.partial(away_kernel, offsets),
            out_shape=(block,) * len(flips),
            in_specs=[VMEM] * (len(sources) + 2) + [ANY],
            out_specs=(VMEM,) * len(flips),
            compiler_params=params(),
            cost_estimate=cost(1e9, 3e6),
        )(*sources, hots, remote_k, after)

    def stay_sum(count, skip, sources, offsets, hots, local, after):
        return pl.pallas_call(
            functools.partial(stay_kernel, offsets, skip),
            out_shape=jax.ShapeDtypeStruct((count, square, atoms), F32),
            in_specs=[VMEM] * (len(sources) + 3) + [ANY] * len(after),
            out_specs=VMEM,
            compiler_params=params(),
            cost_estimate=cost(4e9, 3e6),
        )(*sources, hots, remote_k, local, *after)

    def send(values, masks):
        return [swap(value, "atom", mask) for value, mask in zip(values, masks)]

    inner, outer = mixed
    across, beside = send([inner] * 2, [2, 1])
    far = [outer] + send([outer] * len(high), high)
    [turned] = ordered(across, [(0, sizes[0] * square)], outer)
    near = [inner, across, beside] + send([turned], [1])
    local_inner = local_sum(0, [outer])
    local_outer = local_sum(1, [local_inner])
    far_beside = send(ordered(outer, [(0, sizes[1] * square)], local_inner), [1])
    straight = [0] * len(near)
    counts = [sizes[1] - sizes[1] // 2, sizes[1] // 2]
    skips = [0, counts[0]]
    pieces = [(skip * square, (skip + count) * square) for skip, count in zip(skips, counts)]

    def pass_far(after):
        passed = [ordered(value, pieces, after) for value in far[1:]]
        steps = [[value[index] for value in passed] for index in range(len(pieces))]
        return passed[0][-1], [send(values, [1] * len(values)) for values in steps]

    behind = local_outer
    near_hots = one_hots(near, high, behind)
    near_away = away_sums(sizes[0], near, straight, near_hots, high, behind)
    near_back = send(near_away, high)
    behind, far_next = pass_far(near_away[0])
    stay_inner = stay_sum(sizes[0], 0, near, straight, near_hots, local_inner, [behind])
    after = stay_inner
    far_hots = None
    far_away, far_lists = [], []
    for index, (first, _) in enumerate(pieces):
        sources = far + far_beside + far_next[index]
        offsets = [first] * len(far) + [first] + [0] * len(far_next[index])
        if far_hots is None:
            far_hots = one_hots(sources, [2], after)
        away = away_sums(counts[index], sources, offsets, far_hots, [2], after)
        after = away[0]
        far_away.append(swap(away[0], "atom", 2))
        far_lists.append((sources, offsets))
    results, arrivals = [stay_inner], [near_back]
    for index, (sources, offsets) in enumerate(far_lists):
        after = stay_sum(
            counts[index], skips[index], sources, offsets, far_hots, local_outer,
            [after],
        )
        results.append(after)
        arrivals.append([far_away[index]])
    combined = []
    for stay, received in zip(results, arrivals):
        for value in received:
            stay = stay + value.astype(F32)
        combined.append(stay)
    return jnp.concatenate(combined, 0).reshape(rows, orbital, orbital, atoms)


def solution(mesh):
    in_specs = (P("energy", None, None, "atom"), P(), P(None, "atom"), P(), P(), P("atom", None))
    out_specs = P("energy", None, None, "atom")
    return jax.shard_map(
        per_device, mesh=mesh, in_specs=in_specs, out_specs=out_specs, check_vma=False
    )
```

```python
import functools

import jax
import jax.numpy as jnp
from jax import lax
from jax.experimental import pallas as pl
from jax.experimental.pallas import tpu as pltpu
from jax.sharding import PartitionSpec as P

REMOTE_BONDS = 2
ID_ROWS = 16
P_PART = 4
COST = 1.0
SUBLANES = 8
VMEM_LIMIT = 48 * 1024 * 1024

VMEM = pl.BlockSpec(memory_space=pltpu.VMEM)
ANY = pl.BlockSpec(memory_space=pl.ANY)
F32, BF16 = jnp.float32, jnp.bfloat16


def params():
    return pltpu.CompilerParams(vmem_limit_bytes=VMEM_LIMIT)


def cost(flops, nbytes):
    return pl.CostEstimate(flops=int(flops * COST), bytes_accessed=int(nbytes * COST), transcendentals=0)


def swap(value, axis, mask):
    count = lax.axis_size(axis)
    return lax.ppermute(value, axis, [(i, i ^ mask) for i in range(count)])


def dot(left, right):
    return jnp.dot(left, right, preferred_element_type=F32)


def dot_nt(left, right):
    return lax.dot_general(left, right, (((1,), (1,)), ((), ())), preferred_element_type=F32)


def mix_kernel(group, first, shift_rows_ref, coupling_ref, own_ref, mate_ref, *rest):
    out_ref, table_ref, shift_ref, sem = rest[-4:]
    copy = pltpu.make_async_copy(shift_rows_ref, shift_ref, sem)
    copy.start()
    span, square, atoms = own_ref.shape
    rows = out_ref.shape[0]
    tile = table_ref.shape[2]
    modes = coupling_ref.shape[0] // 2
    me = lax.axis_index("energy")
    base = me // 2 * 2 * span
    move = me % 2 * span
    target = me ^ (2 * group)
    table_ref[...] = jnp.zeros_like(table_ref)
    couplings = coupling_ref[...].astype(F32)
    copy.wait()

    def put(row, source, value):
        place = source - base
        slot = jnp.where(place < span, place + move, place - move)
        inside = jnp.logical_and(place >= 0, place < 2 * span)
        table_ref[row, jnp.where(inside, slot, 2 * span)] = value

    for mode in range(modes):
        shift = shift_ref[mode, 0]
        emission = jnp.broadcast_to(couplings[mode : mode + 1, :], (tile, atoms))
        absorption = jnp.broadcast_to(couplings[modes + mode : modes + mode + 1, :], (tile, atoms))
        if group > 0:
            above = target > me
            sign = jnp.where(above, -shift, shift)
            coupling = jnp.where(above, emission, absorption)
        for row in range(rows):
            energy = target * span + first + row
            if group == 0:
                put(row, energy - shift, emission)
                put(row, energy + shift, absorption)
            else:
                put(row, energy + sign, coupling)

    step = min(32, square)

    def body(block, carry):
        at = pl.multiple_of(block * step, step)
        totals = [None] * rows
        for slot in range(2 * span):
            ref = own_ref if slot < span else mate_ref
            values = ref[slot % span, pl.ds(at, step), :].astype(F32).reshape(
                step // tile, tile, atoms
            )
            for row in range(rows):
                term = table_ref[row, slot][None] * values
                totals[row] = term if totals[row] is None else totals[row] + term
        for row in range(rows):
            out_ref[row, pl.ds(at, step), :] = totals[row].reshape(step, atoms).astype(out_ref.dtype)
        return carry

    lax.fori_loop(0, square // step, body, 0)


def hot(row, width):
    numbers = lax.broadcasted_iota(jnp.int32, (width, row.shape[1]), 0)
    return jnp.where(row == numbers, 1.0, 0.0).astype(BF16)


def prepare_kernel(derivative_ref, columns_ref, after_ref, local_k_ref, remote_k_ref, local_hot_ref, ids_ref):
    bonds, orbital, _ = derivative_ref.shape
    square = orbital * orbital
    atoms = columns_ref.shape[1]
    local_bonds = bonds - REMOTE_BONDS
    row = lax.broadcasted_iota(jnp.int32, (square, orbital), 0)
    row_of = lax.broadcasted_iota(jnp.int32, (square, orbital), 1)
    column = lax.broadcasted_iota(jnp.int32, (orbital, square), 1)
    column_of = lax.broadcasted_iota(jnp.int32, (orbital, square), 0)

    def pick(condition):
        return jnp.where(condition, 1.0, 0.0).astype(BF16)

    row_high, row_low = pick(row // orbital == row_of), pick(row % orbital == row_of)
    column_high, column_low = pick(column // orbital == column_of), pick(column % orbital == column_of)

    def spread(left, matrix, right):
        return dot(left, dot(matrix, right).astype(BF16))

    for bond in range(bonds):
        matrix = derivative_ref[bond]
        product = (
            spread(row_high, matrix, column_high) * spread(row_low, matrix, column_low)
        ).astype(BF16)
        if bond < local_bonds:
            local_k_ref[:, bond * square : (bond + 1) * square] = product
        else:
            at = bond - local_bonds
            remote_k_ref[:, at * square : (at + 1) * square] = product
    first = lax.axis_index("atom") * atoms
    for bond in range(local_bonds):
        local_hot_ref[bond * atoms : (bond + 1) * atoms, :] = hot(
            columns_ref[bond : bond + 1, :] - first, atoms
        )
    rows = []
    for bond in range(local_bonds, bonds):
        number = columns_ref[bond : bond + 1, :]
        rows += [number // atoms, number % atoms]
    place = lax.broadcasted_iota(jnp.int32, ids_ref.shape, 0)
    ids = jnp.zeros(ids_ref.shape, jnp.int32)
    for at, row in enumerate(rows):
        ids = jnp.where(place == at, row, ids)
    ids_ref[...] = ids.astype(F32).astype(BF16)


def copy_kernel(value_ref, *rest):
    rest[-1][...] = value_ref[...]


def pass_kernel(pieces, value_ref, after_ref, *out_refs):
    for index, ((first, end), out_ref) in enumerate(zip(pieces, out_refs)):
        out_ref[: end - first, :] = value_ref[first:end, :]
        if index == 0:
            out_ref[end - first :, :] = value_ref[value_ref.shape[0] - ID_ROWS :, :]


def remote_hot_kernel(bonds, flips, *refs):
    id_refs, out_ref = refs[:-2], refs[-1]
    atoms = id_refs[0].shape[1]
    me = lax.axis_index("atom")
    for place, ids_ref in enumerate(id_refs):
        ids = ids_ref[ids_ref.shape[0] - ID_ROWS :, :].astype(F32).astype(jnp.int32)
        for which, flip in enumerate(flips):
            slab = me ^ flip
            for bond in range(bonds):
                at = (which * bonds + bond) * atoms
                number = (ids[2 * bond : 2 * bond + 1, :] - slab) * atoms + ids[
                    2 * bond + 1 : 2 * bond + 2, :
                ]
                out_ref[at : at + atoms, place * atoms : (place + 1) * atoms] = hot(number, atoms)


def local_kernel(mixed_ref, hot_ref, k_ref, *rest):
    out_ref, sums_ref = rest[-2:]
    rows, square, atoms = out_ref.shape
    bonds = hot_ref.shape[0] // atoms
    group = sums_ref.shape[1] // atoms
    for start in range(0, rows, group):
        count = min(group, rows - start)
        for inner in range(count):
            at = (start + inner) * square
            summed = dot_nt(mixed_ref[at : at + square, :], hot_ref[...]).astype(BF16)
            for bond in range(bonds):
                sums_ref[bond * square : (bond + 1) * square, inner * atoms : (inner + 1) * atoms] = (
                    summed[:, bond * atoms : (bond + 1) * atoms]
                )
        result = dot(k_ref[...], sums_ref[:, : count * atoms])
        for inner in range(count):
            out_ref[start + inner] = result[:, inner * atoms : (inner + 1) * atoms]


def remote_sums(source_refs, offsets, hot_ref, k_ref, rows, first, count, store):
    atoms = source_refs[0].shape[1]
    square = k_ref.shape[0]
    bonds = k_ref.shape[1] // square
    width = bonds * atoms
    group = max(1, 2 // count)
    for start in range(0, rows, group):
        inner = range(start, min(start + group, rows))
        pieces = [[] for _ in range(bonds)]
        for row in inner:
            sources = jnp.concatenate(
                [
                    ref[at + row * square : at + (row + 1) * square, :]
                    for at, ref in zip(offsets, source_refs)
                ],
                axis=1,
            )
            summed = dot_nt(sources, hot_ref[first * width : (first + count) * width, :])
            summed = summed.astype(BF16)
            for which in range(count):
                for bond in range(bonds):
                    at = which * width + bond * atoms
                    pieces[bond].append(summed[:, at : at + atoms])
        stacked = jnp.concatenate([jnp.concatenate(piece, axis=1) for piece in pieces], axis=0)
        result = dot(k_ref[...], stacked)
        for place, row in enumerate(inner):
            for which in range(count):
                at = (place * count + which) * atoms
                store(row, which, result[:, at : at + atoms])


def away_kernel(offsets, *refs):
    source_count = len(offsets)
    source_refs = refs[:source_count]
    hot_ref, k_ref = refs[source_count : source_count + 2]
    count = hot_ref.shape[0] // (k_ref.shape[1] // k_ref.shape[0] * source_refs[0].shape[1]) - 1
    out_refs = refs[len(refs) - count :]
    rows = out_refs[0].shape[0]

    def store(row, which, value):
        out_refs[which][row] = value.astype(BF16)

    remote_sums(source_refs, offsets, hot_ref, k_ref, rows, 1, count, store)


def stay_kernel(offsets, skip, *refs):
    source_count = len(offsets)
    source_refs = refs[:source_count]
    hot_ref, k_ref, local_ref = refs[source_count : source_count + 3]
    out_ref = refs[-1]

    def store(row, which, value):
        out_ref[row] = value + local_ref[skip + row]

    remote_sums(source_refs, offsets, hot_ref, k_ref, out_ref.shape[0], 0, 1, store)


def per_device(green_blocks, derivative, phonon_weight, occupation, mode_shift, neighbours):
    rows, orbital, _, atoms = green_blocks.shape
    square = orbital * orbital
    bonds = derivative.shape[0]
    modes = phonon_weight.shape[0]
    local_bonds = bonds - REMOTE_BONDS
    pairs = lax.axis_size("energy") // 2
    slabs = lax.axis_size("atom")
    high = [4 * i for i in range(1, slabs // 4)]
    last = max(1, rows * P_PART // 8)
    sizes = [rows - last, last]
    firsts = [0, sizes[0]]
    chunks = len(sizes)
    green = green_blocks.reshape(rows, square, atoms)
    columns = neighbours.T

    mate = swap(green, "energy", 1)

    absorption = phonon_weight * occupation[:, None]
    couplings = jnp.concatenate([absorption + phonon_weight, absorption], 0).astype(BF16)
    shift_rows = jnp.broadcast_to(mode_shift[:, None], (modes, atoms))
    green_near = pl.pallas_call(
        copy_kernel,
        out_shape=jax.ShapeDtypeStruct(green.shape, green.dtype),
        in_specs=[VMEM],
        out_specs=VMEM,
        compiler_params=params(),
        cost_estimate=cost(1e6, 1e6),
    )(green)

    def mix(group, chunk, kind, after):
        return pl.pallas_call(
            functools.partial(mix_kernel, group, firsts[chunk]),
            out_shape=jax.ShapeDtypeStruct((sizes[chunk], square, atoms), kind),
            in_specs=[VMEM] * 4 + [ANY] * len(after),
            out_specs=VMEM,
            scratch_shapes=[
                pltpu.VMEM((sizes[chunk], 2 * rows + 1, SUBLANES, atoms), F32),
                pltpu.SMEM((modes, atoms), jnp.int32),
                pltpu.SemaphoreType.DMA,
            ],
            compiler_params=params(),
            cost_estimate=cost(5e8, 1e6),
        )(shift_rows, couplings, green_near, mate, *after)

    def prepare(after):
        return pl.pallas_call(
            prepare_kernel,
            out_shape=(
                jax.ShapeDtypeStruct((square, local_bonds * square), BF16),
                jax.ShapeDtypeStruct((square, REMOTE_BONDS * square), BF16),
                jax.ShapeDtypeStruct((local_bonds * atoms, atoms), BF16),
                jax.ShapeDtypeStruct((ID_ROWS, atoms), BF16),
            ),
            in_specs=[VMEM, VMEM, ANY],
            out_specs=(VMEM,) * 4,
            compiler_params=params(),
            cost_estimate=cost(2e9, 3e6),
        )(derivative, columns, after)

    def local_sum(chunk, after):
        return pl.pallas_call(
            local_kernel,
            out_shape=jax.ShapeDtypeStruct((sizes[chunk], square, atoms), F32),
            in_specs=[VMEM] * 3 + [ANY] * len(after),
            out_specs=VMEM,
            scratch_shapes=[
                pltpu.VMEM((local_bonds * square, min(2, sizes[chunk]) * atoms), BF16)
            ],
            compiler_params=params(),
            cost_estimate=cost(2e9, 3e6),
        )(mixed[chunk], local_hot, local_k, *after)

    own, arrived = [], []
    after = []
    for chunk in range(chunks):
        away = [mix(group, chunk, BF16, after) for group in range(1, pairs)]
        arrived.append([swap(value, "energy", 2 * group) for group, value in enumerate(away, 1)])
        if chunk == 0:
            own.append(mix(0, chunk, F32, away[:1]))
            after = own[-1:]
        else:
            local_k, remote_k, local_hot, ids = prepare(away[0])
    mixed = []
    for chunk in range(chunks):
        if chunk > 0:
            own.append(mix(0, chunk, F32, mixed[-1:] + [local_hot]))
        total = own[chunk]
        for received in arrived[chunk]:
            total = total + received.astype(F32)
        mixed.append(jnp.concatenate([total.astype(BF16).reshape(-1, atoms), ids], 0))

    def ordered(value, pieces, after):
        return pl.pallas_call(
            functools.partial(pass_kernel, pieces),
            out_shape=tuple(
                jax.ShapeDtypeStruct((end - first + (ID_ROWS if first == 0 else 0), atoms), BF16)
                for first, end in pieces
            ),
            in_specs=[VMEM, ANY],
            out_specs=(VMEM,) * len(pieces),
            compiler_params=params(),
            cost_estimate=cost(1e6, 1e6),
        )(value, after)

    def one_hots(sources, flips, after):
        return pl.pallas_call(
            functools.partial(remote_hot_kernel, REMOTE_BONDS, [0] + flips),
            out_shape=jax.ShapeDtypeStruct(
                ((1 + len(flips)) * REMOTE_BONDS * atoms, len(sources) * atoms), BF16
            ),
            in_specs=[VMEM] * len(sources) + [ANY],
            out_specs=VMEM,
            compiler_params=params(),
            cost_estimate=cost(1e8, 1e6),
        )(*sources, after)

    def away_sums(count, sources, offsets, hots, flips, after):
        block = jax.ShapeDtypeStruct((count, square, atoms), BF16)
        return pl.pallas_call(
            functools.partial(away_kernel, offsets),
            out_shape=(block,) * len(flips),
            in_specs=[VMEM] * (len(sources) + 2) + [ANY],
            out_specs=(VMEM,) * len(flips),
            compiler_params=params(),
            cost_estimate=cost(1e9, 3e6),
        )(*sources, hots, remote_k, after)

    def stay_sum(count, skip, sources, offsets, hots, local, after):
        return pl.pallas_call(
            functools.partial(stay_kernel, offsets, skip),
            out_shape=jax.ShapeDtypeStruct((count, square, atoms), F32),
            in_specs=[VMEM] * (len(sources) + 3) + [ANY] * len(after),
            out_specs=VMEM,
            compiler_params=params(),
            cost_estimate=cost(4e9, 3e6),
        )(*sources, hots, remote_k, local, *after)

    def send(values, masks):
        return [swap(value, "atom", mask) for value, mask in zip(values, masks)]

    inner, outer = mixed
    across, beside = send([inner] * 2, [2, 1])
    far = [outer] + send([outer] * len(high), high)
    [turned] = ordered(across, [(0, sizes[0] * square)], outer)
    near = [inner, across, beside] + send([turned], [1])
    local_inner = local_sum(0, [outer])
    local_outer = local_sum(1, [local_inner])
    far_beside = send(ordered(outer, [(0, sizes[1] * square)], local_inner), [1])
    straight = [0] * len(near)
    counts = [sizes[1] - sizes[1] // 2, sizes[1] // 2]
    skips = [0, counts[0]]
    pieces = [(skip * square, (skip + count) * square) for skip, count in zip(skips, counts)]

    def pass_far(after):
        passed = [ordered(value, pieces, after) for value in far[1:]]
        steps = [[value[index] for value in passed] for index in range(len(pieces))]
        return passed[0][-1], [send(values, [1] * len(values)) for values in steps]

    behind = local_outer
    near_hots = one_hots(near, high, behind)
    near_away = away_sums(sizes[0], near, straight, near_hots, high, behind)
    held = [
        pl.pallas_call(
            copy_kernel,
            out_shape=jax.ShapeDtypeStruct(value.shape, value.dtype),
            in_specs=[VMEM, ANY],
            out_specs=VMEM,
            compiler_params=params(),
            cost_estimate=cost(1e6, 1e6),
        )(value, far[-1])
        for value in near_away
    ]
    near_back = send(held, high)
    behind, far_next = pass_far(held[0])
    stay_inner = stay_sum(sizes[0], 0, near, straight, near_hots, local_inner, [behind])
    after = stay_inner
    far_hots = None
    far_away, far_lists = [], []
    for index, (first, _) in enumerate(pieces):
        sources = far + far_beside + far_next[index]
        offsets = [first] * len(far) + [first] + [0] * len(far_next[index])
        if far_hots is None:
            far_hots = one_hots(sources, [2], after)
        away = away_sums(counts[index], sources, offsets, far_hots, [2], after)
        after = away[0]
        far_away.append(swap(away[0], "atom", 2))
        far_lists.append((sources, offsets))
    results, arrivals = [stay_inner], [near_back]
    for index, (sources, offsets) in enumerate(far_lists):
        after = stay_sum(
            counts[index], skips[index], sources, offsets, far_hots, local_outer,
            [after],
        )
        results.append(after)
        arrivals.append([far_away[index]])
    combined = []
    for stay, received in zip(results, arrivals):
        for value in received:
            stay = stay + value.astype(F32)
        combined.append(stay)
    return jnp.concatenate(combined, 0).reshape(rows, orbital, orbital, atoms)


def solution(mesh):
    in_specs = (P("energy", None, None, "atom"), P(), P(None, "atom"), P(), P(), P("atom", None))
    out_specs = P("energy", None, None, "atom")
    return jax.shard_map(
        per_device, mesh=mesh, in_specs=in_specs, out_specs=out_specs, check_vma=False
    )
```

```python
import functools

import jax
import jax.numpy as jnp
from jax import lax
from jax.experimental import pallas as pl
from jax.experimental.pallas import tpu as pltpu
from jax.sharding import PartitionSpec as P

REMOTE_BONDS = 2
ID_ROWS = 16
P_PART = 4
COST = 1.0
SUBLANES = 8
VMEM_LIMIT = 48 * 1024 * 1024

VMEM = pl.BlockSpec(memory_space=pltpu.VMEM)
ANY = pl.BlockSpec(memory_space=pl.ANY)
F32, BF16 = jnp.float32, jnp.bfloat16


def params():
    return pltpu.CompilerParams(vmem_limit_bytes=VMEM_LIMIT)


def cost(flops, nbytes):
    return pl.CostEstimate(flops=int(flops * COST), bytes_accessed=int(nbytes * COST), transcendentals=0)


def swap(value, axis, mask):
    count = lax.axis_size(axis)
    return lax.ppermute(value, axis, [(i, i ^ mask) for i in range(count)])


def dot(left, right):
    return jnp.dot(left, right, preferred_element_type=F32)


def dot_nt(left, right):
    return lax.dot_general(left, right, (((1,), (1,)), ((), ())), preferred_element_type=F32)


def mix_kernel(group, first, shift_rows_ref, coupling_ref, own_ref, mate_ref, *rest):
    out_ref, table_ref, shift_ref, sem = rest[-4:]
    copy = pltpu.make_async_copy(shift_rows_ref, shift_ref, sem)
    copy.start()
    span, square, atoms = own_ref.shape
    rows = out_ref.shape[0]
    tile = table_ref.shape[2]
    modes = coupling_ref.shape[0] // 2
    me = lax.axis_index("energy")
    base = me // 2 * 2 * span
    move = me % 2 * span
    target = me ^ (2 * group)
    table_ref[...] = jnp.zeros_like(table_ref)
    couplings = coupling_ref[...].astype(F32)
    copy.wait()

    def put(row, source, value):
        place = source - base
        slot = jnp.where(place < span, place + move, place - move)
        inside = jnp.logical_and(place >= 0, place < 2 * span)
        table_ref[row, jnp.where(inside, slot, 2 * span)] = value

    for mode in range(modes):
        shift = shift_ref[mode, 0]
        emission = jnp.broadcast_to(couplings[mode : mode + 1, :], (tile, atoms))
        absorption = jnp.broadcast_to(couplings[modes + mode : modes + mode + 1, :], (tile, atoms))
        if group > 0:
            above = target > me
            sign = jnp.where(above, -shift, shift)
            coupling = jnp.where(above, emission, absorption)
        for row in range(rows):
            energy = target * span + first + row
            if group == 0:
                put(row, energy - shift, emission)
                put(row, energy + shift, absorption)
            else:
                put(row, energy + sign, coupling)

    step = min(32, square)

    def body(block, carry):
        at = pl.multiple_of(block * step, step)
        totals = [None] * rows
        for slot in range(2 * span):
            ref = own_ref if slot < span else mate_ref
            values = ref[slot % span, pl.ds(at, step), :].astype(F32).reshape(
                step // tile, tile, atoms
            )
            for row in range(rows):
                term = table_ref[row, slot][None] * values
                totals[row] = term if totals[row] is None else totals[row] + term
        for row in range(rows):
            out_ref[row, pl.ds(at, step), :] = totals[row].reshape(step, atoms).astype(out_ref.dtype)
        return carry

    lax.fori_loop(0, square // step, body, 0)


def hot(row, width):
    numbers = lax.broadcasted_iota(jnp.int32, (width, row.shape[1]), 0)
    return jnp.where(row == numbers, 1.0, 0.0).astype(BF16)


def prepare_kernel(derivative_ref, columns_ref, after_ref, local_k_ref, remote_k_ref, local_hot_ref, ids_ref):
    bonds, orbital, _ = derivative_ref.shape
    square = orbital * orbital
    atoms = columns_ref.shape[1]
    local_bonds = bonds - REMOTE_BONDS
    row = lax.broadcasted_iota(jnp.int32, (square, orbital), 0)
    row_of = lax.broadcasted_iota(jnp.int32, (square, orbital), 1)
    column = lax.broadcasted_iota(jnp.int32, (orbital, square), 1)
    column_of = lax.broadcasted_iota(jnp.int32, (orbital, square), 0)

    def pick(condition):
        return jnp.where(condition, 1.0, 0.0).astype(BF16)

    row_high, row_low = pick(row // orbital == row_of), pick(row % orbital == row_of)
    column_high, column_low = pick(column // orbital == column_of), pick(column % orbital == column_of)

    def spread(left, matrix, right):
        return dot(left, dot(matrix, right).astype(BF16))

    for bond in range(bonds):
        matrix = derivative_ref[bond]
        product = (
            spread(row_high, matrix, column_high) * spread(row_low, matrix, column_low)
        ).astype(BF16)
        if bond < local_bonds:
            local_k_ref[:, bond * square : (bond + 1) * square] = product
        else:
            at = bond - local_bonds
            remote_k_ref[:, at * square : (at + 1) * square] = product
    first = lax.axis_index("atom") * atoms
    for bond in range(local_bonds):
        local_hot_ref[bond * atoms : (bond + 1) * atoms, :] = hot(
            columns_ref[bond : bond + 1, :] - first, atoms
        )
    rows = []
    for bond in range(local_bonds, bonds):
        number = columns_ref[bond : bond + 1, :]
        rows += [number // atoms, number % atoms]
    place = lax.broadcasted_iota(jnp.int32, ids_ref.shape, 0)
    ids = jnp.zeros(ids_ref.shape, jnp.int32)
    for at, row in enumerate(rows):
        ids = jnp.where(place == at, row, ids)
    ids_ref[...] = ids.astype(F32).astype(BF16)


def copy_kernel(value_ref, *rest):
    rest[-1][...] = value_ref[...]


def pass_kernel(pieces, value_ref, after_ref, *out_refs):
    for index, ((first, end), out_ref) in enumerate(zip(pieces, out_refs)):
        out_ref[: end - first, :] = value_ref[first:end, :]
        if index == 0:
            out_ref[end - first :, :] = value_ref[value_ref.shape[0] - ID_ROWS :, :]


def remote_hot_kernel(bonds, flips, *refs):
    id_refs, out_ref = refs[:-2], refs[-1]
    atoms = id_refs[0].shape[1]
    me = lax.axis_index("atom")
    for place, ids_ref in enumerate(id_refs):
        ids = ids_ref[ids_ref.shape[0] - ID_ROWS :, :].astype(F32).astype(jnp.int32)
        for which, flip in enumerate(flips):
            slab = me ^ flip
            for bond in range(bonds):
                at = (which * bonds + bond) * atoms
                number = (ids[2 * bond : 2 * bond + 1, :] - slab) * atoms + ids[
                    2 * bond + 1 : 2 * bond + 2, :
                ]
                out_ref[at : at + atoms, place * atoms : (place + 1) * atoms] = hot(number, atoms)


def local_kernel(mixed_ref, hot_ref, k_ref, *rest):
    out_ref, sums_ref = rest[-2:]
    rows, square, atoms = out_ref.shape
    bonds = hot_ref.shape[0] // atoms
    group = sums_ref.shape[1] // atoms
    for start in range(0, rows, group):
        count = min(group, rows - start)
        for inner in range(count):
            at = (start + inner) * square
            summed = dot_nt(mixed_ref[at : at + square, :], hot_ref[...]).astype(BF16)
            for bond in range(bonds):
                sums_ref[bond * square : (bond + 1) * square, inner * atoms : (inner + 1) * atoms] = (
                    summed[:, bond * atoms : (bond + 1) * atoms]
                )
        result = dot(k_ref[...], sums_ref[:, : count * atoms])
        for inner in range(count):
            out_ref[start + inner] = result[:, inner * atoms : (inner + 1) * atoms]


def remote_sums(source_refs, offsets, hot_ref, k_ref, rows, first, count, store):
    atoms = source_refs[0].shape[1]
    square = k_ref.shape[0]
    bonds = k_ref.shape[1] // square
    width = bonds * atoms
    group = max(1, 2 // count)
    for start in range(0, rows, group):
        inner = range(start, min(start + group, rows))
        pieces = [[] for _ in range(bonds)]
        for row in inner:
            sources = jnp.concatenate(
                [
                    ref[at + row * square : at + (row + 1) * square, :]
                    for at, ref in zip(offsets, source_refs)
                ],
                axis=1,
            )
            summed = dot_nt(sources, hot_ref[first * width : (first + count) * width, :])
            summed = summed.astype(BF16)
            for which in range(count):
                for bond in range(bonds):
                    at = which * width + bond * atoms
                    pieces[bond].append(summed[:, at : at + atoms])
        stacked = jnp.concatenate([jnp.concatenate(piece, axis=1) for piece in pieces], axis=0)
        result = dot(k_ref[...], stacked)
        for place, row in enumerate(inner):
            for which in range(count):
                at = (place * count + which) * atoms
                store(row, which, result[:, at : at + atoms])


def away_kernel(offsets, *refs):
    source_count = len(offsets)
    source_refs = refs[:source_count]
    hot_ref, k_ref = refs[source_count : source_count + 2]
    count = hot_ref.shape[0] // (k_ref.shape[1] // k_ref.shape[0] * source_refs[0].shape[1]) - 1
    out_refs = refs[len(refs) - count :]
    rows = out_refs[0].shape[0]

    def store(row, which, value):
        out_refs[which][row] = value.astype(BF16)

    remote_sums(source_refs, offsets, hot_ref, k_ref, rows, 1, count, store)


def stay_kernel(offsets, skip, *refs):
    source_count = len(offsets)
    source_refs = refs[:source_count]
    hot_ref, k_ref, local_ref = refs[source_count : source_count + 3]
    out_ref = refs[-1]

    def store(row, which, value):
        out_ref[row] = value + local_ref[skip + row]

    remote_sums(source_refs, offsets, hot_ref, k_ref, out_ref.shape[0], 0, 1, store)


def per_device(green_blocks, derivative, phonon_weight, occupation, mode_shift, neighbours):
    rows, orbital, _, atoms = green_blocks.shape
    square = orbital * orbital
    bonds = derivative.shape[0]
    modes = phonon_weight.shape[0]
    local_bonds = bonds - REMOTE_BONDS
    pairs = lax.axis_size("energy") // 2
    slabs = lax.axis_size("atom")
    high = [4 * i for i in range(1, slabs // 4)]
    last = max(1, rows * P_PART // 8)
    sizes = [rows - last, last]
    firsts = [0, sizes[0]]
    chunks = len(sizes)
    green = green_blocks.reshape(rows, square, atoms)
    columns = neighbours.T

    mate = swap(green, "energy", 1)

    absorption = phonon_weight * occupation[:, None]
    couplings = jnp.concatenate([absorption + phonon_weight, absorption], 0).astype(BF16)
    shift_rows = jnp.broadcast_to(mode_shift[:, None], (modes, atoms))
    green_near = pl.pallas_call(
        copy_kernel,
        out_shape=jax.ShapeDtypeStruct(green.shape, green.dtype),
        in_specs=[VMEM],
        out_specs=VMEM,
        compiler_params=params(),
        cost_estimate=cost(1e6, 1e6),
    )(green)

    def mix(group, chunk, kind, after):
        return pl.pallas_call(
            functools.partial(mix_kernel, group, firsts[chunk]),
            out_shape=jax.ShapeDtypeStruct((sizes[chunk], square, atoms), kind),
            in_specs=[VMEM] * 4 + [ANY] * len(after),
            out_specs=VMEM,
            scratch_shapes=[
                pltpu.VMEM((sizes[chunk], 2 * rows + 1, SUBLANES, atoms), F32),
                pltpu.SMEM((modes, atoms), jnp.int32),
                pltpu.SemaphoreType.DMA,
            ],
            compiler_params=params(),
            cost_estimate=cost(5e8, 1e6),
        )(shift_rows, couplings, green_near, mate, *after)

    def prepare(after):
        return pl.pallas_call(
            prepare_kernel,
            out_shape=(
                jax.ShapeDtypeStruct((square, local_bonds * square), BF16),
                jax.ShapeDtypeStruct((square, REMOTE_BONDS * square), BF16),
                jax.ShapeDtypeStruct((local_bonds * atoms, atoms), BF16),
                jax.ShapeDtypeStruct((ID_ROWS, atoms), BF16),
            ),
            in_specs=[VMEM, VMEM, ANY],
            out_specs=(VMEM,) * 4,
            compiler_params=params(),
            cost_estimate=cost(2e9, 3e6),
        )(derivative, columns, after)

    def local_sum(chunk, after):
        return pl.pallas_call(
            local_kernel,
            out_shape=jax.ShapeDtypeStruct((sizes[chunk], square, atoms), F32),
            in_specs=[VMEM] * 3 + [ANY] * len(after),
            out_specs=VMEM,
            scratch_shapes=[
                pltpu.VMEM((local_bonds * square, min(2, sizes[chunk]) * atoms), BF16)
            ],
            compiler_params=params(),
            cost_estimate=cost(2e9, 3e6),
        )(mixed[chunk], local_hot, local_k, *after)

    own, arrived = [], []
    after = []
    for chunk in range(chunks):
        away = [mix(group, chunk, BF16, after) for group in range(1, pairs)]
        arrived.append([swap(value, "energy", 2 * group) for group, value in enumerate(away, 1)])
        if chunk == 0:
            own.append(mix(0, chunk, F32, away[:1]))
            after = own[-1:]
        else:
            local_k, remote_k, local_hot, ids = prepare(away[0])
    mixed = []
    for chunk in range(chunks):
        if chunk > 0:
            own.append(mix(0, chunk, F32, mixed[-1:] + [local_hot]))
        total = own[chunk]
        for received in arrived[chunk]:
            total = total + received.astype(F32)
        mixed.append(jnp.concatenate([total.astype(BF16).reshape(-1, atoms), ids], 0))

    def ordered(value, pieces, after):
        return pl.pallas_call(
            functools.partial(pass_kernel, pieces),
            out_shape=tuple(
                jax.ShapeDtypeStruct((end - first + (ID_ROWS if first == 0 else 0), atoms), BF16)
                for first, end in pieces
            ),
            in_specs=[VMEM, ANY],
            out_specs=(VMEM,) * len(pieces),
            compiler_params=params(),
            cost_estimate=cost(1e6, 1e6),
        )(value, after)

    def one_hots(sources, flips, after):
        return pl.pallas_call(
            functools.partial(remote_hot_kernel, REMOTE_BONDS, [0] + flips),
            out_shape=jax.ShapeDtypeStruct(
                ((1 + len(flips)) * REMOTE_BONDS * atoms, len(sources) * atoms), BF16
            ),
            in_specs=[VMEM] * len(sources) + [ANY],
            out_specs=VMEM,
            compiler_params=params(),
            cost_estimate=cost(1e8, 1e6),
        )(*sources, after)

    def away_sums(count, sources, offsets, hots, flips, after):
        block = jax.ShapeDtypeStruct((count, square, atoms), BF16)
        return pl.pallas_call(
            functools.partial(away_kernel, offsets),
            out_shape=(block,) * len(flips),
            in_specs=[VMEM] * (len(sources) + 2) + [ANY],
            out_specs=(VMEM,) * len(flips),
            compiler_params=params(),
            cost_estimate=cost(1e9, 3e6),
        )(*sources, hots, remote_k, after)

    def stay_sum(count, skip, sources, offsets, hots, local, after):
        return pl.pallas_call(
            functools.partial(stay_kernel, offsets, skip),
            out_shape=jax.ShapeDtypeStruct((count, square, atoms), F32),
            in_specs=[VMEM] * (len(sources) + 3) + [ANY] * len(after),
            out_specs=VMEM,
            compiler_params=params(),
            cost_estimate=cost(4e9, 3e6),
        )(*sources, hots, remote_k, local, *after)

    def send(values, masks):
        return [swap(value, "atom", mask) for value, mask in zip(values, masks)]

    inner, outer = mixed
    across, beside = send([inner] * 2, [2, 1])
    far = [outer] + send([outer] * len(high), high)
    [turned] = ordered(across, [(0, sizes[0] * square)], outer)
    near = [inner, across, beside] + send([turned], [1])
    local_inner = local_sum(0, [outer])
    local_outer = local_sum(1, [local_inner])
    far_beside = send(ordered(outer, [(0, sizes[1] * square)], local_inner), [1])
    straight = [0] * len(near)
    counts = [sizes[1] - sizes[1] // 2, sizes[1] // 2]
    skips = [0, counts[0]]
    pieces = [(skip * square, (skip + count) * square) for skip, count in zip(skips, counts)]

    def pass_far(after):
        passed = [ordered(value, pieces, after) for value in far[1:]]
        steps = [[value[index] for value in passed] for index in range(len(pieces))]
        return passed[0][-1], [send(values, [1] * len(values)) for values in steps]

    behind = local_outer
    near_hots = one_hots(near, high, behind)
    near_away = away_sums(sizes[0], near, straight, near_hots, high, behind)
    near_back = send(near_away, high)
    behind, far_next = pass_far(near_away[0])
    stay_inner = stay_sum(sizes[0], 0, near, straight, near_hots, local_inner, [behind])
    after = stay_inner
    far_hots = None
    far_away, far_lists = [], []
    for index, (first, _) in enumerate(pieces):
        sources = far + far_beside + far_next[index]
        offsets = [first] * len(far) + [first] + [0] * len(far_next[index])
        if far_hots is None:
            far_hots = one_hots(sources, [2], after)
        away = away_sums(counts[index], sources, offsets, far_hots, [2], after)
        after = away[0]
        far_away.append(swap(away[0], "atom", 2))
        far_lists.append((sources, offsets))
    results, arrivals = [stay_inner], [near_back]
    for index, (sources, offsets) in enumerate(far_lists):
        after = stay_sum(
            counts[index], skips[index], sources, offsets, far_hots, local_outer,
            [after],
        )
        results.append(after)
        arrivals.append([far_away[index]])
    combined = []
    for stay, received in zip(results, arrivals):
        for value in received:
            stay = stay + value.astype(F32)
        combined.append(stay)
    return jnp.concatenate(combined, 0).reshape(rows, orbital, orbital, atoms)


def solution(mesh):
    in_specs = (P("energy", None, None, "atom"), P(), P(None, "atom"), P(), P(), P("atom", None))
    out_specs = P("energy", None, None, "atom")
    return jax.shard_map(
        per_device, mesh=mesh, in_specs=in_specs, out_specs=out_specs, check_vma=False
    )
```

```python
import functools

import jax
import jax.numpy as jnp
from jax import lax
from jax.experimental import pallas as pl
from jax.experimental.pallas import tpu as pltpu
from jax.sharding import PartitionSpec as P

REMOTE_BONDS = 2
ID_ROWS = 16
P_PART = 4
COST = 1.0
SUBLANES = 8
VMEM_LIMIT = 48 * 1024 * 1024

VMEM = pl.BlockSpec(memory_space=pltpu.VMEM)
ANY = pl.BlockSpec(memory_space=pl.ANY)
F32, BF16 = jnp.float32, jnp.bfloat16


def params():
    return pltpu.CompilerParams(vmem_limit_bytes=VMEM_LIMIT)


def cost(flops, nbytes):
    return pl.CostEstimate(flops=int(flops * COST), bytes_accessed=int(nbytes * COST), transcendentals=0)


def swap(value, axis, mask):
    count = lax.axis_size(axis)
    return lax.ppermute(value, axis, [(i, i ^ mask) for i in range(count)])


def dot(left, right):
    return jnp.dot(left, right, preferred_element_type=F32)


def dot_nt(left, right):
    return lax.dot_general(left, right, (((1,), (1,)), ((), ())), preferred_element_type=F32)


def mix_kernel(group, first, shift_rows_ref, coupling_ref, own_ref, mate_ref, *rest):
    out_ref, table_ref, shift_ref, sem = rest[-4:]
    copy = pltpu.make_async_copy(shift_rows_ref, shift_ref, sem)
    copy.start()
    span, square, atoms = own_ref.shape
    rows = out_ref.shape[0]
    tile = table_ref.shape[2]
    modes = coupling_ref.shape[0] // 2
    me = lax.axis_index("energy")
    base = me // 2 * 2 * span
    move = me % 2 * span
    target = me ^ (2 * group)
    table_ref[...] = jnp.zeros_like(table_ref)
    couplings = coupling_ref[...].astype(F32)
    copy.wait()

    def put(row, source, value):
        place = source - base
        slot = jnp.where(place < span, place + move, place - move)
        inside = jnp.logical_and(place >= 0, place < 2 * span)
        table_ref[row, jnp.where(inside, slot, 2 * span)] = value

    for mode in range(modes):
        shift = shift_ref[mode, 0]
        emission = jnp.broadcast_to(couplings[mode : mode + 1, :], (tile, atoms))
        absorption = jnp.broadcast_to(couplings[modes + mode : modes + mode + 1, :], (tile, atoms))
        if group > 0:
            above = target > me
            sign = jnp.where(above, -shift, shift)
            coupling = jnp.where(above, emission, absorption)
        for row in range(rows):
            energy = target * span + first + row
            if group == 0:
                put(row, energy - shift, emission)
                put(row, energy + shift, absorption)
            else:
                put(row, energy + sign, coupling)

    step = min(32, square)

    def body(block, carry):
        at = pl.multiple_of(block * step, step)
        totals = [None] * rows
        for slot in range(2 * span):
            ref = own_ref if slot < span else mate_ref
            values = ref[slot % span, pl.ds(at, step), :].astype(F32).reshape(
                step // tile, tile, atoms
            )
            for row in range(rows):
                term = table_ref[row, slot][None] * values
                totals[row] = term if totals[row] is None else totals[row] + term
        for row in range(rows):
            out_ref[row, pl.ds(at, step), :] = totals[row].reshape(step, atoms).astype(out_ref.dtype)
        return carry

    lax.fori_loop(0, square // step, body, 0)


def hot(row, width):
    numbers = lax.broadcasted_iota(jnp.int32, (width, row.shape[1]), 0)
    return jnp.where(row == numbers, 1.0, 0.0).astype(BF16)


def prepare_kernel(derivative_ref, columns_ref, after_ref, local_k_ref, remote_k_ref, local_hot_ref):
    bonds, orbital, _ = derivative_ref.shape
    square = orbital * orbital
    atoms = columns_ref.shape[1]
    local_bonds = bonds - REMOTE_BONDS
    row = lax.broadcasted_iota(jnp.int32, (square, orbital), 0)
    row_of = lax.broadcasted_iota(jnp.int32, (square, orbital), 1)
    column = lax.broadcasted_iota(jnp.int32, (orbital, square), 1)
    column_of = lax.broadcasted_iota(jnp.int32, (orbital, square), 0)

    def pick(condition):
        return jnp.where(condition, 1.0, 0.0).astype(BF16)

    row_high, row_low = pick(row // orbital == row_of), pick(row % orbital == row_of)
    column_high, column_low = pick(column // orbital == column_of), pick(column % orbital == column_of)

    def spread(left, matrix, right):
        return dot(left, dot(matrix, right).astype(BF16))

    for bond in range(bonds):
        matrix = derivative_ref[bond]
        product = (
            spread(row_high, matrix, column_high) * spread(row_low, matrix, column_low)
        ).astype(BF16)
        if bond < local_bonds:
            local_k_ref[:, bond * square : (bond + 1) * square] = product
        else:
            at = bond - local_bonds
            remote_k_ref[:, at * square : (at + 1) * square] = product
    first = lax.axis_index("atom") * atoms
    for bond in range(local_bonds):
        local_hot_ref[bond * atoms : (bond + 1) * atoms, :] = hot(
            columns_ref[bond : bond + 1, :] - first, atoms
        )


def ids_kernel(columns_ref, ids_ref):
    bonds, atoms = columns_ref.shape
    rows = []
    for bond in range(bonds - REMOTE_BONDS, bonds):
        number = columns_ref[bond : bond + 1, :]
        rows += [number // atoms, number % atoms]
    place = lax.broadcasted_iota(jnp.int32, ids_ref.shape, 0)
    ids = jnp.zeros(ids_ref.shape, jnp.int32)
    for at, row in enumerate(rows):
        ids = jnp.where(place == at, row, ids)
    ids_ref[...] = ids.astype(F32).astype(BF16)


def copy_kernel(value_ref, *rest):
    rest[-1][...] = value_ref[...]


def pass_kernel(pieces, value_ref, after_ref, *out_refs):
    for index, ((first, end), out_ref) in enumerate(zip(pieces, out_refs)):
        out_ref[: end - first, :] = value_ref[first:end, :]
        if index == 0:
            out_ref[end - first :, :] = value_ref[value_ref.shape[0] - ID_ROWS :, :]


def remote_hot_kernel(bonds, flips, *refs):
    id_refs, out_ref = refs[:-2], refs[-1]
    atoms = id_refs[0].shape[1]
    me = lax.axis_index("atom")
    for place, ids_ref in enumerate(id_refs):
        ids = ids_ref[ids_ref.shape[0] - ID_ROWS :, :].astype(F32).astype(jnp.int32)
        for which, flip in enumerate(flips):
            slab = me ^ flip
            for bond in range(bonds):
                at = (which * bonds + bond) * atoms
                number = (ids[2 * bond : 2 * bond + 1, :] - slab) * atoms + ids[
                    2 * bond + 1 : 2 * bond + 2, :
                ]
                out_ref[at : at + atoms, place * atoms : (place + 1) * atoms] = hot(number, atoms)


def local_kernel(mixed_ref, hot_ref, k_ref, *rest):
    out_ref, sums_ref = rest[-2:]
    rows, square, atoms = out_ref.shape
    bonds = hot_ref.shape[0] // atoms
    group = sums_ref.shape[1] // atoms
    for start in range(0, rows, group):
        count = min(group, rows - start)
        for inner in range(count):
            at = (start + inner) * square
            summed = dot_nt(mixed_ref[at : at + square, :], hot_ref[...]).astype(BF16)
            for bond in range(bonds):
                sums_ref[bond * square : (bond + 1) * square, inner * atoms : (inner + 1) * atoms] = (
                    summed[:, bond * atoms : (bond + 1) * atoms]
                )
        result = dot(k_ref[...], sums_ref[:, : count * atoms])
        for inner in range(count):
            out_ref[start + inner] = result[:, inner * atoms : (inner + 1) * atoms]


def remote_sums(source_refs, offsets, hot_ref, k_ref, rows, first, count, store):
    atoms = source_refs[0].shape[1]
    square = k_ref.shape[0]
    bonds = k_ref.shape[1] // square
    width = bonds * atoms
    group = max(1, 2 // count)
    for start in range(0, rows, group):
        inner = range(start, min(start + group, rows))
        pieces = [[] for _ in range(bonds)]
        for row in inner:
            sources = jnp.concatenate(
                [
                    ref[at + row * square : at + (row + 1) * square, :]
                    for at, ref in zip(offsets, source_refs)
                ],
                axis=1,
            )
            summed = dot_nt(sources, hot_ref[first * width : (first + count) * width, :])
            summed = summed.astype(BF16)
            for which in range(count):
                for bond in range(bonds):
                    at = which * width + bond * atoms
                    pieces[bond].append(summed[:, at : at + atoms])
        stacked = jnp.concatenate([jnp.concatenate(piece, axis=1) for piece in pieces], axis=0)
        result = dot(k_ref[...], stacked)
        for place, row in enumerate(inner):
            for which in range(count):
                at = (place * count + which) * atoms
                store(row, which, result[:, at : at + atoms])


def away_kernel(offsets, *refs):
    source_count = len(offsets)
    source_refs = refs[:source_count]
    hot_ref, k_ref = refs[source_count : source_count + 2]
    count = hot_ref.shape[0] // (k_ref.shape[1] // k_ref.shape[0] * source_refs[0].shape[1]) - 1
    out_refs = refs[len(refs) - count :]
    rows = out_refs[0].shape[0]

    def store(row, which, value):
        out_refs[which][row] = value.astype(BF16)

    remote_sums(source_refs, offsets, hot_ref, k_ref, rows, 1, count, store)


def stay_kernel(offsets, skip, *refs):
    source_count = len(offsets)
    source_refs = refs[:source_count]
    hot_ref, k_ref, local_ref = refs[source_count : source_count + 3]
    out_ref = refs[-1]

    def store(row, which, value):
        out_ref[row] = value + local_ref[skip + row]

    remote_sums(source_refs, offsets, hot_ref, k_ref, out_ref.shape[0], 0, 1, store)


def per_device(green_blocks, derivative, phonon_weight, occupation, mode_shift, neighbours):
    rows, orbital, _, atoms = green_blocks.shape
    square = orbital * orbital
    bonds = derivative.shape[0]
    modes = phonon_weight.shape[0]
    local_bonds = bonds - REMOTE_BONDS
    pairs = lax.axis_size("energy") // 2
    slabs = lax.axis_size("atom")
    high = [4 * i for i in range(1, slabs // 4)]
    last = max(1, rows * P_PART // 8)
    sizes = [rows - last, last]
    firsts = [0, sizes[0]]
    chunks = len(sizes)
    green = green_blocks.reshape(rows, square, atoms)
    columns = neighbours.T

    mate = swap(green, "energy", 1)

    absorption = phonon_weight * occupation[:, None]
    couplings = jnp.concatenate([absorption + phonon_weight, absorption], 0).astype(BF16)
    shift_rows = jnp.broadcast_to(mode_shift[:, None], (modes, atoms))
    green_near = pl.pallas_call(
        copy_kernel,
        out_shape=jax.ShapeDtypeStruct(green.shape, green.dtype),
        in_specs=[VMEM],
        out_specs=VMEM,
        compiler_params=params(),
        cost_estimate=cost(1e6, 1e6),
    )(green)

    def mix(group, chunk, kind, after):
        return pl.pallas_call(
            functools.partial(mix_kernel, group, firsts[chunk]),
            out_shape=jax.ShapeDtypeStruct((sizes[chunk], square, atoms), kind),
            in_specs=[VMEM] * 4 + [ANY] * len(after),
            out_specs=VMEM,
            scratch_shapes=[
                pltpu.VMEM((sizes[chunk], 2 * rows + 1, SUBLANES, atoms), F32),
                pltpu.SMEM((modes, atoms), jnp.int32),
                pltpu.SemaphoreType.DMA,
            ],
            compiler_params=params(),
            cost_estimate=cost(5e8, 1e6),
        )(shift_rows, couplings, green_near, mate, *after)

    def prepare(after):
        return pl.pallas_call(
            prepare_kernel,
            out_shape=(
                jax.ShapeDtypeStruct((square, local_bonds * square), BF16),
                jax.ShapeDtypeStruct((square, REMOTE_BONDS * square), BF16),
                jax.ShapeDtypeStruct((local_bonds * atoms, atoms), BF16),
            ),
            in_specs=[VMEM, VMEM, ANY],
            out_specs=(VMEM,) * 3,
            compiler_params=params(),
            cost_estimate=cost(2e9, 3e6),
        )(derivative, columns, after)

    def local_sum(chunk, after, flops=2e9):
        return pl.pallas_call(
            local_kernel,
            out_shape=jax.ShapeDtypeStruct((sizes[chunk], square, atoms), F32),
            in_specs=[VMEM] * 3 + [ANY] * len(after),
            out_specs=VMEM,
            scratch_shapes=[
                pltpu.VMEM((local_bonds * square, min(2, sizes[chunk]) * atoms), BF16)
            ],
            compiler_params=params(),
            cost_estimate=cost(flops, 3e6),
        )(mixed[chunk], local_hot, local_k, *after)

    own, arrived = [], []
    after = []
    for chunk in range(chunks):
        away = [mix(group, chunk, BF16, after) for group in range(1, pairs)]
        arrived.append([swap(value, "energy", 2 * group) for group, value in enumerate(away, 1)])
        own.append(mix(0, chunk, F32, away[:1]))
        after = own[-1:]
    ids = pl.pallas_call(
        ids_kernel,
        out_shape=jax.ShapeDtypeStruct((ID_ROWS, atoms), BF16),
        in_specs=[VMEM],
        out_specs=VMEM,
        compiler_params=params(),
        cost_estimate=cost(1e6, 1e6),
    )(columns)
    mixed = []
    for chunk in range(chunks):
        total = own[chunk]
        if chunk > 0:
            total = pl.pallas_call(
                copy_kernel,
                out_shape=jax.ShapeDtypeStruct(total.shape, total.dtype),
                in_specs=[VMEM, ANY],
                out_specs=VMEM,
                compiler_params=params(),
                cost_estimate=cost(1e6, 1e6),
            )(total, mixed[-1])
        for received in arrived[chunk]:
            total = total + received.astype(F32)
        mixed.append(jnp.concatenate([total.astype(BF16).reshape(-1, atoms), ids], 0))

    def ordered(value, pieces, after):
        return pl.pallas_call(
            functools.partial(pass_kernel, pieces),
            out_shape=tuple(
                jax.ShapeDtypeStruct((end - first + (ID_ROWS if first == 0 else 0), atoms), BF16)
                for first, end in pieces
            ),
            in_specs=[VMEM, ANY],
            out_specs=(VMEM,) * len(pieces),
            compiler_params=params(),
            cost_estimate=cost(1e6, 1e6),
        )(value, after)

    def one_hots(sources, flips, after):
        return pl.pallas_call(
            functools.partial(remote_hot_kernel, REMOTE_BONDS, [0] + flips),
            out_shape=jax.ShapeDtypeStruct(
                ((1 + len(flips)) * REMOTE_BONDS * atoms, len(sources) * atoms), BF16
            ),
            in_specs=[VMEM] * len(sources) + [ANY],
            out_specs=VMEM,
            compiler_params=params(),
            cost_estimate=cost(1e8, 1e6),
        )(*sources, after)

    def away_sums(count, sources, offsets, hots, flips, after):
        block = jax.ShapeDtypeStruct((count, square, atoms), BF16)
        return pl.pallas_call(
            functools.partial(away_kernel, offsets),
            out_shape=(block,) * len(flips),
            in_specs=[VMEM] * (len(sources) + 2) + [ANY],
            out_specs=(VMEM,) * len(flips),
            compiler_params=params(),
            cost_estimate=cost(1e9, 3e6),
        )(*sources, hots, remote_k, after)

    def stay_sum(count, skip, sources, offsets, hots, local, after, flops):
        return pl.pallas_call(
            functools.partial(stay_kernel, offsets, skip),
            out_shape=jax.ShapeDtypeStruct((count, square, atoms), F32),
            in_specs=[VMEM] * (len(sources) + 3) + [ANY] * len(after),
            out_specs=VMEM,
            compiler_params=params(),
            cost_estimate=cost(flops, 3e6),
        )(*sources, hots, remote_k, local, *after)

    def send(values, masks):
        return [swap(value, "atom", mask) for value, mask in zip(values, masks)]

    inner, outer = mixed
    across, beside = send([inner] * 2, [2, 1])
    far = [outer] + send([outer] * len(high), high)
    [turned] = ordered(across, [(0, sizes[0] * square)], outer)
    near = [inner, across, beside] + send([turned], [1])
    local_k, remote_k, local_hot = prepare(turned)
    local_inner = local_sum(0, [])
    far_beside = send(ordered(outer, [(0, sizes[1] * square)], local_inner), [1])
    straight = [0] * len(near)
    counts = [sizes[1] - sizes[1] // 2, sizes[1] // 2]
    skips = [0, counts[0]]
    pieces = [(skip * square, (skip + count) * square) for skip, count in zip(skips, counts)]

    def pass_far(after):
        passed = [ordered(value, pieces, after) for value in far[1:]]
        steps = [[value[index] for value in passed] for index in range(len(pieces))]
        return passed[0][-1], [send(values, [1] * len(values)) for values in steps]

    behind = local_inner
    near_hots = one_hots(near, high, behind)
    near_away = away_sums(sizes[0], near, straight, near_hots, high, behind)
    near_back = send(near_away, high)
    behind, far_next = pass_far(near_away[0])
    stay_inner = stay_sum(sizes[0], 0, near, straight, near_hots, local_inner, [behind], 4e9)
    after = stay_inner
    far_hots = None
    far_away, far_lists = [], []
    for index, (first, _) in enumerate(pieces):
        sources = far + far_beside + far_next[index]
        offsets = [first] * len(far) + [first] + [0] * len(far_next[index])
        if far_hots is None:
            far_hots = one_hots(sources, [2], after)
        away = away_sums(counts[index], sources, offsets, far_hots, [2], after)
        after = away[0]
        far_away.append(swap(away[0], "atom", 2))
        far_lists.append((sources, offsets))
    local_outer = local_sum(1, [after], 1e6)
    results, arrivals = [stay_inner], [near_back]
    for index, (sources, offsets) in enumerate(far_lists):
        after = stay_sum(
            counts[index], skips[index], sources, offsets, far_hots, local_outer,
            [after],
            1e6,
        )
        results.append(after)
        arrivals.append([far_away[index]])
    combined = []
    for stay, received in zip(results, arrivals):
        for value in received:
            stay = stay + value.astype(F32)
        combined.append(stay)
    return jnp.concatenate(combined, 0).reshape(rows, orbital, orbital, atoms)


def solution(mesh):
    in_specs = (P("energy", None, None, "atom"), P(), P(None, "atom"), P(), P(), P("atom", None))
    out_specs = P("energy", None, None, "atom")
    return jax.shard_map(
        per_device, mesh=mesh, in_specs=in_specs, out_specs=out_specs, check_vma=False
    )
```

```python
import functools

import jax
import jax.numpy as jnp
from jax import lax
from jax.experimental import pallas as pl
from jax.experimental.pallas import tpu as pltpu
from jax.sharding import PartitionSpec as P

REMOTE_BONDS = 2
ID_ROWS = 16
P_PART = 4
COST = 1.0
SUBLANES = 8
VMEM_LIMIT = 48 * 1024 * 1024

VMEM = pl.BlockSpec(memory_space=pltpu.VMEM)
ANY = pl.BlockSpec(memory_space=pl.ANY)
F32, BF16 = jnp.float32, jnp.bfloat16


def params():
    return pltpu.CompilerParams(vmem_limit_bytes=VMEM_LIMIT)


def cost(flops, nbytes):
    return pl.CostEstimate(flops=int(flops * COST), bytes_accessed=int(nbytes * COST), transcendentals=0)


def swap(value, axis, mask):
    count = lax.axis_size(axis)
    return lax.ppermute(value, axis, [(i, i ^ mask) for i in range(count)])


def dot(left, right):
    return jnp.dot(left, right, preferred_element_type=F32)


def dot_nt(left, right):
    return lax.dot_general(left, right, (((1,), (1,)), ((), ())), preferred_element_type=F32)


def mix_kernel(group, first, shift_rows_ref, coupling_ref, own_ref, mate_ref, *rest):
    out_ref, table_ref, shift_ref, sem = rest[-4:]
    copy = pltpu.make_async_copy(shift_rows_ref, shift_ref, sem)
    copy.start()
    span, square, atoms = own_ref.shape
    rows = out_ref.shape[0]
    tile = table_ref.shape[2]
    modes = coupling_ref.shape[0] // 2
    me = lax.axis_index("energy")
    base = me // 2 * 2 * span
    move = me % 2 * span
    target = me ^ (2 * group)
    table_ref[...] = jnp.zeros_like(table_ref)
    couplings = coupling_ref[...].astype(F32)
    copy.wait()

    def put(row, source, value):
        place = source - base
        slot = jnp.where(place < span, place + move, place - move)
        inside = jnp.logical_and(place >= 0, place < 2 * span)
        table_ref[row, jnp.where(inside, slot, 2 * span)] = value

    for mode in range(modes):
        shift = shift_ref[mode, 0]
        emission = jnp.broadcast_to(couplings[mode : mode + 1, :], (tile, atoms))
        absorption = jnp.broadcast_to(couplings[modes + mode : modes + mode + 1, :], (tile, atoms))
        if group > 0:
            above = target > me
            sign = jnp.where(above, -shift, shift)
            coupling = jnp.where(above, emission, absorption)
        for row in range(rows):
            energy = target * span + first + row
            if group == 0:
                put(row, energy - shift, emission)
                put(row, energy + shift, absorption)
            else:
                put(row, energy + sign, coupling)

    step = min(32, square)

    def body(block, carry):
        at = pl.multiple_of(block * step, step)
        totals = [None] * rows
        for slot in range(2 * span):
            ref = own_ref if slot < span else mate_ref
            values = ref[slot % span, pl.ds(at, step), :].astype(F32).reshape(
                step // tile, tile, atoms
            )
            for row in range(rows):
                term = table_ref[row, slot][None] * values
                totals[row] = term if totals[row] is None else totals[row] + term
        for row in range(rows):
            out_ref[row, pl.ds(at, step), :] = totals[row].reshape(step, atoms).astype(out_ref.dtype)
        return carry

    lax.fori_loop(0, square // step, body, 0)


def hot(row, width):
    numbers = lax.broadcasted_iota(jnp.int32, (width, row.shape[1]), 0)
    return jnp.where(row == numbers, 1.0, 0.0).astype(BF16)


def prepare_kernel(derivative_ref, columns_ref, after_ref, local_k_ref, remote_k_ref, local_hot_ref, ids_ref):
    bonds, orbital, _ = derivative_ref.shape
    square = orbital * orbital
    atoms = columns_ref.shape[1]
    local_bonds = bonds - REMOTE_BONDS
    row = lax.broadcasted_iota(jnp.int32, (square, orbital), 0)
    row_of = lax.broadcasted_iota(jnp.int32, (square, orbital), 1)
    column = lax.broadcasted_iota(jnp.int32, (orbital, square), 1)
    column_of = lax.broadcasted_iota(jnp.int32, (orbital, square), 0)

    def pick(condition):
        return jnp.where(condition, 1.0, 0.0).astype(BF16)

    row_high, row_low = pick(row // orbital == row_of), pick(row % orbital == row_of)
    column_high, column_low = pick(column // orbital == column_of), pick(column % orbital == column_of)

    def spread(left, matrix, right):
        return dot(left, dot(matrix, right).astype(BF16))

    for bond in range(bonds):
        matrix = derivative_ref[bond]
        product = (
            spread(row_high, matrix, column_high) * spread(row_low, matrix, column_low)
        ).astype(BF16)
        if bond < local_bonds:
            local_k_ref[:, bond * square : (bond + 1) * square] = product
        else:
            at = bond - local_bonds
            remote_k_ref[:, at * square : (at + 1) * square] = product
    first = lax.axis_index("atom") * atoms
    for bond in range(local_bonds):
        local_hot_ref[bond * atoms : (bond + 1) * atoms, :] = hot(
            columns_ref[bond : bond + 1, :] - first, atoms
        )
    rows = []
    for bond in range(local_bonds, bonds):
        number = columns_ref[bond : bond + 1, :]
        rows += [number // atoms, number % atoms]
    place = lax.broadcasted_iota(jnp.int32, ids_ref.shape, 0)
    ids = jnp.zeros(ids_ref.shape, jnp.int32)
    for at, row in enumerate(rows):
        ids = jnp.where(place == at, row, ids)
    ids_ref[...] = ids.astype(F32).astype(BF16)


def copy_kernel(value_ref, *rest):
    rest[-1][...] = value_ref[...]


def pass_kernel(pieces, value_ref, after_ref, *out_refs):
    for index, ((first, end), out_ref) in enumerate(zip(pieces, out_refs)):
        out_ref[: end - first, :] = value_ref[first:end, :]
        if index == 0:
            out_ref[end - first :, :] = value_ref[value_ref.shape[0] - ID_ROWS :, :]


def remote_hot_kernel(bonds, flips, *refs):
    id_refs, out_ref = refs[:-2], refs[-1]
    atoms = id_refs[0].shape[1]
    me = lax.axis_index("atom")
    for place, ids_ref in enumerate(id_refs):
        ids = ids_ref[ids_ref.shape[0] - ID_ROWS :, :].astype(F32).astype(jnp.int32)
        for which, flip in enumerate(flips):
            slab = me ^ flip
            for bond in range(bonds):
                at = (which * bonds + bond) * atoms
                number = (ids[2 * bond : 2 * bond + 1, :] - slab) * atoms + ids[
                    2 * bond + 1 : 2 * bond + 2, :
                ]
                out_ref[at : at + atoms, place * atoms : (place + 1) * atoms] = hot(number, atoms)


def local_kernel(mixed_ref, hot_ref, k_ref, *rest):
    out_ref, sums_ref = rest[-2:]
    rows, square, atoms = out_ref.shape
    bonds = hot_ref.shape[0] // atoms
    group = sums_ref.shape[1] // atoms
    for start in range(0, rows, group):
        count = min(group, rows - start)
        for inner in range(count):
            at = (start + inner) * square
            summed = dot_nt(mixed_ref[at : at + square, :], hot_ref[...]).astype(BF16)
            for bond in range(bonds):
                sums_ref[bond * square : (bond + 1) * square, inner * atoms : (inner + 1) * atoms] = (
                    summed[:, bond * atoms : (bond + 1) * atoms]
                )
        result = dot(k_ref[...], sums_ref[:, : count * atoms])
        for inner in range(count):
            out_ref[start + inner] = result[:, inner * atoms : (inner + 1) * atoms]


def remote_sums(source_refs, offsets, hot_ref, k_ref, rows, first, count, store):
    atoms = source_refs[0].shape[1]
    square = k_ref.shape[0]
    bonds = k_ref.shape[1] // square
    width = bonds * atoms
    group = max(1, 2 // count)
    for start in range(0, rows, group):
        inner = range(start, min(start + group, rows))
        pieces = [[] for _ in range(bonds)]
        for row in inner:
            sources = jnp.concatenate(
                [
                    ref[at + row * square : at + (row + 1) * square, :]
                    for at, ref in zip(offsets, source_refs)
                ],
                axis=1,
            )
            summed = dot_nt(sources, hot_ref[first * width : (first + count) * width, :])
            summed = summed.astype(BF16)
            for which in range(count):
                for bond in range(bonds):
                    at = which * width + bond * atoms
                    pieces[bond].append(summed[:, at : at + atoms])
        stacked = jnp.concatenate([jnp.concatenate(piece, axis=1) for piece in pieces], axis=0)
        result = dot(k_ref[...], stacked)
        for place, row in enumerate(inner):
            for which in range(count):
                at = (place * count + which) * atoms
                store(row, which, result[:, at : at + atoms])


def away_kernel(offsets, *refs):
    source_count = len(offsets)
    source_refs = refs[:source_count]
    hot_ref, k_ref = refs[source_count : source_count + 2]
    count = hot_ref.shape[0] // (k_ref.shape[1] // k_ref.shape[0] * source_refs[0].shape[1]) - 1
    out_refs = refs[len(refs) - count :]
    rows = out_refs[0].shape[0]

    def store(row, which, value):
        out_refs[which][row] = value.astype(BF16)

    remote_sums(source_refs, offsets, hot_ref, k_ref, rows, 1, count, store)


def stay_kernel(offsets, skip, *refs):
    source_count = len(offsets)
    source_refs = refs[:source_count]
    hot_ref, k_ref, local_ref = refs[source_count : source_count + 3]
    out_ref = refs[-1]

    def store(row, which, value):
        out_ref[row] = value + local_ref[skip + row]

    remote_sums(source_refs, offsets, hot_ref, k_ref, out_ref.shape[0], 0, 1, store)


def per_device(green_blocks, derivative, phonon_weight, occupation, mode_shift, neighbours):
    rows, orbital, _, atoms = green_blocks.shape
    square = orbital * orbital
    bonds = derivative.shape[0]
    modes = phonon_weight.shape[0]
    local_bonds = bonds - REMOTE_BONDS
    pairs = lax.axis_size("energy") // 2
    slabs = lax.axis_size("atom")
    high = [4 * i for i in range(1, slabs // 4)]
    last = max(1, rows * P_PART // 8)
    sizes = [rows - last, last]
    firsts = [0, sizes[0]]
    chunks = len(sizes)
    green = green_blocks.reshape(rows, square, atoms)
    columns = neighbours.T

    mate = swap(green, "energy", 1)

    absorption = phonon_weight * occupation[:, None]
    couplings = jnp.concatenate([absorption + phonon_weight, absorption], 0).astype(BF16)
    shift_rows = jnp.broadcast_to(mode_shift[:, None], (modes, atoms))
    green_near = pl.pallas_call(
        copy_kernel,
        out_shape=jax.ShapeDtypeStruct(green.shape, green.dtype),
        in_specs=[VMEM],
        out_specs=VMEM,
        compiler_params=params(),
        cost_estimate=cost(1e6, 1e6),
    )(green)

    def mix(group, chunk, kind, after):
        return pl.pallas_call(
            functools.partial(mix_kernel, group, firsts[chunk]),
            out_shape=jax.ShapeDtypeStruct((sizes[chunk], square, atoms), kind),
            in_specs=[VMEM] * 4 + [ANY] * len(after),
            out_specs=VMEM,
            scratch_shapes=[
                pltpu.VMEM((sizes[chunk], 2 * rows + 1, SUBLANES, atoms), F32),
                pltpu.SMEM((modes, atoms), jnp.int32),
                pltpu.SemaphoreType.DMA,
            ],
            compiler_params=params(),
            cost_estimate=cost(5e8, 1e6),
        )(shift_rows, couplings, green_near, mate, *after)

    def prepare(after):
        return pl.pallas_call(
            prepare_kernel,
            out_shape=(
                jax.ShapeDtypeStruct((square, local_bonds * square), BF16),
                jax.ShapeDtypeStruct((square, REMOTE_BONDS * square), BF16),
                jax.ShapeDtypeStruct((local_bonds * atoms, atoms), BF16),
                jax.ShapeDtypeStruct((ID_ROWS, atoms), BF16),
            ),
            in_specs=[VMEM, VMEM, ANY],
            out_specs=(VMEM,) * 4,
            compiler_params=params(),
            cost_estimate=cost(2e9, 3e6),
        )(derivative, columns, after)

    def local_sum(chunk, after):
        return pl.pallas_call(
            local_kernel,
            out_shape=jax.ShapeDtypeStruct((sizes[chunk], square, atoms), F32),
            in_specs=[VMEM] * 3 + [ANY] * len(after),
            out_specs=VMEM,
            scratch_shapes=[
                pltpu.VMEM((local_bonds * square, min(2, sizes[chunk]) * atoms), BF16)
            ],
            compiler_params=params(),
            cost_estimate=cost(2e9, 3e6),
        )(mixed[chunk], local_hot, local_k, *after)

    own, arrived = [], []
    after = []
    for chunk in range(chunks):
        away = [mix(group, chunk, BF16, after) for group in range(1, pairs)]
        arrived.append([swap(value, "energy", 2 * group) for group, value in enumerate(away, 1)])
        if chunk == 0:
            own.append(mix(0, chunk, F32, away[:1]))
            after = own[-1:]
        else:
            local_k, remote_k, local_hot, ids = prepare(away[0])
    mixed = []
    for chunk in range(chunks):
        if chunk > 0:
            own.append(mix(0, chunk, F32, mixed[-1:] + [local_hot]))
        total = own[chunk]
        for received in arrived[chunk]:
            total = total + received.astype(F32)
        mixed.append(jnp.concatenate([total.astype(BF16).reshape(-1, atoms), ids], 0))

    def ordered(value, pieces, after):
        return pl.pallas_call(
            functools.partial(pass_kernel, pieces),
            out_shape=tuple(
                jax.ShapeDtypeStruct((end - first + (ID_ROWS if first == 0 else 0), atoms), BF16)
                for first, end in pieces
            ),
            in_specs=[VMEM, ANY],
            out_specs=(VMEM,) * len(pieces),
            compiler_params=params(),
            cost_estimate=cost(1e6, 1e6),
        )(value, after)

    def one_hots(sources, flips, after):
        return pl.pallas_call(
            functools.partial(remote_hot_kernel, REMOTE_BONDS, [0] + flips),
            out_shape=jax.ShapeDtypeStruct(
                ((1 + len(flips)) * REMOTE_BONDS * atoms, len(sources) * atoms), BF16
            ),
            in_specs=[VMEM] * len(sources) + [ANY],
            out_specs=VMEM,
            compiler_params=params(),
            cost_estimate=cost(1e8, 1e6),
        )(*sources, after)

    def away_sums(count, sources, offsets, hots, flips, after):
        block = jax.ShapeDtypeStruct((count, square, atoms), BF16)
        return pl.pallas_call(
            functools.partial(away_kernel, offsets),
            out_shape=(block,) * len(flips),
            in_specs=[VMEM] * (len(sources) + 2) + [ANY],
            out_specs=(VMEM,) * len(flips),
            compiler_params=params(),
            cost_estimate=cost(1e9, 3e6),
        )(*sources, hots, remote_k, after)

    def stay_sum(count, skip, sources, offsets, hots, local, after):
        return pl.pallas_call(
            functools.partial(stay_kernel, offsets, skip),
            out_shape=jax.ShapeDtypeStruct((count, square, atoms), F32),
            in_specs=[VMEM] * (len(sources) + 3) + [ANY] * len(after),
            out_specs=VMEM,
            compiler_params=params(),
            cost_estimate=cost(4e9, 3e6),
        )(*sources, hots, remote_k, local, *after)

    def send(values, masks):
        return [swap(value, "atom", mask) for value, mask in zip(values, masks)]

    inner, outer = mixed
    across, beside = send([inner] * 2, [2, 1])
    far = [outer] + send([outer] * len(high), high)
    [turned] = ordered(across, [(0, sizes[0] * square)], outer)
    near = [inner, across, beside] + send([turned], [1])
    local_inner = local_sum(0, [outer])
    local_outer = local_sum(1, [local_inner])
    far_beside = send(ordered(outer, [(0, sizes[1] * square)], local_inner), [1])
    straight = [0] * len(near)
    counts = [sizes[1] - sizes[1] // 2, sizes[1] // 2]
    skips = [0, counts[0]]
    pieces = [(skip * square, (skip + count) * square) for skip, count in zip(skips, counts)]

    def pass_far(after):
        passed = [ordered(value, pieces, after) for value in far[1:]]
        steps = [[value[index] for value in passed] for index in range(len(pieces))]
        return passed[0][-1], [send(values, [1] * len(values)) for values in steps]

    behind, far_next = pass_far(local_outer)
    near_hots = one_hots(near, high, behind)
    near_away = away_sums(sizes[0], near, straight, near_hots, high, behind)
    near_back = send(near_away, high)
    behind = near_away[0]
    stay_inner = stay_sum(sizes[0], 0, near, straight, near_hots, local_inner, [behind])
    after = stay_inner
    far_hots = None
    far_away, far_lists = [], []
    for index, (first, _) in enumerate(pieces):
        sources = far + far_beside + far_next[index]
        offsets = [first] * len(far) + [first] + [0] * len(far_next[index])
        if far_hots is None:
            far_hots = one_hots(sources, [2], after)
        away = away_sums(counts[index], sources, offsets, far_hots, [2], after)
        after = away[0]
        far_away.append(swap(away[0], "atom", 2))
        far_lists.append((sources, offsets))
    results, arrivals = [stay_inner], [near_back]
    for index, (sources, offsets) in enumerate(far_lists):
        after = stay_sum(
            counts[index], skips[index], sources, offsets, far_hots, local_outer,
            [after],
        )
        results.append(after)
        arrivals.append([far_away[index]])
    combined = []
    for stay, received in zip(results, arrivals):
        for value in received:
            stay = stay + value.astype(F32)
        combined.append(stay)
    return jnp.concatenate(combined, 0).reshape(rows, orbital, orbital, atoms)


def solution(mesh):
    in_specs = (P("energy", None, None, "atom"), P(), P(None, "atom"), P(), P(), P("atom", None))
    out_specs = P("energy", None, None, "atom")
    return jax.shard_map(
        per_device, mesh=mesh, in_specs=in_specs, out_specs=out_specs, check_vma=False
    )
```

```python
import functools

import jax
import jax.numpy as jnp
from jax import lax
from jax.experimental import pallas as pl
from jax.experimental.pallas import tpu as pltpu
from jax.sharding import PartitionSpec as P

REMOTE_BONDS = 2
ID_ROWS = 16
P_PART = 4
COST = 1.0
SUBLANES = 8
VMEM_LIMIT = 48 * 1024 * 1024

VMEM = pl.BlockSpec(memory_space=pltpu.VMEM)
ANY = pl.BlockSpec(memory_space=pl.ANY)
F32, BF16 = jnp.float32, jnp.bfloat16


def params():
    return pltpu.CompilerParams(vmem_limit_bytes=VMEM_LIMIT)


def cost(flops, nbytes):
    return pl.CostEstimate(flops=int(flops * COST), bytes_accessed=int(nbytes * COST), transcendentals=0)


def swap(value, axis, mask):
    count = lax.axis_size(axis)
    return lax.ppermute(value, axis, [(i, i ^ mask) for i in range(count)])


def dot(left, right):
    return jnp.dot(left, right, preferred_element_type=F32)


def dot_nt(left, right):
    return lax.dot_general(left, right, (((1,), (1,)), ((), ())), preferred_element_type=F32)


def mix_kernel(group, first, shift_rows_ref, coupling_ref, own_ref, mate_ref, *rest):
    out_ref, table_ref, shift_ref, sem = rest[-4:]
    copy = pltpu.make_async_copy(shift_rows_ref, shift_ref, sem)
    copy.start()
    span, square, atoms = own_ref.shape
    rows = out_ref.shape[0]
    tile = table_ref.shape[2]
    modes = coupling_ref.shape[0] // 2
    me = lax.axis_index("energy")
    base = me // 2 * 2 * span
    move = me % 2 * span
    target = me ^ (2 * group)
    table_ref[...] = jnp.zeros_like(table_ref)
    couplings = coupling_ref[...].astype(F32)
    copy.wait()

    def put(row, source, value):
        place = source - base
        slot = jnp.where(place < span, place + move, place - move)
        inside = jnp.logical_and(place >= 0, place < 2 * span)
        table_ref[row, jnp.where(inside, slot, 2 * span)] = value

    for mode in range(modes):
        shift = shift_ref[mode, 0]
        emission = jnp.broadcast_to(couplings[mode : mode + 1, :], (tile, atoms))
        absorption = jnp.broadcast_to(couplings[modes + mode : modes + mode + 1, :], (tile, atoms))
        if group > 0:
            above = target > me
            sign = jnp.where(above, -shift, shift)
            coupling = jnp.where(above, emission, absorption)
        for row in range(rows):
            energy = target * span + first + row
            if group == 0:
                put(row, energy - shift, emission)
                put(row, energy + shift, absorption)
            else:
                put(row, energy + sign, coupling)

    step = min(32, square)

    def body(block, carry):
        at = pl.multiple_of(block * step, step)
        totals = [None] * rows
        for slot in range(2 * span):
            ref = own_ref if slot < span else mate_ref
            values = ref[slot % span, pl.ds(at, step), :].astype(F32).reshape(
                step // tile, tile, atoms
            )
            for row in range(rows):
                term = table_ref[row, slot][None] * values
                totals[row] = term if totals[row] is None else totals[row] + term
        for row in range(rows):
            out_ref[row, pl.ds(at, step), :] = totals[row].reshape(step, atoms).astype(out_ref.dtype)
        return carry

    lax.fori_loop(0, square // step, body, 0)


def hot(row, width):
    numbers = lax.broadcasted_iota(jnp.int32, (width, row.shape[1]), 0)
    return jnp.where(row == numbers, 1.0, 0.0).astype(BF16)


def prepare_kernel(derivative_ref, columns_ref, after_ref, local_k_ref, remote_k_ref, local_hot_ref, ids_ref):
    bonds, orbital, _ = derivative_ref.shape
    square = orbital * orbital
    atoms = columns_ref.shape[1]
    local_bonds = bonds - REMOTE_BONDS
    row = lax.broadcasted_iota(jnp.int32, (square, orbital), 0)
    row_of = lax.broadcasted_iota(jnp.int32, (square, orbital), 1)
    column = lax.broadcasted_iota(jnp.int32, (orbital, square), 1)
    column_of = lax.broadcasted_iota(jnp.int32, (orbital, square), 0)

    def pick(condition):
        return jnp.where(condition, 1.0, 0.0).astype(BF16)

    row_high, row_low = pick(row // orbital == row_of), pick(row % orbital == row_of)
    column_high, column_low = pick(column // orbital == column_of), pick(column % orbital == column_of)

    def spread(left, matrix, right):
        return dot(left, dot(matrix, right).astype(BF16))

    for bond in range(bonds):
        matrix = derivative_ref[bond]
        product = (
            spread(row_high, matrix, column_high) * spread(row_low, matrix, column_low)
        ).astype(BF16)
        if bond < local_bonds:
            local_k_ref[:, bond * square : (bond + 1) * square] = product
        else:
            at = bond - local_bonds
            remote_k_ref[:, at * square : (at + 1) * square] = product
    first = lax.axis_index("atom") * atoms
    for bond in range(local_bonds):
        local_hot_ref[bond * atoms : (bond + 1) * atoms, :] = hot(
            columns_ref[bond : bond + 1, :] - first, atoms
        )
    rows = []
    for bond in range(local_bonds, bonds):
        number = columns_ref[bond : bond + 1, :]
        rows += [number // atoms, number % atoms]
    place = lax.broadcasted_iota(jnp.int32, ids_ref.shape, 0)
    ids = jnp.zeros(ids_ref.shape, jnp.int32)
    for at, row in enumerate(rows):
        ids = jnp.where(place == at, row, ids)
    ids_ref[...] = ids.astype(F32).astype(BF16)


def copy_kernel(value_ref, *rest):
    rest[-1][...] = value_ref[...]


def pass_kernel(pieces, value_ref, after_ref, *out_refs):
    for index, ((first, end), out_ref) in enumerate(zip(pieces, out_refs)):
        out_ref[: end - first, :] = value_ref[first:end, :]
        if index == 0:
            out_ref[end - first :, :] = value_ref[value_ref.shape[0] - ID_ROWS :, :]


def remote_hot_kernel(bonds, flips, *refs):
    id_refs, out_ref = refs[:-2], refs[-1]
    atoms = id_refs[0].shape[1]
    me = lax.axis_index("atom")
    for place, ids_ref in enumerate(id_refs):
        ids = ids_ref[ids_ref.shape[0] - ID_ROWS :, :].astype(F32).astype(jnp.int32)
        for which, flip in enumerate(flips):
            slab = me ^ flip
            for bond in range(bonds):
                at = (which * bonds + bond) * atoms
                number = (ids[2 * bond : 2 * bond + 1, :] - slab) * atoms + ids[
                    2 * bond + 1 : 2 * bond + 2, :
                ]
                out_ref[at : at + atoms, place * atoms : (place + 1) * atoms] = hot(number, atoms)


def local_kernel(mixed_ref, hot_ref, k_ref, *rest):
    out_ref, sums_ref = rest[-2:]
    rows, square, atoms = out_ref.shape
    bonds = hot_ref.shape[0] // atoms
    group = sums_ref.shape[1] // atoms
    for start in range(0, rows, group):
        count = min(group, rows - start)
        for inner in range(count):
            at = (start + inner) * square
            summed = dot_nt(mixed_ref[at : at + square, :], hot_ref[...]).astype(BF16)
            for bond in range(bonds):
                sums_ref[bond * square : (bond + 1) * square, inner * atoms : (inner + 1) * atoms] = (
                    summed[:, bond * atoms : (bond + 1) * atoms]
                )
        result = dot(k_ref[...], sums_ref[:, : count * atoms])
        for inner in range(count):
            out_ref[start + inner] = result[:, inner * atoms : (inner + 1) * atoms]


def remote_sums(source_refs, offsets, hot_ref, k_ref, rows, first, count, store):
    atoms = source_refs[0].shape[1]
    square = k_ref.shape[0]
    bonds = k_ref.shape[1] // square
    width = bonds * atoms
    group = max(1, 2 // count)
    for start in range(0, rows, group):
        inner = range(start, min(start + group, rows))
        pieces = [[] for _ in range(bonds)]
        for row in inner:
            sources = jnp.concatenate(
                [
                    ref[at + row * square : at + (row + 1) * square, :]
                    for at, ref in zip(offsets, source_refs)
                ],
                axis=1,
            )
            summed = dot_nt(sources, hot_ref[first * width : (first + count) * width, :])
            summed = summed.astype(BF16)
            for which in range(count):
                for bond in range(bonds):
                    at = which * width + bond * atoms
                    pieces[bond].append(summed[:, at : at + atoms])
        stacked = jnp.concatenate([jnp.concatenate(piece, axis=1) for piece in pieces], axis=0)
        result = dot(k_ref[...], stacked)
        for place, row in enumerate(inner):
            for which in range(count):
                at = (place * count + which) * atoms
                store(row, which, result[:, at : at + atoms])


def away_kernel(offsets, *refs):
    source_count = len(offsets)
    source_refs = refs[:source_count]
    hot_ref, k_ref = refs[source_count : source_count + 2]
    count = hot_ref.shape[0] // (k_ref.shape[1] // k_ref.shape[0] * source_refs[0].shape[1]) - 1
    out_refs = refs[len(refs) - count :]
    rows = out_refs[0].shape[0]

    def store(row, which, value):
        out_refs[which][row] = value.astype(BF16)

    remote_sums(source_refs, offsets, hot_ref, k_ref, rows, 1, count, store)


def stay_kernel(offsets, skip, *refs):
    source_count = len(offsets)
    source_refs = refs[:source_count]
    hot_ref, k_ref, local_ref = refs[source_count : source_count + 3]
    out_ref = refs[-1]

    def store(row, which, value):
        out_ref[row] = value + local_ref[skip + row]

    remote_sums(source_refs, offsets, hot_ref, k_ref, out_ref.shape[0], 0, 1, store)


def per_device(green_blocks, derivative, phonon_weight, occupation, mode_shift, neighbours):
    rows, orbital, _, atoms = green_blocks.shape
    square = orbital * orbital
    bonds = derivative.shape[0]
    modes = phonon_weight.shape[0]
    local_bonds = bonds - REMOTE_BONDS
    pairs = lax.axis_size("energy") // 2
    slabs = lax.axis_size("atom")
    high = [4 * i for i in range(1, slabs // 4)]
    last = max(1, rows * P_PART // 8)
    sizes = [rows - last, last]
    firsts = [0, sizes[0]]
    chunks = len(sizes)
    green = green_blocks.reshape(rows, square, atoms)
    columns = neighbours.T

    mate = swap(green, "energy", 1)

    absorption = phonon_weight * occupation[:, None]
    couplings = jnp.concatenate([absorption + phonon_weight, absorption], 0).astype(BF16)
    shift_rows = jnp.broadcast_to(mode_shift[:, None], (modes, atoms))
    green_near = pl.pallas_call(
        copy_kernel,
        out_shape=jax.ShapeDtypeStruct(green.shape, green.dtype),
        in_specs=[VMEM],
        out_specs=VMEM,
        compiler_params=params(),
        cost_estimate=cost(1e6, 1e6),
    )(green)

    def mix(group, chunk, kind, after):
        return pl.pallas_call(
            functools.partial(mix_kernel, group, firsts[chunk]),
            out_shape=jax.ShapeDtypeStruct((sizes[chunk], square, atoms), kind),
            in_specs=[VMEM] * 4 + [ANY] * len(after),
            out_specs=VMEM,
            scratch_shapes=[
                pltpu.VMEM((sizes[chunk], 2 * rows + 1, SUBLANES, atoms), F32),
                pltpu.SMEM((modes, atoms), jnp.int32),
                pltpu.SemaphoreType.DMA,
            ],
            compiler_params=params(),
            cost_estimate=cost(5e8, 1e6),
        )(shift_rows, couplings, green_near, mate, *after)

    def prepare(after):
        return pl.pallas_call(
            prepare_kernel,
            out_shape=(
                jax.ShapeDtypeStruct((square, local_bonds * square), BF16),
                jax.ShapeDtypeStruct((square, REMOTE_BONDS * square), BF16),
                jax.ShapeDtypeStruct((local_bonds * atoms, atoms), BF16),
                jax.ShapeDtypeStruct((ID_ROWS, atoms), BF16),
            ),
            in_specs=[VMEM, VMEM, ANY],
            out_specs=(VMEM,) * 4,
            compiler_params=params(),
            cost_estimate=cost(2e9, 3e6),
        )(derivative, columns, after)

    def local_sum(chunk, after):
        return pl.pallas_call(
            local_kernel,
            out_shape=jax.ShapeDtypeStruct((sizes[chunk], square, atoms), F32),
            in_specs=[VMEM] * 3 + [ANY] * len(after),
            out_specs=VMEM,
            scratch_shapes=[
                pltpu.VMEM((local_bonds * square, min(2, sizes[chunk]) * atoms), BF16)
            ],
            compiler_params=params(),
            cost_estimate=cost(2e9, 3e6),
        )(mixed[chunk], local_hot, local_k, *after)

    own, arrived = [], []
    after = []
    for chunk in range(chunks):
        away = [mix(group, chunk, BF16, after) for group in range(1, pairs)]
        arrived.append([swap(value, "energy", 2 * group) for group, value in enumerate(away, 1)])
        if chunk == 0:
            own.append(mix(0, chunk, F32, away[:1]))
            after = own[-1:]
        else:
            local_k, remote_k, local_hot, ids = prepare(away[0])
    mixed = []
    for chunk in range(chunks):
        if chunk > 0:
            own.append(mix(0, chunk, F32, mixed[-1:] + [local_hot]))
        total = own[chunk]
        for received in arrived[chunk]:
            total = total + received.astype(F32)
        mixed.append(jnp.concatenate([total.astype(BF16).reshape(-1, atoms), ids], 0))

    def ordered(value, pieces, after):
        return pl.pallas_call(
            functools.partial(pass_kernel, pieces),
            out_shape=tuple(
                jax.ShapeDtypeStruct((end - first + (ID_ROWS if first == 0 else 0), atoms), BF16)
                for first, end in pieces
            ),
            in_specs=[VMEM, ANY],
            out_specs=(VMEM,) * len(pieces),
            compiler_params=params(),
            cost_estimate=cost(1e6, 1e6),
        )(value, after)

    def one_hots(sources, flips, after):
        return pl.pallas_call(
            functools.partial(remote_hot_kernel, REMOTE_BONDS, [0] + flips),
            out_shape=jax.ShapeDtypeStruct(
                ((1 + len(flips)) * REMOTE_BONDS * atoms, len(sources) * atoms), BF16
            ),
            in_specs=[VMEM] * len(sources) + [ANY],
            out_specs=VMEM,
            compiler_params=params(),
            cost_estimate=cost(1e8, 1e6),
        )(*sources, after)

    def away_sums(count, sources, offsets, hots, flips, after):
        block = jax.ShapeDtypeStruct((count, square, atoms), BF16)
        return pl.pallas_call(
            functools.partial(away_kernel, offsets),
            out_shape=(block,) * len(flips),
            in_specs=[VMEM] * (len(sources) + 2) + [ANY],
            out_specs=(VMEM,) * len(flips),
            compiler_params=params(),
            cost_estimate=cost(1e9, 3e6),
        )(*sources, hots, remote_k, after)

    def stay_sum(count, skip, sources, offsets, hots, local, after):
        return pl.pallas_call(
            functools.partial(stay_kernel, offsets, skip),
            out_shape=jax.ShapeDtypeStruct((count, square, atoms), F32),
            in_specs=[VMEM] * (len(sources) + 3) + [ANY] * len(after),
            out_specs=VMEM,
            compiler_params=params(),
            cost_estimate=cost(4e9, 3e6),
        )(*sources, hots, remote_k, local, *after)

    def send(values, masks):
        return [swap(value, "atom", mask) for value, mask in zip(values, masks)]

    inner, outer = mixed
    across, beside = send([inner] * 2, [2, 1])
    far = [outer] + send([outer] * len(high), high)
    [turned] = ordered(across, [(0, sizes[0] * square)], outer)
    near = [inner, across, beside] + send([turned], [1])
    local_inner = local_sum(0, [outer])
    local_outer = local_sum(1, [local_inner])
    far_beside = send(ordered(outer, [(0, sizes[1] * square)], local_inner), [1])
    straight = [0] * len(near)
    counts = [sizes[1] // 4, sizes[1] - sizes[1] // 4]
    skips = [0, counts[0]]
    pieces = [(skip * square, (skip + count) * square) for skip, count in zip(skips, counts)]

    def pass_far(after):
        passed = [ordered(value, pieces, after) for value in far[1:]]
        steps = [[value[index] for value in passed] for index in range(len(pieces))]
        return passed[0][-1], [send(values, [1] * len(values)) for values in steps]

    behind = local_outer
    near_hots = one_hots(near, high, behind)
    near_away = away_sums(sizes[0], near, straight, near_hots, high, behind)
    near_back = send(near_away, high)
    behind, far_next = pass_far(near_away[0])
    stay_inner = stay_sum(sizes[0], 0, near, straight, near_hots, local_inner, [behind])
    after = stay_inner
    far_hots = None
    far_away, far_lists = [], []
    for index, (first, _) in enumerate(pieces):
        sources = far + far_beside + far_next[index]
        offsets = [first] * len(far) + [first] + [0] * len(far_next[index])
        if far_hots is None:
            far_hots = one_hots(sources, [2], after)
        away = away_sums(counts[index], sources, offsets, far_hots, [2], after)
        after = away[0]
        far_away.append(swap(away[0], "atom", 2))
        far_lists.append((sources, offsets))
    results, arrivals = [stay_inner], [near_back]
    for index, (sources, offsets) in enumerate(far_lists):
        after = stay_sum(
            counts[index], skips[index], sources, offsets, far_hots, local_outer,
            [after],
        )
        results.append(after)
        arrivals.append([far_away[index]])
    combined = []
    for stay, received in zip(results, arrivals):
        for value in received:
            stay = stay + value.astype(F32)
        combined.append(stay)
    return jnp.concatenate(combined, 0).reshape(rows, orbital, orbital, atoms)


def solution(mesh):
    in_specs = (P("energy", None, None, "atom"), P(), P(None, "atom"), P(), P(), P("atom", None))
    out_specs = P("energy", None, None, "atom")
    return jax.shard_map(
        per_device, mesh=mesh, in_specs=in_specs, out_specs=out_specs, check_vma=False
    )
```

```python
import functools

import jax
import jax.numpy as jnp
from jax import lax
from jax.experimental import pallas as pl
from jax.experimental.pallas import tpu as pltpu
from jax.sharding import PartitionSpec as P

REMOTE_BONDS = 2
ID_ROWS = 16
P_PART = 4
COST = 1.0
SUBLANES = 8
VMEM_LIMIT = 48 * 1024 * 1024

VMEM = pl.BlockSpec(memory_space=pltpu.VMEM)
ANY = pl.BlockSpec(memory_space=pl.ANY)
F32, BF16 = jnp.float32, jnp.bfloat16


def params():
    return pltpu.CompilerParams(vmem_limit_bytes=VMEM_LIMIT)


def cost(flops, nbytes):
    return pl.CostEstimate(flops=int(flops * COST), bytes_accessed=int(nbytes * COST), transcendentals=0)


def swap(value, axis, mask):
    count = lax.axis_size(axis)
    return lax.ppermute(value, axis, [(i, i ^ mask) for i in range(count)])


def dot(left, right):
    return jnp.dot(left, right, preferred_element_type=F32)


def dot_nt(left, right):
    return lax.dot_general(left, right, (((1,), (1,)), ((), ())), preferred_element_type=F32)


def mix_kernel(group, first, shift_rows_ref, coupling_ref, own_ref, mate_ref, *rest):
    out_ref, table_ref, shift_ref, sem = rest[-4:]
    copy = pltpu.make_async_copy(shift_rows_ref, shift_ref, sem)
    copy.start()
    span, square, atoms = own_ref.shape
    rows = out_ref.shape[0]
    tile = table_ref.shape[2]
    modes = coupling_ref.shape[0] // 2
    me = lax.axis_index("energy")
    base = me // 2 * 2 * span
    move = me % 2 * span
    target = me ^ (2 * group)
    table_ref[...] = jnp.zeros_like(table_ref)
    couplings = coupling_ref[...].astype(F32)
    copy.wait()

    def put(row, source, value):
        place = source - base
        slot = jnp.where(place < span, place + move, place - move)
        inside = jnp.logical_and(place >= 0, place < 2 * span)
        table_ref[row, jnp.where(inside, slot, 2 * span)] = value

    for mode in range(modes):
        shift = shift_ref[mode, 0]
        emission = jnp.broadcast_to(couplings[mode : mode + 1, :], (tile, atoms))
        absorption = jnp.broadcast_to(couplings[modes + mode : modes + mode + 1, :], (tile, atoms))
        if group > 0:
            above = target > me
            sign = jnp.where(above, -shift, shift)
            coupling = jnp.where(above, emission, absorption)
        for row in range(rows):
            energy = target * span + first + row
            if group == 0:
                put(row, energy - shift, emission)
                put(row, energy + shift, absorption)
            else:
                put(row, energy + sign, coupling)

    step = min(32, square)

    def body(block, carry):
        at = pl.multiple_of(block * step, step)
        totals = [None] * rows
        for slot in range(2 * span):
            ref = own_ref if slot < span else mate_ref
            values = ref[slot % span, pl.ds(at, step), :].astype(F32).reshape(
                step // tile, tile, atoms
            )
            for row in range(rows):
                term = table_ref[row, slot][None] * values
                totals[row] = term if totals[row] is None else totals[row] + term
        for row in range(rows):
            out_ref[row, pl.ds(at, step), :] = totals[row].reshape(step, atoms).astype(out_ref.dtype)
        return carry

    lax.fori_loop(0, square // step, body, 0)


def hot(row, width):
    numbers = lax.broadcasted_iota(jnp.int32, (width, row.shape[1]), 0)
    return jnp.where(row == numbers, 1.0, 0.0).astype(BF16)


def prepare_kernel(derivative_ref, columns_ref, after_ref, local_k_ref, remote_k_ref, local_hot_ref, ids_ref):
    bonds, orbital, _ = derivative_ref.shape
    square = orbital * orbital
    atoms = columns_ref.shape[1]
    local_bonds = bonds - REMOTE_BONDS
    row = lax.broadcasted_iota(jnp.int32, (square, orbital), 0)
    row_of = lax.broadcasted_iota(jnp.int32, (square, orbital), 1)
    column = lax.broadcasted_iota(jnp.int32, (orbital, square), 1)
    column_of = lax.broadcasted_iota(jnp.int32, (orbital, square), 0)

    def pick(condition):
        return jnp.where(condition, 1.0, 0.0).astype(BF16)

    row_high, row_low = pick(row // orbital == row_of), pick(row % orbital == row_of)
    column_high, column_low = pick(column // orbital == column_of), pick(column % orbital == column_of)

    def spread(left, matrix, right):
        return dot(left, dot(matrix, right).astype(BF16))

    for bond in range(bonds):
        matrix = derivative_ref[bond]
        product = (
            spread(row_high, matrix, column_high) * spread(row_low, matrix, column_low)
        ).astype(BF16)
        if bond < local_bonds:
            local_k_ref[:, bond * square : (bond + 1) * square] = product
        else:
            at = bond - local_bonds
            remote_k_ref[:, at * square : (at + 1) * square] = product
    first = lax.axis_index("atom") * atoms
    for bond in range(local_bonds):
        local_hot_ref[bond * atoms : (bond + 1) * atoms, :] = hot(
            columns_ref[bond : bond + 1, :] - first, atoms
        )
    rows = []
    for bond in range(local_bonds, bonds):
        number = columns_ref[bond : bond + 1, :]
        rows += [number // atoms, number % atoms]
    place = lax.broadcasted_iota(jnp.int32, ids_ref.shape, 0)
    ids = jnp.zeros(ids_ref.shape, jnp.int32)
    for at, row in enumerate(rows):
        ids = jnp.where(place == at, row, ids)
    ids_ref[...] = ids.astype(F32).astype(BF16)


def copy_kernel(value_ref, *rest):
    rest[-1][...] = value_ref[...]


def pass_kernel(pieces, value_ref, after_ref, *out_refs):
    for index, ((first, end), out_ref) in enumerate(zip(pieces, out_refs)):
        out_ref[: end - first, :] = value_ref[first:end, :]
        if index == 0:
            out_ref[end - first :, :] = value_ref[value_ref.shape[0] - ID_ROWS :, :]


def remote_hot_kernel(bonds, flips, *refs):
    id_refs, out_ref = refs[:-2], refs[-1]
    atoms = id_refs[0].shape[1]
    me = lax.axis_index("atom")
    for place, ids_ref in enumerate(id_refs):
        ids = ids_ref[ids_ref.shape[0] - ID_ROWS :, :].astype(F32).astype(jnp.int32)
        for which, flip in enumerate(flips):
            slab = me ^ flip
            for bond in range(bonds):
                at = (which * bonds + bond) * atoms
                number = (ids[2 * bond : 2 * bond + 1, :] - slab) * atoms + ids[
                    2 * bond + 1 : 2 * bond + 2, :
                ]
                out_ref[at : at + atoms, place * atoms : (place + 1) * atoms] = hot(number, atoms)


def local_kernel(mixed_ref, hot_ref, k_ref, *rest):
    out_ref, sums_ref = rest[-2:]
    rows, square, atoms = out_ref.shape
    bonds = hot_ref.shape[0] // atoms
    group = sums_ref.shape[1] // atoms
    for start in range(0, rows, group):
        count = min(group, rows - start)
        for inner in range(count):
            at = (start + inner) * square
            summed = dot_nt(mixed_ref[at : at + square, :], hot_ref[...]).astype(BF16)
            for bond in range(bonds):
                sums_ref[bond * square : (bond + 1) * square, inner * atoms : (inner + 1) * atoms] = (
                    summed[:, bond * atoms : (bond + 1) * atoms]
                )
        result = dot(k_ref[...], sums_ref[:, : count * atoms])
        for inner in range(count):
            out_ref[start + inner] = result[:, inner * atoms : (inner + 1) * atoms]


def remote_sums(source_refs, offsets, hot_ref, k_ref, rows, first, count, store):
    atoms = source_refs[0].shape[1]
    square = k_ref.shape[0]
    bonds = k_ref.shape[1] // square
    width = bonds * atoms
    group = max(1, 2 // count)
    for start in range(0, rows, group):
        inner = range(start, min(start + group, rows))
        pieces = [[] for _ in range(bonds)]
        for row in inner:
            sources = jnp.concatenate(
                [
                    ref[at + row * square : at + (row + 1) * square, :]
                    for at, ref in zip(offsets, source_refs)
                ],
                axis=1,
            )
            summed = dot_nt(sources, hot_ref[first * width : (first + count) * width, :])
            summed = summed.astype(BF16)
            for which in range(count):
                for bond in range(bonds):
                    at = which * width + bond * atoms
                    pieces[bond].append(summed[:, at : at + atoms])
        stacked = jnp.concatenate([jnp.concatenate(piece, axis=1) for piece in pieces], axis=0)
        result = dot(k_ref[...], stacked)
        for place, row in enumerate(inner):
            for which in range(count):
                at = (place * count + which) * atoms
                store(row, which, result[:, at : at + atoms])


def away_kernel(offsets, *refs):
    source_count = len(offsets)
    source_refs = refs[:source_count]
    hot_ref, k_ref = refs[source_count : source_count + 2]
    count = hot_ref.shape[0] // (k_ref.shape[1] // k_ref.shape[0] * source_refs[0].shape[1]) - 1
    out_refs = refs[len(refs) - count :]
    rows = out_refs[0].shape[0]

    def store(row, which, value):
        out_refs[which][row] = value.astype(BF16)

    remote_sums(source_refs, offsets, hot_ref, k_ref, rows, 1, count, store)


def stay_kernel(offsets, skip, *refs):
    source_count = len(offsets)
    source_refs = refs[:source_count]
    hot_ref, k_ref, local_ref = refs[source_count : source_count + 3]
    out_ref = refs[-1]

    def store(row, which, value):
        out_ref[row] = value + local_ref[skip + row]

    remote_sums(source_refs, offsets, hot_ref, k_ref, out_ref.shape[0], 0, 1, store)


def per_device(green_blocks, derivative, phonon_weight, occupation, mode_shift, neighbours):
    rows, orbital, _, atoms = green_blocks.shape
    square = orbital * orbital
    bonds = derivative.shape[0]
    modes = phonon_weight.shape[0]
    local_bonds = bonds - REMOTE_BONDS
    pairs = lax.axis_size("energy") // 2
    slabs = lax.axis_size("atom")
    high = [4 * i for i in range(1, slabs // 4)]
    last = max(1, rows * P_PART // 8)
    sizes = [rows - last, last]
    firsts = [0, sizes[0]]
    chunks = len(sizes)
    green = green_blocks.reshape(rows, square, atoms)
    columns = neighbours.T

    mate = swap(green, "energy", 1)

    absorption = phonon_weight * occupation[:, None]
    couplings = jnp.concatenate([absorption + phonon_weight, absorption], 0).astype(BF16)
    shift_rows = jnp.broadcast_to(mode_shift[:, None], (modes, atoms))
    green_near = pl.pallas_call(
        copy_kernel,
        out_shape=jax.ShapeDtypeStruct(green.shape, green.dtype),
        in_specs=[VMEM],
        out_specs=VMEM,
        compiler_params=params(),
        cost_estimate=cost(1e6, 1e6),
    )(green)

    def mix(group, chunk, kind, after):
        return pl.pallas_call(
            functools.partial(mix_kernel, group, firsts[chunk]),
            out_shape=jax.ShapeDtypeStruct((sizes[chunk], square, atoms), kind),
            in_specs=[VMEM] * 4 + [ANY] * len(after),
            out_specs=VMEM,
            scratch_shapes=[
                pltpu.VMEM((sizes[chunk], 2 * rows + 1, SUBLANES, atoms), F32),
                pltpu.SMEM((modes, atoms), jnp.int32),
                pltpu.SemaphoreType.DMA,
            ],
            compiler_params=params(),
            cost_estimate=cost(5e8, 1e6),
        )(shift_rows, couplings, green_near, mate, *after)

    def prepare(after):
        return pl.pallas_call(
            prepare_kernel,
            out_shape=(
                jax.ShapeDtypeStruct((square, local_bonds * square), BF16),
                jax.ShapeDtypeStruct((square, REMOTE_BONDS * square), BF16),
                jax.ShapeDtypeStruct((local_bonds * atoms, atoms), BF16),
                jax.ShapeDtypeStruct((ID_ROWS, atoms), BF16),
            ),
            in_specs=[VMEM, VMEM, ANY],
            out_specs=(VMEM,) * 4,
            compiler_params=params(),
            cost_estimate=cost(2e9, 3e6),
        )(derivative, columns, after)

    def local_sum(chunk, after):
        return pl.pallas_call(
            local_kernel,
            out_shape=jax.ShapeDtypeStruct((sizes[chunk], square, atoms), F32),
            in_specs=[VMEM] * 3 + [ANY] * len(after),
            out_specs=VMEM,
            scratch_shapes=[
                pltpu.VMEM((local_bonds * square, min(2, sizes[chunk]) * atoms), BF16)
            ],
            compiler_params=params(),
            cost_estimate=cost(2e9, 3e6),
        )(mixed[chunk], local_hot, local_k, *after)

    own, arrived = [], []
    after = []
    for chunk in range(chunks):
        away = [mix(group, chunk, BF16, after) for group in range(1, pairs)]
        arrived.append([swap(value, "energy", 2 * group) for group, value in enumerate(away, 1)])
        if chunk == 0:
            own.append(mix(0, chunk, F32, away[:1]))
            after = own[-1:]
        else:
            local_k, remote_k, local_hot, ids = prepare(away[0])
    mixed = []
    for chunk in range(chunks):
        if chunk > 0:
            own.append(mix(0, chunk, F32, mixed[-1:] + [local_hot]))
        total = own[chunk]
        for received in arrived[chunk]:
            total = total + received.astype(F32)
        mixed.append(jnp.concatenate([total.astype(BF16).reshape(-1, atoms), ids], 0))

    def ordered(value, pieces, after):
        return pl.pallas_call(
            functools.partial(pass_kernel, pieces),
            out_shape=tuple(
                jax.ShapeDtypeStruct((end - first + (ID_ROWS if first == 0 else 0), atoms), BF16)
                for first, end in pieces
            ),
            in_specs=[VMEM, ANY],
            out_specs=(VMEM,) * len(pieces),
            compiler_params=params(),
            cost_estimate=cost(1e6, 1e6),
        )(value, after)

    def one_hots(sources, flips, after):
        return pl.pallas_call(
            functools.partial(remote_hot_kernel, REMOTE_BONDS, [0] + flips),
            out_shape=jax.ShapeDtypeStruct(
                ((1 + len(flips)) * REMOTE_BONDS * atoms, len(sources) * atoms), BF16
            ),
            in_specs=[VMEM] * len(sources) + [ANY],
            out_specs=VMEM,
            compiler_params=params(),
            cost_estimate=cost(1e8, 1e6),
        )(*sources, after)

    def away_sums(count, sources, offsets, hots, flips, after):
        block = jax.ShapeDtypeStruct((count, square, atoms), BF16)
        return pl.pallas_call(
            functools.partial(away_kernel, offsets),
            out_shape=(block,) * len(flips),
            in_specs=[VMEM] * (len(sources) + 2) + [ANY],
            out_specs=(VMEM,) * len(flips),
            compiler_params=params(),
            cost_estimate=cost(1e9, 3e6),
        )(*sources, hots, remote_k, after)

    def stay_sum(count, skip, sources, offsets, hots, local, after):
        return pl.pallas_call(
            functools.partial(stay_kernel, offsets, skip),
            out_shape=jax.ShapeDtypeStruct((count, square, atoms), F32),
            in_specs=[VMEM] * (len(sources) + 3) + [ANY] * len(after),
            out_specs=VMEM,
            compiler_params=params(),
            cost_estimate=cost(4e9, 3e6),
        )(*sources, hots, remote_k, local, *after)

    def send(values, masks):
        return [swap(value, "atom", mask) for value, mask in zip(values, masks)]

    inner, outer = mixed
    across, beside = send([inner] * 2, [2, 1])
    far = [outer] + send([outer] * len(high), high)
    [turned] = ordered(across, [(0, sizes[0] * square)], outer)
    near = [inner, across, beside] + send([turned], [1])
    local_inner = local_sum(0, [outer])
    far_beside = send(ordered(outer, [(0, sizes[1] * square)], local_inner), [1])
    straight = [0] * len(near)
    counts = [sizes[1] - sizes[1] // 2, sizes[1] // 2]
    skips = [0, counts[0]]
    pieces = [(skip * square, (skip + count) * square) for skip, count in zip(skips, counts)]

    def pass_far(after):
        passed = [ordered(value, pieces, after) for value in far[1:]]
        steps = [[value[index] for value in passed] for index in range(len(pieces))]
        return passed[0][-1], [send(values, [1] * len(values)) for values in steps]

    behind = local_inner
    near_hots = one_hots(near, high, behind)
    near_away = away_sums(sizes[0], near, straight, near_hots, high, behind)
    near_back = send(near_away, high)
    behind, far_next = pass_far(near_away[0])
    stay_inner = stay_sum(sizes[0], 0, near, straight, near_hots, local_inner, [behind])
    local_outer = local_sum(1, [stay_inner])
    after = local_outer
    far_hots = None
    far_away, far_lists = [], []
    for index, (first, _) in enumerate(pieces):
        sources = far + far_beside + far_next[index]
        offsets = [first] * len(far) + [first] + [0] * len(far_next[index])
        if far_hots is None:
            far_hots = one_hots(sources, [2], after)
        away = away_sums(counts[index], sources, offsets, far_hots, [2], after)
        after = away[0]
        far_away.append(swap(away[0], "atom", 2))
        far_lists.append((sources, offsets))
    results, arrivals = [stay_inner], [near_back]
    for index, (sources, offsets) in enumerate(far_lists):
        after = stay_sum(
            counts[index], skips[index], sources, offsets, far_hots, local_outer,
            [after],
        )
        results.append(after)
        arrivals.append([far_away[index]])
    combined = []
    for stay, received in zip(results, arrivals):
        for value in received:
            stay = stay + value.astype(F32)
        combined.append(stay)
    return jnp.concatenate(combined, 0).reshape(rows, orbital, orbital, atoms)


def solution(mesh):
    in_specs = (P("energy", None, None, "atom"), P(), P(None, "atom"), P(), P(), P("atom", None))
    out_specs = P("energy", None, None, "atom")
    return jax.shard_map(
        per_device, mesh=mesh, in_specs=in_specs, out_specs=out_specs, check_vma=False
    )
```
